256 devices in a mesh: dp: 32 (over z_hi, x, core), fsdp: 8 (over y, z_lo).
Axes of the slice: x: 4, y: 4, z: 8 (z_hi: 4, z_lo: 2; z = z_hi * 2 + z_lo), core: 2. Of those that a mesh axis runs over, the one named last changes fastest.
Arguments:
- waveform_rows: bfloat16 [32768, 1024], P(('dp', 'fsdp')), may hold values from -6 to 6
- conv_weight: bfloat16 [1024, 512], P('fsdp'), may hold values from -0.1875 to 0.1875
- proj_weight: bfloat16 [512, 1280], P('fsdp'), may hold values from -0.25 to 0.25
- ffn_pair: bfloat16 [2560, 2, 1280], P('fsdp', None, 'dp'), may hold values from -0.15625 to 0.15625
- owner: int32 [32768, 1], P(('dp', 'fsdp')), may hold values from 0 to 31; in each aligned block of 128 rows (0 to 127, 128 to 255, ...) at most 6 rows name the same one
- frame_live: int32 [32768], P(('dp', 'fsdp')), may hold values 0 or 1
- cotangent: bfloat16 [49152, 1280], P(('dp', 'fsdp')), may hold values from -0.125 to 0.125
Outputs:
- encoded: bfloat16 [49152, 1280], P(('dp', 'fsdp'))
- grad_pair: float32 [2560, 2, 1280], P('fsdp', None, 'dp')
The draws below stay inside these ranges and needn't reach their ends.
Inputs may be any that keep to these rules, and one draw needn't show every extreme that they name: In the rows of one device no owner is named more than 6 times, a bound that some block reaches.
All inputs are finite; a program needn't handle non-finite values. No bound on the sum of `frame_live` on one device may be relied on, other than what follows from the above.
Results may differ from the reference program's by a relative error of at most 0.038.
Values may be sent and summed in bfloat16 or wider, within the bound.
No kernel may reach another device: no remote copies, remote signals or barrier semaphores. Data moves between devices by JAX's collectives and lax.ppermute only.
A program may use at most 192 MiB of HBM per device.

```python
import math
import jax
import jax.numpy as jnp
import numpy as np
from jax import lax

CH = 512
D = 1280
FFW = 2560
ROWS_DEV = 128
CAP = 6
SLOTS = 192
ROWS = 32768
N_DP = 32
N_FSDP = 8
DEVICES = 256


def touch_ends(values, key, least, top_value):
    extent = values.shape
    place = [jax.random.randint(jax.random.fold_in(key, axis), (), 0, extent[axis]) for axis in range(len(extent))]
    values = values.at[tuple(place)].set(least)
    longest = extent.index(max(extent))
    place[longest] = (place[longest] + 1) % extent[longest]
    return values.at[tuple(place)].set(top_value)


def strengthened(result, own_key, source, target, shards_of, factor):
    owner, partner = [(jnp.arange(result.shape[axis_at]) // (result.shape[axis_at] // shards_of)).reshape([-1 if axis == axis_at else 1 for axis in range(result.ndim)]) for axis_at in (source, target)]
    chosen = jax.random.permutation(own_key, shards_of)[partner]
    strong = (owner == chosen) | (owner == (partner + shards_of // 2) % shards_of)
    return jnp.where(strong, factor * result, result)


def block_levels(own_key, extent, shards, smallest, largest):
    def one(dim, parts):
        heights = jax.random.uniform(jax.random.fold_in(jax.random.fold_in(own_key, 6), dim), (parts,), jnp.float32, smallest / len(shards), largest / len(shards))
        return jnp.repeat(jnp.exp(heights), extent[dim] // parts).reshape((-1,) + (1,) * (len(extent) - dim - 1))

    gain = one(*shards[0])
    for cut in shards[1:]:
        gain = gain * one(*cut)
    return gain


def assign_block(stream_key, own, number, rows, amount, top, reach, slope):
    sequence = jax.random.permutation(stream_key, amount)
    heavy_load, usual = portions_of(amount, rows * top, reach, slope, True), portions_of(amount, rows * top, reach, slope, False)
    places = jnp.arange(amount)

    def named(sizes, rotation):
        used = int((sizes > 0).sum())
        fixed = max(1, used // 4)
        moved = fixed + (places - fixed + rotation * (used - fixed)) % max(1, amount - fixed)
        return jnp.zeros((amount,), jnp.int32).at[sequence[jnp.where(places < fixed, places, moved)]].set(jnp.asarray(sizes, jnp.int32))

    sizes = jnp.where(number % 4 == 0, named(heavy_load, number // 4), named(usual, number - number // 4 - 1))
    mixed = jax.random.permutation(jax.random.fold_in(own, 3), amount)
    source_of, sink = mixed[0:amount // 2 * 2:2], mixed[1:amount // 2 * 2:2]
    slack = jnp.minimum(sizes[source_of] - 1, reach - sizes[sink]) // 2
    slack = jnp.where((source_of == sequence[0]) | (sink == sequence[0]) | (sizes[sink] == 0), 0, jnp.maximum(slack, 0))
    moved = jax.random.randint(jax.random.fold_in(own, 4), (amount // 2,), 0, 1 << 20) % (slack + 1)
    sizes = sizes.at[source_of].add(-moved).at[sink].add(moved)
    members = jnp.searchsorted(jnp.cumsum(sizes), jnp.arange(rows * top), side="right").astype(jnp.int32)
    table = members.reshape(top, rows).T
    table = table[jax.random.permutation(jax.random.fold_in(own, 1), rows)]
    rotation = jax.random.randint(jax.random.fold_in(own, 2), (rows, 1), 0, top)
    return jnp.take_along_axis(table, (jnp.arange(top)[None, :] + rotation) % top, axis=1)


def portions_of(count, total, reach, lean, full):
    portions = [(1 << 20) // math.isqrt(rank ** lean) + 1 for rank in range(1, count + 1)]
    largest = reach if full else min(reach, max(-(-total // count), total * portions[0] // sum(portions)))
    least = 1 if total - largest >= count - 1 else 0
    holding, spare = [largest] + [least] * (count - 1), total - largest - least * (count - 1)
    while spare > 0:
        candidates = [i for i in range(1, count) if holding[i] < largest] or [i for i in range(1, count) if holding[i] < reach]
        mass, budget = sum([portions[i] for i in candidates]), spare
        for i in candidates:
            more = min(reach - holding[i], max(1, budget * portions[i] // mass), spare)
            holding[i] = holding[i] + more
            spare = spare - more
    return np.array(holding)


def bell_draw(stream_key, shape, scale, reach, pieces=(), kind=jnp.bfloat16):
    level = block_levels(stream_key, shape, pieces, -0.22, 0.18) if pieces else 1.0
    drawn = jax.random.normal(stream_key, shape, jnp.float32) * scale * level
    return jnp.minimum(jnp.maximum(drawn, -reach), reach).astype(kind)


def bell_draw_with(key, shape, width, bound, cuts, heavy, held_as=jnp.bfloat16):
    array = width * jax.random.normal(key, shape, jnp.float32)
    if cuts:
        array = array * block_levels(key, shape, cuts, -0.22, 0.18)
    return jnp.clip(strengthened(array, jax.random.fold_in(key, 3), *heavy), -bound, bound).astype(held_as)


def setup_inputs(seed: int = 0) -> dict:
    streams_of = jax.random.split(jax.random.key(seed), 8)
    waveform_rows = bell_draw(streams_of[0], (ROWS, 2 * CH), 1.0, 6.0, ((0, 256),))
    conv_weight = bell_draw(streams_of[1], (2 * CH, CH), (2 * CH) ** -0.5, 0.1875, ((0, 8),))
    proj_weight = bell_draw(streams_of[2], (CH, D), CH ** -0.5, 0.25, ((0, 8),))
    ffn_pair = bell_draw(streams_of[3], (FFW, 2, D), D ** -0.5, 0.15625, ((0, 8), (2, 32)))
    owner_keys = jax.random.split(jax.random.fold_in(streams_of[4], 1), ROWS // ROWS_DEV)
    owner_turns = jax.random.permutation(jax.random.fold_in(streams_of[4], 3), ROWS // ROWS_DEV)
    owner = jax.vmap(lambda own, number: assign_block(jax.random.fold_in(streams_of[4], 2), own, number, ROWS_DEV, N_DP, 1, CAP, 0))(owner_keys, owner_turns).reshape((ROWS, 1))
    frame_live = touch_ends((jax.random.randint(streams_of[5], (ROWS,), 0, 4) < 3).astype(jnp.int32), jax.random.fold_in(streams_of[5], 1), 0, 1)
    cotangent = bell_draw_with(streams_of[6], (DEVICES * SLOTS, D), ROWS ** -0.5, 0.125, ((0, 256),), (0, 1, 256, 6.0))
    return {"waveform_rows": waveform_rows, "conv_weight": conv_weight, "proj_weight": proj_weight, "ffn_pair": ffn_pair, "owner": owner, "frame_live": frame_live, "cotangent": cotangent}


epsilon = 1e-05

def gelu_exact(values):
    return jax.nn.gelu(values, approximate=False)

def gelu_slope(values):
    cumulative = 0.5 * (1.0 + lax.erf(values * 0.7071067811865476))
    density = jnp.exp(-0.5 * values * values) * 0.3989422804014327
    return cumulative + values * density

def normalize(values):
    mean_value = lax.optimization_barrier(jnp.mean(values, axis=-1, keepdims=True))
    centered = values - mean_value
    variance = lax.optimization_barrier(jnp.mean(centered * centered, axis=-1, keepdims=True))
    return centered * lax.rsqrt(variance + epsilon)

def reference(waveform_rows, conv_weight, proj_weight, ffn_pair, owner, frame_live, cotangent):
    target = owner[:, 0].reshape(DEVICES, ROWS_DEV)
    onehot = (target[:, :, None] == jnp.arange(N_DP, dtype=jnp.int32)[None, None, :]).astype(jnp.int32)
    before = jnp.cumsum(onehot, axis=1) - onehot
    position = lax.optimization_barrier(jnp.sum(before * onehot, axis=2)).astype(jnp.int32)
    device_ids = jnp.arange(DEVICES, dtype=jnp.int32)
    source_dp = device_ids // N_FSDP
    source_fsdp = device_ids % N_FSDP
    destination = ((target * N_FSDP + source_fsdp[:, None]) * SLOTS + source_dp[:, None] * CAP + position).reshape(-1).astype(jnp.int32)
    incoming = jnp.zeros((DEVICES * SLOTS, 2 * CH), jnp.bfloat16).at[destination].set(waveform_rows)
    slot_flags = jnp.zeros((DEVICES * SLOTS,), jnp.int32).at[destination].set(1 + frame_live)
    up_rows = ffn_pair[:, 0, :]
    down_rows = ffn_pair[:, 1, :]

    def one_device(total, inputs):
        row_block, flags_block, cot_block = inputs
        conv_out = jnp.dot(row_block, conv_weight, preferred_element_type=jnp.float32)
        features = normalize(gelu_exact(conv_out)).astype(jnp.bfloat16)
        stream = jnp.dot(features, proj_weight, preferred_element_type=jnp.float32).astype(jnp.bfloat16)
        stream_wide = stream.astype(jnp.float32)
        normed = normalize(stream_wide).astype(jnp.bfloat16)
        hidden_pre = jnp.dot(normed, up_rows.T, preferred_element_type=jnp.float32)
        hidden = gelu_exact(hidden_pre).astype(jnp.bfloat16)
        mixed = stream_wide + jnp.dot(hidden, down_rows, preferred_element_type=jnp.float32)
        occupied = (flags_block > 0).astype(jnp.float32)
        encoded = (mixed * occupied[:, None]).astype(jnp.bfloat16)
        live_mask = (flags_block == 2).astype(jnp.bfloat16)
        grad_out = cot_block * live_mask[:, None]
        grad_hidden = jnp.dot(grad_out, down_rows.T, preferred_element_type=jnp.float32)
        grad_pre = (grad_hidden * gelu_slope(hidden_pre)).astype(jnp.bfloat16)
        up_term = jnp.dot(grad_pre.T, normed, preferred_element_type=jnp.float32)
        down_term = jnp.dot(hidden.T, grad_out, preferred_element_type=jnp.float32)
        term = jnp.stack([up_term, down_term], axis=1).astype(jnp.bfloat16)
        term = lax.optimization_barrier(term)
        return (total + term.astype(jnp.float32), encoded)
    start_total = jnp.zeros((FFW, 2, D), jnp.float32)
    inputs = (incoming.reshape(DEVICES, SLOTS, 2 * CH), slot_flags.reshape(DEVICES, SLOTS), cotangent.reshape(DEVICES, SLOTS, D))
    grad_pair, encoded = lax.scan(one_device, start_total, inputs)
    return (encoded.reshape(DEVICES * SLOTS, D), grad_pair)
```

```python
import jax
import jax.numpy as jnp
import numpy as np
from jax import lax
from jax.sharding import Mesh
from jax.sharding import PartitionSpec as P

epsilon = 1e-05
bf16 = jnp.bfloat16
f32 = jnp.float32

CAP = 6
PAD = 8


def gelu_exact(values):
    return jax.nn.gelu(values, approximate=False)


def gelu_slope(values):
    cumulative = 0.5 * (1.0 + lax.erf(values * 0.7071067811865476))
    density = jnp.exp(-0.5 * values * values) * 0.3989422804014327
    return cumulative + values * density


def normalize(values):
    mean_value = jnp.mean(values, axis=-1, keepdims=True)
    centered = values - mean_value
    variance = jnp.mean(centered * centered, axis=-1, keepdims=True)
    return centered * lax.rsqrt(variance + epsilon)


def gathered(values, axis, count):
    spread = jnp.broadcast_to(values[None], (count,) + values.shape)
    return lax.all_to_all(spread, axis, split_axis=0, concat_axis=0, tiled=True)


def dot(a, b, dims=((1,), (0,))):
    return lax.dot_general(a, b, (dims, ((), ())), preferred_element_type=f32)


def per_device(waveform_rows, conv_weight, proj_weight, ffn_pair, owner, frame_live, cotangent):
    n_dp = 32
    slots = n_dp * CAP
    dp = ("zh", "x", "c")
    fsdp = ("y", "zl")
    z = ("zh", "zl")
    local_pair = jnp.transpose(ffn_pair, (2, 1, 0)).reshape(40, 640)
    pair = lax.all_gather(local_pair, ("zh", "x", "c", "zl"), axis=0, tiled=True)
    cot_all = lax.all_gather(cotangent, "y", axis=0, tiled=True)

    target = owner[:, 0]
    onehot = (target[:, None] == jnp.arange(n_dp, dtype=jnp.int32)[None, :]).astype(jnp.int32)
    before = jnp.cumsum(onehot, axis=0) - onehot
    position = jnp.sum(before * onehot, axis=1)
    slot_index = target * PAD + position
    matches = slot_index[None, :] == jnp.arange(n_dp * PAD, dtype=jnp.int32)[:, None]
    outgoing = dot(matches.astype(bf16), waveform_rows).astype(bf16)
    flags = jnp.sum(jnp.where(matches, (1 + frame_live)[None, :], 0), axis=1).astype(bf16)
    flags = jnp.pad(flags.reshape(n_dp, 1, PAD), ((0, 0), (0, 0), (0, 1024 - PAD)))
    outgoing = jnp.concatenate(
        [outgoing.reshape(n_dp, PAD, 1024)[:, :CAP], flags, jnp.zeros_like(flags)], axis=1
    )
    incoming = lax.all_to_all(outgoing, dp, split_axis=0, concat_axis=0, tiled=True)
    conv_full = gathered(conv_weight, fsdp, 8).reshape(1024, 512)
    proj_full = gathered(proj_weight, fsdp, 8).reshape(512, 1280)

    slot_flags = incoming[:, CAP, :CAP].reshape(1, slots)
    rows = incoming[:, :CAP].reshape(slots, 1024)
    own_features = normalize(gelu_exact(dot(rows, conv_full))).astype(bf16)
    flag_rows = jnp.pad(slot_flags, ((0, 15), (0, 512 - slots)))
    block = jnp.concatenate([own_features, flag_rows], axis=0)
    blocks = gathered(block, "y", 4)
    features = blocks[:, :slots].reshape(4 * slots, 512)
    all_flags = blocks[:, slots, :slots].reshape(4 * slots)

    stream = dot(features, proj_full).astype(bf16)
    normed = normalize(stream.astype(f32)).astype(bf16)
    pair = pair.reshape(32, 2, 40, 2, 320)
    weights = jnp.transpose(pair, (3, 0, 2, 1, 4)).reshape(2, 1280, 640)
    up, down = weights[0], weights[1]
    hidden_pre = dot(normed, up)
    hidden = gelu_exact(hidden_pre).astype(bf16)
    partial = dot(hidden, down, ((1,), (1,))).reshape(4, slots, 1280)
    y = lax.axis_index("y")
    own = lax.dynamic_index_in_dim(partial, y, 0, keepdims=False)
    own = own + lax.dynamic_slice_in_dim(stream, y * slots, slots, 0).astype(f32)
    rest = partial.astype(bf16)
    for step in range(1, 4):
        piece = lax.dynamic_index_in_dim(rest, lax.rem(y + step, 4), 0, keepdims=False)
        arrived = lax.ppermute(piece, "y", [(k, (k + step) % 4) for k in range(4)])
        own = own + arrived.astype(f32)
    occupied = (slot_flags.reshape(slots) > 0).astype(f32)
    encoded = (own * occupied[:, None]).astype(bf16)

    live_mask = (all_flags == 2).astype(bf16)
    grad_out = cot_all * live_mask[:, None]
    grad_hidden = dot(grad_out, down)
    grad_pre = (grad_hidden * gelu_slope(hidden_pre)).astype(bf16)
    first = ((0,), (0,))
    up_term = dot(normed, grad_pre, first)
    down_term = dot(grad_out, hidden, first)
    terms = jnp.stack([up_term, down_term]).astype(bf16).reshape(2, 4, 4, 2, 40, 2, 320)
    terms = jnp.transpose(terms, (3, 2, 1, 5, 4, 0, 6)).reshape(2, 1280, 640)
    c = lax.axis_index("c")
    away = lax.dynamic_index_in_dim(terms, 1 - c, 0, keepdims=False)
    kept = lax.dynamic_index_in_dim(terms, c, 0, keepdims=False)
    arrived = lax.ppermute(away, "c", [(0, 1), (1, 0)])
    total = (kept.astype(f32) + arrived.astype(f32)).astype(bf16).reshape(4, 320, 640)
    total = lax.all_to_all(total, "x", split_axis=0, concat_axis=0, tiled=True)
    total = jnp.sum(total.astype(f32), axis=0).astype(bf16).reshape(8, 40, 640)
    total = lax.all_to_all(total, z, split_axis=0, concat_axis=0, tiled=True)
    total = jnp.sum(total.astype(f32), axis=0)
    grad_pair = jnp.transpose(total.reshape(40, 2, 320), (2, 1, 0))
    return (encoded, grad_pair)


def solution(mesh):
    names = ("zh", "x", "c", "y", "zl")
    fine = Mesh(np.asarray(mesh.devices).reshape(4, 4, 2, 4, 2), names)
    dp = ("zh", "x", "c")
    fsdp = ("y", "zl")
    everyone = dp + fsdp
    return jax.shard_map(
        per_device,
        mesh=fine,
        in_specs=(
            P(everyone, None),
            P(fsdp, None),
            P(fsdp, None),
            P(fsdp, None, dp),
            P(everyone, None),
            P(everyone),
            P(everyone, None),
        ),
        out_specs=(P(everyone, None), P(fsdp, None, dp)),
        check_vma=False,
    )
```

```python
import functools

import jax
import jax.numpy as jnp
import numpy as np
from jax import lax
from jax.experimental import pallas as pl
from jax.experimental.pallas import tpu as pltpu
from jax.sharding import Mesh
from jax.sharding import PartitionSpec as P

epsilon = 1e-05
bf16 = jnp.bfloat16
f32 = jnp.float32
i32 = jnp.int32

N_DP = 32
CAP = 6
PAD = 8
SLOTS = 192
CH = 512
D = 1280
UNITS = 320
LANES = 384
WIDE = 2 * LANES
BLOCK = 40
ZX = ("zh", "zl")

VMEM = pl.BlockSpec(memory_space=pltpu.VMEM)
SMEM = pl.BlockSpec(memory_space=pltpu.SMEM)


def dot(a, b, dims=((1,), (0,))):
    return lax.dot_general(a, b, (dims, ((), ())), preferred_element_type=f32)


def iota(shape, dim):
    return lax.broadcasted_iota(i32, shape, dim)


def normalize(values):
    mean_value = jnp.mean(values, axis=-1, keepdims=True)
    centered = values - mean_value
    variance = jnp.mean(centered * centered, axis=-1, keepdims=True)
    return centered * lax.rsqrt(variance + epsilon)


def call(kernel, out_shape, args, flops, bytes_accessed, scratch=(), vmem=48 << 20, smem=0, name=None):
    return pl.pallas_call(
        kernel,
        out_shape=out_shape,
        in_specs=[SMEM] * smem + [VMEM] * (len(args) - smem),
        out_specs=jax.tree.map(lambda _: VMEM, out_shape),
        scratch_shapes=list(scratch),
        compiler_params=pltpu.CompilerParams(vmem_limit_bytes=vmem),
        cost_estimate=pl.CostEstimate(
            flops=flops, bytes_accessed=bytes_accessed, transcendentals=0
        ),
        name=name,
    )(*args)


def pack_kernel(pair, packed):
    up = pair[0].astype(f32)
    down = pair[1].astype(f32)
    blank = jnp.zeros((BLOCK, LANES - UNITS), f32)
    up = jnp.concatenate([up, blank], axis=1)
    down = jnp.concatenate([down, blank], axis=1)
    packed[...] = pack_pair(up, down).astype(bf16)


def pack_pair(up, down):
    turned = pltpu.roll(down, 64, 1)
    lane = iota((BLOCK, 128), 1)
    middle = jnp.where(lane < 64, up[:, 256:], turned[:, :128])
    return jnp.concatenate([up[:, :256], middle, turned[:, 128:]], axis=1)


def unpack_pair(packed):
    used = iota((BLOCK, LANES), 1) < UNITS
    up = jnp.where(used, packed[:, :LANES], 0.0)
    down = pltpu.roll(packed[:, 256:], LANES - 64, 1)
    return up, jnp.where(used, down, 0.0)


def route_kernel(owner, live, rows, outgoing):
    count = rows.shape[0]
    target = owner[...]
    onehot = (target == iota((count, 128), 1)).astype(f32)
    earlier = (iota((count, count), 1) < iota((count, count), 0)).astype(bf16)
    before = dot(earlier, onehot.astype(bf16))
    position = jnp.sum(before * onehot, axis=1, keepdims=True).astype(i32)
    diagonal = iota((count, count), 0) == iota((count, count), 1)
    state = 1.0 + jnp.sum(
        jnp.where(diagonal, live[...].astype(f32), 0.0), axis=1, keepdims=True
    )
    slot = iota((count, N_DP * PAD), 1)
    placement = (target * PAD + position == slot).astype(bf16)
    flag_row = (target * PAD + CAP == slot).astype(bf16)
    flag_value = jnp.where(position == iota((count, 128), 1), state, 0.0).astype(bf16)
    first = ((0,), (0,))
    outgoing[...] = dot(placement, rows[...], first).astype(bf16)
    flags = dot(flag_row, flag_value, first)
    outgoing[:, :128] = (outgoing[:, :128].astype(f32) + flags).astype(bf16)


def front_kernel(place, incoming, *refs):
    pieces, (block, flags_out, conv) = refs[:4], refs[4:]
    y, zl = place[0], place[1]
    for step in range(4):
        for other in range(2):
            start = lax.rem(y - step + 4, 4) * 256 + lax.rem(zl + other, 2) * 128
            conv[pl.ds(pl.multiple_of(start, 128), 128), :] = pieces[step][
                other * 128 : other * 128 + 128, :
            ]
    raw = incoming[...]
    conv_out = dot(raw, conv[...])
    active = 0.5 * conv_out * (1.0 + lax.erf(conv_out * 0.7071067811865476))
    features = normalize(active).astype(bf16)
    slot = iota((SLOTS, N_DP * PAD), 0)
    row = iota((SLOTS, N_DP * PAD), 1)
    owner, rank = slot // CAP, slot % CAP
    compact = (row == owner * PAD + rank).astype(bf16)
    block[:SLOTS, :] = dot(compact, features).astype(bf16)
    flag_rows = dot((row == owner * PAD + CAP).astype(bf16), raw[:, :128])
    lane = iota((SLOTS, 128), 1)
    flags = jnp.sum(
        jnp.where(lane == iota((SLOTS, 128), 0) % CAP, flag_rows, 0.0), axis=1, keepdims=True
    )
    flags_out[...] = flags
    wide = iota((SLOTS, CH), 1) == iota((SLOTS, CH), 0)
    as_row = jnp.sum(jnp.where(wide, flags, 0.0), axis=0, keepdims=True)
    block[SLOTS:, :] = jnp.broadcast_to(as_row, (16, CH)).astype(bf16)


def weights_kernel(place, *refs):
    pieces, (up, down, wide_up, wide_down) = refs[:8], refs[8:]
    zh, x, c, zl = place[0], place[1], place[2], place[3]
    for core in range(2):
        for step in range(4):
            piece = pieces[core * 4 + step]
            base = lax.rem(x - step + 4, 4) * 80 + lax.rem(c + core, 2) * 40

            def one(k, carry):
                row = lax.rem(zh - k // 2 + 4, 4) * 320 + base
                half = lax.rem(zl + k, 2)
                rows = pl.ds(pl.multiple_of(row, 8), BLOCK)
                a, b = unpack_pair(piece[k].astype(f32))
                wide_up[half, rows, :] = a
                wide_down[half, rows, :] = b
                return carry

            lax.fori_loop(0, 8, one, 0)
    for half in range(2):
        up[:, half * LANES : (half + 1) * LANES] = wide_up[half].astype(bf16)
        down[:, half * LANES : (half + 1) * LANES] = wide_down[half].astype(bf16)


def ffn_kernel(place, cot, up, down, *refs):
    blocks, protos, refs = refs[:4], refs[4:8], refs[8:]
    own, away1, away2, away3, kept, sent, refs = *refs[:6], refs[6:]
    proj, feats, live, normed, hidden, grad_pre, grad_out, wide_up, wide_down = refs
    y, zl, c = place[0], place[1], place[2]
    for step in range(4):
        for other in range(2):
            start = lax.rem(y - step + 4, 4) * 128 + lax.rem(zl + other, 2) * 64
            proj[pl.ds(pl.multiple_of(start, 64), 64), :] = protos[step][
                other * 64 : other * 64 + 64, :
            ]
        feats[step] = blocks[step][:SLOTS, :]
        flags = blocks[step][SLOTS : SLOTS + 16, :].astype(f32)[:1, :]
        wide = iota((SLOTS, CH), 1) == iota((SLOTS, CH), 0)
        flags = jnp.sum(jnp.where(wide, flags, 0.0), axis=1, keepdims=True)
        live[step] = (flags == 2.0).astype(f32)

    def forward(step, carry):
        rows = pl.ds(pl.multiple_of(step * SLOTS, SLOTS), SLOTS)
        stream = dot(feats[step], proj[...]).astype(bf16).astype(f32)
        normed[rows, :] = normalize(stream).astype(bf16)
        pre = dot(normed[rows, :], up[...])
        cumulative = 0.5 * (1.0 + lax.erf(pre * 0.7071067811865476))
        density = jnp.exp(-0.5 * pre * pre) * 0.3989422804014327
        hidden[rows, :] = (pre * cumulative).astype(bf16)
        slope = cumulative + pre * density
        partial = dot(hidden[rows, :], down[...], ((1,), (1,)))

        @pl.when(step == 0)
        def _():
            own[...] = partial + stream

        for k, away in enumerate((away1, away2, away3)):

            @pl.when(step == k + 1)
            def _():
                away[...] = partial.astype(bf16)

        there = lax.rem(y - step + 4, 4) * SLOTS
        masked = cot[pl.ds(pl.multiple_of(there, SLOTS), SLOTS), :].astype(f32) * live[step]
        grad_out[rows, :] = masked.astype(bf16)
        grad_hidden = dot(grad_out[rows, :], down[...])
        grad_pre[rows, :] = (grad_hidden * slope).astype(bf16)
        return carry

    lax.fori_loop(0, 4, forward, 0)

    def backward(part, carry):
        columns = pl.ds(pl.multiple_of(part * 640, 640), 640)
        first = ((0,), (0,))
        wide_up[...] = dot(normed[:, columns], grad_pre[...], first)
        wide_down[...] = dot(grad_out[:, columns], hidden[...], first)

        def place_block(k, carry):
            zh, x = k // 4, lax.rem(k, 4)
            for other, out in enumerate((kept, sent)):
                row = zh * 320 + x * 80 + lax.rem(c + other, 2) * BLOCK
                rows = pl.ds(pl.multiple_of(row, 8), BLOCK)
                for half in range(2):
                    lanes = slice(half * LANES, (half + 1) * LANES)
                    block = pack_pair(wide_up[rows, lanes], wide_down[rows, lanes])
                    out[x, (part * 2 + zh) * 2 + half] = block.astype(bf16)
            return carry

        lax.fori_loop(0, 8, place_block, 0)
        return carry

    lax.fori_loop(0, 2, backward, 0)


def last_kernel(arrived, out):
    total = arrived[0].astype(f32)
    for k in range(1, 8):
        total = total + arrived[k].astype(f32)
    up, down = unpack_pair(total)
    out[0] = up[:, :UNITS]
    out[1] = down[:, :UNITS]


def ring(values, axis, size, step):
    return lax.ppermute(values, axis, [(k, (k + step) % size) for k in range(size)])


def around(values, axis, size):
    return [values] + [ring(values, axis, size, step) for step in range(1, size)]


def per_device(waveform_rows, conv_weight, proj_weight, ffn_pair, owner, frame_live, cotangent):
    dp = ("zh", "x", "c")
    zh, x, c, y, zl = (lax.axis_index(name).astype(i32) for name in ("zh", "x", "c", "y", "zl"))
    cot_all = lax.all_gather(cotangent, "y", axis=0, tiled=True)

    packed = call(
        pack_kernel,
        jax.ShapeDtypeStruct((BLOCK, 2 * UNITS), bf16),
        [jnp.transpose(ffn_pair, (1, 2, 0))],
        1 << 16, 1 << 17, name="pack",
    )
    both = jnp.stack([packed, ring(packed, "zl", 2, 1)])
    along_z = jnp.concatenate(around(both, "zh", 4), axis=0)
    along_x = around(along_z, "x", 4)
    pieces = along_x + [ring(piece, "c", 2, 1) for piece in along_x]

    conv_pair = jnp.concatenate([conv_weight, ring(conv_weight, "zl", 2, 1)], axis=0)
    conv_pieces = around(conv_pair, "y", 4)
    proj_pair = jnp.concatenate([proj_weight, ring(proj_weight, "zl", 2, 1)], axis=0)
    proj_pieces = around(proj_pair, "y", 4)

    outgoing = call(
        route_kernel,
        jax.ShapeDtypeStruct((N_DP * PAD, 1024), bf16),
        [owner, frame_live.reshape(1, -1), waveform_rows],
        2 * 256 * 128 * 1152, 1 << 20, name="route",
    )
    incoming = lax.all_to_all(
        outgoing.reshape(N_DP, PAD, 1024), dp, split_axis=0, concat_axis=0, tiled=True
    ).reshape(N_DP * PAD, 1024)

    block, flags = call(
        front_kernel,
        (
            jax.ShapeDtypeStruct((SLOTS + 16, CH), bf16),
            jax.ShapeDtypeStruct((SLOTS, 1), f32),
        ),
        [jnp.stack([y, zl]), incoming, *conv_pieces],
        2 * 256 * 1024 * 512, 2 << 20,
        scratch=[pltpu.VMEM((1024, CH), bf16)], smem=1, name="front",
    )
    blocks = around(block, "y", 4)

    up, down = call(
        weights_kernel,
        (jax.ShapeDtypeStruct((D, WIDE), bf16),) * 2,
        [jnp.stack([zh, x, c, zl]), *pieces],
        1 << 22, 8 << 20,
        scratch=[pltpu.VMEM((2, D, LANES), f32)] * 2, smem=1, name="weights",
    )
    rows = 4 * SLOTS
    piece = jax.ShapeDtypeStruct((SLOTS, D), bf16)
    terms = jax.ShapeDtypeStruct((4, 8, BLOCK, 2 * UNITS), bf16)
    own, away1, away2, away3, kept, sent = call(
        ffn_kernel,
        (jax.ShapeDtypeStruct((SLOTS, D), f32), piece, piece, piece, terms, terms),
        [jnp.stack([y, zl, c]), cot_all, up, down, *blocks, *proj_pieces],
        2 * rows * D * (CH + 5 * WIDE), 16 << 20,
        scratch=[
            pltpu.VMEM((CH, D), bf16),
            pltpu.VMEM((4, SLOTS, CH), bf16),
            pltpu.VMEM((4, SLOTS, 1), f32),
            pltpu.VMEM((rows, D), bf16),
            pltpu.VMEM((rows, WIDE), bf16),
            pltpu.VMEM((rows, WIDE), bf16),
            pltpu.VMEM((rows, D), bf16),
            pltpu.VMEM((640, WIDE), f32),
            pltpu.VMEM((640, WIDE), f32),
        ],
        smem=1, name="ffn",
    )
    for step, away in ((1, away1), (2, away2), (3, away3)):
        own = own + ring(away, "y", 4, 4 - step).astype(f32)
    encoded = (own * (flags > 0).astype(f32)).astype(bf16)

    total = kept.astype(f32) + ring(sent, "c", 2, 1).astype(f32)
    total = lax.all_to_all(total.astype(bf16), "x", split_axis=0, concat_axis=0, tiled=True)
    total = jnp.sum(total.astype(f32), axis=0).astype(bf16)
    total = lax.all_to_all(total, ZX, split_axis=0, concat_axis=0, tiled=True)
    grad_pair = call(
        last_kernel,
        jax.ShapeDtypeStruct((2, BLOCK, UNITS), f32),
        [total],
        1 << 18, 1 << 19, name="last",
    )
    return (encoded, jnp.transpose(grad_pair, (2, 0, 1)))


def solution(mesh):
    names = ("zh", "x", "c", "y", "zl")
    fine = Mesh(np.asarray(mesh.devices).reshape(4, 4, 2, 4, 2), names)
    dp = ("zh", "x", "c")
    fsdp = ("y", "zl")
    everyone = dp + fsdp
    return jax.shard_map(
        per_device,
        mesh=fine,
        in_specs=(
            P(everyone, None),
            P(fsdp, None),
            P(fsdp, None),
            P(fsdp, None, dp),
            P(everyone, None),
            P(everyone),
            P(everyone, None),
        ),
        out_specs=(P(everyone, None), P(fsdp, None, dp)),
        check_vma=False,
    )
```

```python
import functools

import jax
import jax.numpy as jnp
import numpy as np
from jax import lax
from jax.experimental import pallas as pl
from jax.experimental.pallas import tpu as pltpu
from jax.sharding import Mesh
from jax.sharding import PartitionSpec as P

epsilon = 1e-05
bf16 = jnp.bfloat16
f32 = jnp.float32
i32 = jnp.int32

N_DP = 32
CAP = 6
PAD = 8
SLOTS = 192
CH = 512
D = 1280
UNITS = 320
LANES = 384
WIDE = 2 * LANES
BLOCK = 40
ZX = ("zh", "zl")

VMEM = pl.BlockSpec(memory_space=pltpu.VMEM)
SMEM = pl.BlockSpec(memory_space=pltpu.SMEM)
HBM = pl.BlockSpec(memory_space=pltpu.HBM)


def dot(a, b, dims=((1,), (0,))):
    return lax.dot_general(a, b, (dims, ((), ())), preferred_element_type=f32)


def iota(shape, dim):
    return lax.broadcasted_iota(i32, shape, dim)


def normalize(values):
    mean_value = jnp.mean(values, axis=-1, keepdims=True)
    centered = values - mean_value
    variance = jnp.mean(centered * centered, axis=-1, keepdims=True)
    return centered * lax.rsqrt(variance + epsilon)


def call(kernel, out_shape, args, flops, bytes_accessed, scratch=(), vmem=12 << 20, smem=0, hbm=0, name=None):
    return pl.pallas_call(
        kernel,
        out_shape=out_shape,
        in_specs=[SMEM] * smem + [VMEM] * (len(args) - smem - hbm) + [HBM] * hbm,
        out_specs=jax.tree.map(lambda _: VMEM, out_shape),
        scratch_shapes=list(scratch),
        compiler_params=pltpu.CompilerParams(vmem_limit_bytes=vmem),
        cost_estimate=pl.CostEstimate(
            flops=flops, bytes_accessed=bytes_accessed, transcendentals=0
        ),
        name=name,
    )(*args)


def pack_kernel(pair, packed):
    up = pair[0].astype(f32)
    down = pair[1].astype(f32)
    blank = jnp.zeros((BLOCK, LANES - UNITS), f32)
    up = jnp.concatenate([up, blank], axis=1)
    down = jnp.concatenate([down, blank], axis=1)
    packed[...] = pack_pair(up, down).astype(bf16)


def pack_pair(up, down):
    turned = pltpu.roll(down, 64, 1)
    lane = iota((BLOCK, 128), 1)
    middle = jnp.where(lane < 64, up[:, 256:], turned[:, :128])
    return jnp.concatenate([up[:, :256], middle, turned[:, 128:]], axis=1)


def unpack_pair(packed):
    used = iota((BLOCK, LANES), 1) < UNITS
    up = jnp.where(used, packed[:, :LANES], 0.0)
    down = pltpu.roll(packed[:, 256:], LANES - 64, 1)
    return up, jnp.where(used, down, 0.0)


def route_kernel(owner, live, rows, outgoing):
    count = rows.shape[0]
    diagonal = iota((count, count), 0) == iota((count, count), 1)
    target = jnp.sum(jnp.where(diagonal, owner[...], 0), axis=1, keepdims=True)
    onehot = (target == iota((count, 128), 1)).astype(f32)
    earlier = (iota((count, count), 1) < iota((count, count), 0)).astype(bf16)
    before = dot(earlier, onehot.astype(bf16))
    position = jnp.sum(before * onehot, axis=1, keepdims=True).astype(i32)
    state = 1.0 + jnp.sum(
        jnp.where(diagonal, live[...].astype(f32), 0.0), axis=1, keepdims=True
    )
    slot = iota((count, N_DP * PAD), 1)
    placement = (target * PAD + position == slot).astype(bf16)
    flag_row = (target * PAD + CAP == slot).astype(bf16)
    flag_value = jnp.where(position == iota((count, 128), 1), state, 0.0).astype(bf16)
    first = ((0,), (0,))
    outgoing[...] = dot(placement, rows[...], first).astype(bf16)
    flags = dot(flag_row, flag_value, first)
    outgoing[:, :128] = (outgoing[:, :128].astype(f32) + flags).astype(bf16)


def front_kernel(place, incoming, *refs):
    pieces, (block, flags_out, conv, arrival) = refs[:8], refs[8:]
    y, zl = place[0], place[1]
    copies = []
    for step in range(4):
        for other in range(2):
            k = step * 2 + other
            start = lax.rem(y - step + 4, 4) * 256 + lax.rem(zl + other, 2) * 128
            rows = pl.ds(pl.multiple_of(start, 128), 128)
            copies.append(pltpu.make_async_copy(pieces[k], conv.at[rows, :], arrival.at[k]))
            copies[-1].start()
    for copy in copies:
        copy.wait()
    raw = incoming[...]
    conv_out = dot(raw, conv[...])
    active = 0.5 * conv_out * (1.0 + lax.erf(conv_out * 0.7071067811865476))
    features = normalize(active).astype(bf16)
    slot = iota((SLOTS, N_DP * PAD), 0)
    row = iota((SLOTS, N_DP * PAD), 1)
    owner, rank = slot // CAP, slot % CAP
    compact = (row == owner * PAD + rank).astype(bf16)
    block[:SLOTS, :] = dot(compact, features).astype(bf16)
    flag_rows = dot((row == owner * PAD + CAP).astype(bf16), raw[:, :128])
    lane = iota((SLOTS, 128), 1)
    flags = jnp.sum(
        jnp.where(lane == iota((SLOTS, 128), 0) % CAP, flag_rows, 0.0), axis=1, keepdims=True
    )
    flags_out[...] = flags
    wide = iota((SLOTS, CH), 1) == iota((SLOTS, CH), 0)
    as_row = jnp.sum(jnp.where(wide, flags, 0.0), axis=0, keepdims=True)
    block[SLOTS:, :] = jnp.broadcast_to(as_row, (16, CH)).astype(bf16)


def weights_kernel(place, *refs):
    pieces, (up, down, wide_up, wide_down) = refs[:8], refs[8:]
    z, x, c = place[0], place[1], place[2]
    for core in range(2):
        for step in range(4):
            piece = pieces[core * 4 + step]
            base = lax.rem(x - step + 4, 4) * 80 + lax.rem(c + core, 2) * 40

            def one(k, carry):
                there = lax.rem(z - k + 8, 8)
                row = (there // 2) * 320 + base
                half = lax.rem(there, 2)
                rows = pl.ds(pl.multiple_of(row, 8), BLOCK)
                a, b = unpack_pair(piece[k].astype(f32))
                wide_up[half, rows, :] = a
                wide_down[half, rows, :] = b
                return carry

            lax.fori_loop(0, 8, one, 0, unroll=True)
    for half in range(2):
        up[:, half * LANES : (half + 1) * LANES] = wide_up[half].astype(bf16)
        down[:, half * LANES : (half + 1) * LANES] = wide_down[half].astype(bf16)


def ffn_kernel(place, cot_in, up_in, down_in, *refs):
    blocks, protos, refs = refs[:4], refs[4:8], refs[8:]
    own, away1, away2, away3, kept, sent, refs = *refs[:6], refs[6:]
    proj, feats, live, normed, hidden, grad_pre, grad_out, wide_up, wide_down, *refs = refs
    cot, up, down, arrival = refs
    y, zl, c = place[0], place[1], place[2]
    copies = []

    def fetch(source, target):
        copy = pltpu.make_async_copy(source, target, arrival.at[len(copies)])
        copy.start()
        copies.append(copy)

    for step in range(4):
        fetch(blocks[step], feats.at[step])
    for step in range(4):
        for other in range(2):
            start = lax.rem(y - step + 4, 4) * 128 + lax.rem(zl + other, 2) * 64
            rows = pl.ds(pl.multiple_of(start, 64), 64)
            fetch(protos[step].at[pl.ds(other * 64, 64), :], proj.at[rows, :])
    fetch(up_in, up)
    fetch(down_in, down)
    fetch(cot_in, cot)
    for copy in copies[:13]:
        copy.wait()
    for step in range(4):
        flags = feats[step, SLOTS : SLOTS + 16, :].astype(f32)[:1, :]
        wide = iota((SLOTS, CH), 1) == iota((SLOTS, CH), 0)
        flags = jnp.sum(jnp.where(wide, flags, 0.0), axis=1, keepdims=True)
        live[step] = (flags == 2.0).astype(f32)

    def forward(step, carry):
        rows = pl.ds(pl.multiple_of(step * SLOTS, SLOTS), SLOTS)
        stream = dot(feats[step, :SLOTS, :], proj[...]).astype(bf16).astype(f32)
        normed[rows, :] = normalize(stream).astype(bf16)
        pre = dot(normed[rows, :], up[...])
        cumulative = 0.5 * (1.0 + lax.erf(pre * 0.7071067811865476))
        density = jnp.exp(-0.5 * pre * pre) * 0.3989422804014327
        hidden[rows, :] = (pre * cumulative).astype(bf16)
        slope = cumulative + pre * density

        @pl.when(step == 0)
        def _():
            copies[13].wait()
            copies[14].wait()

        partial = dot(hidden[rows, :], down[...], ((1,), (1,)))

        @pl.when(step == 0)
        def _():
            own[...] = partial + stream

        for k, away in enumerate((away1, away2, away3)):

            @pl.when(step == k + 1)
            def _():
                away[...] = partial.astype(bf16)

        there = lax.rem(y - step + 4, 4) * SLOTS
        masked = cot[pl.ds(pl.multiple_of(there, SLOTS), SLOTS), :].astype(f32) * live[step]
        grad_out[rows, :] = masked.astype(bf16)
        grad_hidden = dot(grad_out[rows, :], down[...])
        grad_pre[rows, :] = (grad_hidden * slope).astype(bf16)
        return carry

    lax.fori_loop(0, 4, forward, 0)

    def backward(part, carry):
        columns = pl.ds(pl.multiple_of(part * 640, 640), 640)
        first = ((0,), (0,))
        wide_up[...] = dot(normed[:, columns], grad_pre[...], first)
        wide_down[...] = dot(grad_out[:, columns], hidden[...], first)

        def place_block(k, carry):
            zh, x = k // 4, lax.rem(k, 4)
            for other, out in enumerate((kept, sent)):
                row = zh * 320 + x * 80 + lax.rem(c + other, 2) * BLOCK
                rows = pl.ds(pl.multiple_of(row, 8), BLOCK)
                for half in range(2):
                    lanes = slice(half * LANES, (half + 1) * LANES)
                    block = pack_pair(wide_up[rows, lanes], wide_down[rows, lanes])
                    out[x, (part * 2 + zh) * 2 + half] = block.astype(bf16)
            return carry

        lax.fori_loop(0, 8, place_block, 0)
        return carry

    lax.fori_loop(0, 2, backward, 0)


def core_sum_kernel(place, kept, arrived, *outs):
    x = place[0]
    for step, out in enumerate(outs):
        there = lax.rem(x + step, 4)
        out[...] = (kept[there].astype(f32) + arrived[there].astype(f32)).astype(bf16)


def x_sum_kernel(*refs):
    total = refs[0][...].astype(f32)
    for ref in refs[1:-1]:
        total = total + ref[...].astype(f32)
    refs[-1][...] = total.astype(bf16)


def last_kernel(arrived, out):
    total = arrived[0].astype(f32)
    for k in range(1, 8):
        total = total + arrived[k].astype(f32)
    up, down = unpack_pair(total)
    out[0] = up[:, :UNITS]
    out[1] = down[:, :UNITS]


def ring(values, axis, size, step):
    return lax.ppermute(values, axis, [(k, (k + step) % size) for k in range(size)])


def around(values, axis, size):
    return [values] + [ring(values, axis, size, step) for step in range(1, size)]


def grid(values):
    pieces = []
    for step in range(8):
        dy, dz = step // 2, step % 2
        order = [(k, ((k // 2 + dy) % 4) * 2 + (k % 2 ^ dz)) for k in range(8)]
        pieces.append(lax.ppermute(values, ("y", "zl"), order) if step else values)
    return pieces


def per_device(waveform_rows, conv_weight, proj_weight, ffn_pair, owner, frame_live, cotangent):
    dp = ("zh", "x", "c")
    zh, x, c, y, zl = (lax.axis_index(name).astype(i32) for name in ("zh", "x", "c", "y", "zl"))
    cot_all = lax.all_gather(cotangent, "y", axis=0, tiled=True)

    packed = call(
        pack_kernel,
        jax.ShapeDtypeStruct((BLOCK, 2 * UNITS), bf16),
        [jnp.transpose(ffn_pair, (1, 2, 0))],
        1 << 16, 1 << 17, name="pack",
    )
    conv_pieces = grid(conv_weight)
    along_z = jnp.stack(around(packed, ZX, 8))
    along_x = around(along_z, "x", 4)
    proj_weight, _ = lax.optimization_barrier((proj_weight, conv_pieces[-1]))
    proj_pair = jnp.concatenate([proj_weight, ring(proj_weight, "zl", 2, 1)], axis=0)
    proj_pieces = around(proj_pair, "y", 4)

    outgoing = call(
        route_kernel,
        jax.ShapeDtypeStruct((N_DP * PAD, 1024), bf16),
        [owner.reshape(1, -1), frame_live.reshape(1, -1), waveform_rows],
        2 * 256 * 128 * 1152, 1 << 20, name="route",
    )
    incoming = lax.all_to_all(
        outgoing.reshape(N_DP, PAD, 1024), dp, split_axis=0, concat_axis=0, tiled=True
    ).reshape(N_DP * PAD, 1024)

    block, flags = call(
        front_kernel,
        (
            jax.ShapeDtypeStruct((SLOTS + 16, CH), bf16),
            jax.ShapeDtypeStruct((SLOTS, 1), f32),
        ),
        [jnp.stack([y, zl]), incoming, *conv_pieces],
        2 * 256 * 1024 * 512, 2 << 20,
        scratch=[pltpu.VMEM((1024, CH), bf16), pltpu.SemaphoreType.DMA((8,))],
        smem=1, hbm=8, name="front",
    )
    blocks = around(block, "y", 4)
    block, *along_x = lax.optimization_barrier((block, *along_x))
    pieces = along_x + [ring(piece, "c", 2, 1) for piece in along_x]

    up, down = call(
        weights_kernel,
        (jax.ShapeDtypeStruct((D, WIDE), bf16),) * 2,
        [jnp.stack([zh * 2 + zl, x, c]), *pieces],
        1 << 22, 8 << 20,
        scratch=[pltpu.VMEM((2, D, LANES), f32)] * 2, vmem=24 << 20, smem=1, name="weights",
    )
    rows = 4 * SLOTS
    piece = jax.ShapeDtypeStruct((SLOTS, D), bf16)
    terms = jax.ShapeDtypeStruct((4, 8, BLOCK, 2 * UNITS), bf16)
    own, away1, away2, away3, kept, sent = call(
        ffn_kernel,
        (jax.ShapeDtypeStruct((SLOTS, D), f32), piece, piece, piece, terms, terms),
        [jnp.stack([y, zl, c]), cot_all, up, down, *blocks, *proj_pieces],
        2 * rows * D * (CH + 5 * WIDE), 16 << 20,
        scratch=[
            pltpu.VMEM((CH, D), bf16),
            pltpu.VMEM((4, SLOTS + 16, CH), bf16),
            pltpu.VMEM((4, SLOTS, 1), f32),
            pltpu.VMEM((rows, D), bf16),
            pltpu.VMEM((rows, WIDE), bf16),
            pltpu.VMEM((rows, WIDE), bf16),
            pltpu.VMEM((rows, D), bf16),
            pltpu.VMEM((640, WIDE), f32),
            pltpu.VMEM((640, WIDE), f32),
            pltpu.VMEM((rows, D), bf16),
            pltpu.VMEM((D, WIDE), bf16),
            pltpu.VMEM((D, WIDE), bf16),
            pltpu.SemaphoreType.DMA((15,)),
        ],
        vmem=36 << 20, smem=1, hbm=11, name="ffn",
    )
    tile = jax.ShapeDtypeStruct((8, BLOCK, 2 * UNITS), bf16)
    parts = call(
        core_sum_kernel,
        (tile,) * 4,
        [x[None], kept, ring(sent, "c", 2, 1)],
        1 << 20, 5 << 20, smem=1, name="core_sum",
    )
    total = call(
        x_sum_kernel,
        tile,
        [parts[0]] + [ring(parts[step], "x", 4, step) for step in range(1, 4)],
        1 << 20, 2 << 20, name="x_sum",
    )
    away1, away2, away3, _ = lax.optimization_barrier((away1, away2, away3, parts[0]))
    for step, away in ((1, away1), (2, away2), (3, away3)):
        own = own + ring(away, "y", 4, 4 - step).astype(f32)
    encoded = (own * (flags > 0).astype(f32)).astype(bf16)
    total = lax.all_to_all(total, ZX, split_axis=0, concat_axis=0, tiled=True)
    grad_pair = call(
        last_kernel,
        jax.ShapeDtypeStruct((2, BLOCK, UNITS), f32),
        [total],
        1 << 18, 1 << 19, name="last",
    )
    return (encoded, jnp.transpose(grad_pair, (2, 0, 1)))


def solution(mesh):
    names = ("zh", "x", "c", "y", "zl")
    fine = Mesh(np.asarray(mesh.devices).reshape(4, 4, 2, 4, 2), names)
    dp = ("zh", "x", "c")
    fsdp = ("y", "zl")
    everyone = dp + fsdp
    return jax.shard_map(
        per_device,
        mesh=fine,
        in_specs=(
            P(everyone, None),
            P(fsdp, None),
            P(fsdp, None),
            P(fsdp, None, dp),
            P(everyone, None),
            P(everyone),
            P(everyone, None),
        ),
        out_specs=(P(everyone, None), P(fsdp, None, dp)),
        check_vma=False,
    )
```

```python
import functools

import jax
import jax.numpy as jnp
import numpy as np
from jax import lax
from jax.experimental import pallas as pl
from jax.experimental.pallas import tpu as pltpu
from jax.sharding import Mesh
from jax.sharding import PartitionSpec as P

epsilon = 1e-05
bf16 = jnp.bfloat16
f32 = jnp.float32
i32 = jnp.int32

N_DP = 32
CAP = 6
PAD = 8
SLOTS = 192
CH = 512
D = 1280
UNITS = 320
LANES = 384
WIDE = 2 * LANES
BLOCK = 40
ZX = ("zh", "zl")

VMEM = pl.BlockSpec(memory_space=pltpu.VMEM)
SMEM = pl.BlockSpec(memory_space=pltpu.SMEM)
HBM = pl.BlockSpec(memory_space=pltpu.HBM)


def dot(a, b, dims=((1,), (0,))):
    return lax.dot_general(a, b, (dims, ((), ())), preferred_element_type=f32)


def iota(shape, dim):
    return lax.broadcasted_iota(i32, shape, dim)


def normalize(values):
    mean_value = jnp.mean(values, axis=-1, keepdims=True)
    centered = values - mean_value
    variance = jnp.mean(centered * centered, axis=-1, keepdims=True)
    return centered * lax.rsqrt(variance + epsilon)


def call(kernel, out_shape, args, flops, bytes_accessed, scratch=(), vmem=12 << 20, smem=0, hbm=0, name=None):
    args = list(args)
    for k in range(len(args) - hbm, len(args)):
        args[k] = pltpu.with_memory_space_constraint(args[k], pltpu.HBM)
    return pl.pallas_call(
        kernel,
        out_shape=out_shape,
        in_specs=[SMEM] * smem + [VMEM] * (len(args) - smem - hbm) + [HBM] * hbm,
        out_specs=jax.tree.map(lambda _: VMEM, out_shape),
        scratch_shapes=list(scratch),
        compiler_params=pltpu.CompilerParams(vmem_limit_bytes=vmem),
        cost_estimate=pl.CostEstimate(
            flops=flops, bytes_accessed=bytes_accessed, transcendentals=0
        ),
        name=name,
    )(*args)


def pack_kernel(pair, packed):
    up = pair[0].astype(f32)
    down = pair[1].astype(f32)
    blank = jnp.zeros((BLOCK, LANES - UNITS), f32)
    up = jnp.concatenate([up, blank], axis=1)
    down = jnp.concatenate([down, blank], axis=1)
    packed[...] = pack_pair(up, down).astype(bf16)


def pack_pair(up, down):
    turned = pltpu.roll(down, 64, 1)
    lane = iota((BLOCK, 128), 1)
    middle = jnp.where(lane < 64, up[:, 256:], turned[:, :128])
    return jnp.concatenate([up[:, :256], middle, turned[:, 128:]], axis=1)


def unpack_pair(packed):
    used = iota((BLOCK, LANES), 1) < UNITS
    up = jnp.where(used, packed[:, :LANES], 0.0)
    down = pltpu.roll(packed[:, 256:], LANES - 64, 1)
    return up, jnp.where(used, down, 0.0)


def route_kernel(owner, live, rows, outgoing):
    count = rows.shape[0]
    diagonal = iota((count, count), 0) == iota((count, count), 1)
    target = jnp.sum(jnp.where(diagonal, owner[...], 0), axis=1, keepdims=True)
    onehot = (target == iota((count, 128), 1)).astype(f32)
    earlier = (iota((count, count), 1) < iota((count, count), 0)).astype(bf16)
    before = dot(earlier, onehot.astype(bf16))
    position = jnp.sum(before * onehot, axis=1, keepdims=True).astype(i32)
    state = 1.0 + jnp.sum(
        jnp.where(diagonal, live[...].astype(f32), 0.0), axis=1, keepdims=True
    )
    slot = iota((count, N_DP * PAD), 1)
    placement = (target * PAD + position == slot).astype(bf16)
    flag_row = (target * PAD + CAP == slot).astype(bf16)
    flag_value = jnp.where(position == iota((count, 128), 1), state, 0.0).astype(bf16)
    first = ((0,), (0,))
    outgoing[...] = dot(placement, rows[...], first).astype(bf16)
    flags = dot(flag_row, flag_value, first)
    outgoing[:, :128] = (outgoing[:, :128].astype(f32) + flags).astype(bf16)


def front_kernel(place, incoming, *refs):
    pieces, (block, flags_out, conv, arrival) = refs[:4], refs[4:]
    y, zl = place[0], place[1]
    copies = []
    for step in range(4):
        for other in range(2):
            k = step * 2 + other
            start = lax.rem(y - step + 4, 4) * 256 + lax.rem(zl + other, 2) * 128
            rows = pl.ds(pl.multiple_of(start, 128), 128)
            source = pieces[step].at[pl.ds(other * 128, 128), :]
            copies.append(pltpu.make_async_copy(source, conv.at[rows, :], arrival.at[k]))
            copies[-1].start()
    for copy in copies:
        copy.wait()
    raw = incoming[...]
    conv_out = dot(raw, conv[...])
    active = 0.5 * conv_out * (1.0 + lax.erf(conv_out * 0.7071067811865476))
    features = normalize(active).astype(bf16)
    slot = iota((SLOTS, N_DP * PAD), 0)
    row = iota((SLOTS, N_DP * PAD), 1)
    owner, rank = slot // CAP, slot % CAP
    compact = (row == owner * PAD + rank).astype(bf16)
    block[:SLOTS, :] = dot(compact, features).astype(bf16)
    flag_rows = dot((row == owner * PAD + CAP).astype(bf16), raw[:, :128])
    lane = iota((SLOTS, 128), 1)
    flags = jnp.sum(
        jnp.where(lane == iota((SLOTS, 128), 0) % CAP, flag_rows, 0.0), axis=1, keepdims=True
    )
    flags_out[...] = flags
    wide = iota((SLOTS, CH), 1) == iota((SLOTS, CH), 0)
    as_row = jnp.sum(jnp.where(wide, flags, 0.0), axis=0, keepdims=True)
    block[SLOTS:, :] = jnp.broadcast_to(as_row, (16, CH)).astype(bf16)


def weights_kernel(place, *refs):
    pieces, (up, down, wide_up, wide_down) = refs[:8], refs[8:]
    zh, x, c, zl = place[0], place[1], place[2], place[3]
    for core in range(2):
        for step in range(4):
            piece = pieces[core * 4 + step]
            base = lax.rem(x - step + 4, 4) * 80 + lax.rem(c + core, 2) * 40

            def one(k, carry):
                row = lax.rem(zh - k // 2 + 4, 4) * 320 + base
                half = lax.rem(zl + k, 2)
                rows = pl.ds(pl.multiple_of(row, 8), BLOCK)
                a, b = unpack_pair(piece[k].astype(f32))
                wide_up[half, rows, :] = a
                wide_down[half, rows, :] = b
                return carry

            lax.fori_loop(0, 8, one, 0, unroll=True)
    for half in range(2):
        up[:, half * LANES : (half + 1) * LANES] = wide_up[half].astype(bf16)
        down[:, half * LANES : (half + 1) * LANES] = wide_down[half].astype(bf16)


def ffn_kernel(place, cot_in, up_in, down_in, *refs):
    blocks, protos, refs = refs[:4], refs[4:8], refs[8:]
    own, away1, away2, away3, kept, sent, refs = *refs[:6], refs[6:]
    proj, feats, live, normed, hidden, grad_pre, grad_out, wide_up, wide_down, *refs = refs
    cot, up, down, arrival = refs
    y, zl, c = place[0], place[1], place[2]
    copies = []

    def fetch(source, target):
        copy = pltpu.make_async_copy(source, target, arrival.at[len(copies)])
        copy.start()
        copies.append(copy)

    for step in range(4):
        fetch(blocks[step], feats.at[step])
    for step in range(4):
        for other in range(2):
            start = lax.rem(y - step + 4, 4) * 128 + lax.rem(zl + other, 2) * 64
            rows = pl.ds(pl.multiple_of(start, 64), 64)
            fetch(protos[step].at[pl.ds(other * 64, 64), :], proj.at[rows, :])
    fetch(up_in, up)
    fetch(down_in, down)
    fetch(cot_in, cot)
    for copy in copies[:13]:
        copy.wait()
    for step in range(4):
        flags = feats[step, SLOTS : SLOTS + 16, :].astype(f32)[:1, :]
        wide = iota((SLOTS, CH), 1) == iota((SLOTS, CH), 0)
        flags = jnp.sum(jnp.where(wide, flags, 0.0), axis=1, keepdims=True)
        live[step] = (flags == 2.0).astype(f32)

    def forward(step, carry):
        rows = pl.ds(pl.multiple_of(step * SLOTS, SLOTS), SLOTS)
        stream = dot(feats[step, :SLOTS, :], proj[...]).astype(bf16).astype(f32)
        normed[rows, :] = normalize(stream).astype(bf16)
        pre = dot(normed[rows, :], up[...])
        cumulative = 0.5 * (1.0 + lax.erf(pre * 0.7071067811865476))
        density = jnp.exp(-0.5 * pre * pre) * 0.3989422804014327
        hidden[rows, :] = (pre * cumulative).astype(bf16)
        slope = cumulative + pre * density

        @pl.when(step == 0)
        def _():
            copies[13].wait()
            copies[14].wait()

        partial = dot(hidden[rows, :], down[...], ((1,), (1,)))

        @pl.when(step == 0)
        def _():
            own[...] = partial + stream

        for k, away in enumerate((away1, away2, away3)):

            @pl.when(step == k + 1)
            def _():
                away[...] = partial.astype(bf16)

        there = lax.rem(y - step + 4, 4) * SLOTS
        masked = cot[pl.ds(pl.multiple_of(there, SLOTS), SLOTS), :].astype(f32) * live[step]
        grad_out[rows, :] = masked.astype(bf16)
        grad_hidden = dot(grad_out[rows, :], down[...])
        grad_pre[rows, :] = (grad_hidden * slope).astype(bf16)
        return carry

    lax.fori_loop(0, 4, forward, 0)

    def backward(part, carry):
        columns = pl.ds(pl.multiple_of(part * 640, 640), 640)
        first = ((0,), (0,))
        wide_up[...] = dot(normed[:, columns], grad_pre[...], first)
        wide_down[...] = dot(grad_out[:, columns], hidden[...], first)

        def place_block(k, carry):
            zh, x = k // 4, lax.rem(k, 4)
            for other, out in enumerate((kept, sent)):
                row = zh * 320 + x * 80 + lax.rem(c + other, 2) * BLOCK
                rows = pl.ds(pl.multiple_of(row, 8), BLOCK)
                for half in range(2):
                    lanes = slice(half * LANES, (half + 1) * LANES)
                    block = pack_pair(wide_up[rows, lanes], wide_down[rows, lanes])
                    out[x, (part * 2 + zh) * 2 + half] = block.astype(bf16)
            return carry

        lax.fori_loop(0, 8, place_block, 0)
        return carry

    lax.fori_loop(0, 2, backward, 0)


def core_sum_kernel(place, kept, arrived, *outs):
    x = place[0]
    for step, out in enumerate(outs):
        there = lax.rem(x + step, 4)
        out[...] = (kept[there].astype(f32) + arrived[there].astype(f32)).astype(bf16)


def x_sum_kernel(*refs):
    total = refs[0][...].astype(f32)
    for ref in refs[1:-1]:
        total = total + ref[...].astype(f32)
    refs[-1][...] = total.astype(bf16)


def last_kernel(arrived, out):
    total = arrived[0].astype(f32)
    for k in range(1, 8):
        total = total + arrived[k].astype(f32)
    up, down = unpack_pair(total)
    out[0] = up[:, :UNITS]
    out[1] = down[:, :UNITS]


def ring(values, axis, size, step):
    return lax.ppermute(values, axis, [(k, (k + step) % size) for k in range(size)])


def around(values, axis, size):
    return [values] + [ring(values, axis, size, step) for step in range(1, size)]


def per_device(waveform_rows, conv_weight, proj_weight, ffn_pair, owner, frame_live, cotangent):
    dp = ("zh", "x", "c")
    zh, x, c, y, zl = (lax.axis_index(name).astype(i32) for name in ("zh", "x", "c", "y", "zl"))
    cot_all = lax.all_gather(cotangent, "y", axis=0, tiled=True)

    packed = call(
        pack_kernel,
        jax.ShapeDtypeStruct((BLOCK, 2 * UNITS), bf16),
        [jnp.transpose(ffn_pair, (1, 2, 0))],
        1 << 16, 1 << 17, name="pack",
    )
    both = jnp.stack([packed, ring(packed, "zl", 2, 1)])
    conv_pair = jnp.concatenate([conv_weight, ring(conv_weight, "zl", 2, 1)], axis=0)
    proj_pair = jnp.concatenate([proj_weight, ring(proj_weight, "zl", 2, 1)], axis=0)
    along_z = jnp.concatenate(around(both, "zh", 4), axis=0)

    outgoing = call(
        route_kernel,
        jax.ShapeDtypeStruct((N_DP * PAD, 1024), bf16),
        [owner.reshape(1, -1), frame_live.reshape(1, -1), waveform_rows],
        2 * 256 * 128 * 1152, 1 << 20, name="route",
    )
    outgoing, along_z, conv_pair, proj_pair = lax.optimization_barrier(
        (outgoing, along_z, conv_pair, proj_pair)
    )
    along_x = around(along_z, "x", 4)
    conv_pieces = around(conv_pair, "y", 4)
    proj_pair, _ = lax.optimization_barrier((proj_pair, conv_pieces[1]))
    proj_pieces = around(proj_pair, "y", 4)
    incoming = lax.all_to_all(
        outgoing.reshape(N_DP, PAD, 1024), dp, split_axis=0, concat_axis=0, tiled=True
    ).reshape(N_DP * PAD, 1024)
    incoming, *proj_pieces = lax.optimization_barrier((incoming, *proj_pieces))

    block, flags = call(
        front_kernel,
        (
            jax.ShapeDtypeStruct((SLOTS + 16, CH), bf16),
            jax.ShapeDtypeStruct((SLOTS, 1), f32),
        ),
        [jnp.stack([y, zl]), incoming, *conv_pieces],
        2 * 256 * 1024 * 512, 2 << 20,
        scratch=[pltpu.VMEM((1024, CH), bf16), pltpu.SemaphoreType.DMA((8,))],
        smem=1, hbm=4, name="front",
    )
    blocks = around(block, "y", 4)
    _, _, _, *along_x = lax.optimization_barrier((*blocks[1:], *along_x))
    pieces = along_x + [ring(piece, "c", 2, 1) for piece in along_x]

    up, down = call(
        weights_kernel,
        (jax.ShapeDtypeStruct((D, WIDE), bf16),) * 2,
        [jnp.stack([zh, x, c, zl]), *pieces],
        1 << 22, 8 << 20,
        scratch=[pltpu.VMEM((2, D, LANES), f32)] * 2, vmem=24 << 20, smem=1, name="weights",
    )
    rows = 4 * SLOTS
    piece = jax.ShapeDtypeStruct((SLOTS, D), bf16)
    terms = jax.ShapeDtypeStruct((4, 8, BLOCK, 2 * UNITS), bf16)
    own, away1, away2, away3, kept, sent = call(
        ffn_kernel,
        (jax.ShapeDtypeStruct((SLOTS, D), f32), piece, piece, piece, terms, terms),
        [jnp.stack([y, zl, c]), cot_all, up, down, *blocks, *proj_pieces],
        2 * rows * D * (CH + 5 * WIDE), 16 << 20,
        scratch=[
            pltpu.VMEM((CH, D), bf16),
            pltpu.VMEM((4, SLOTS + 16, CH), bf16),
            pltpu.VMEM((4, SLOTS, 1), f32),
            pltpu.VMEM((rows, D), bf16),
            pltpu.VMEM((rows, WIDE), bf16),
            pltpu.VMEM((rows, WIDE), bf16),
            pltpu.VMEM((rows, D), bf16),
            pltpu.VMEM((640, WIDE), f32),
            pltpu.VMEM((640, WIDE), f32),
            pltpu.VMEM((rows, D), bf16),
            pltpu.VMEM((D, WIDE), bf16),
            pltpu.VMEM((D, WIDE), bf16),
            pltpu.SemaphoreType.DMA((15,)),
        ],
        vmem=36 << 20, smem=1, hbm=11, name="ffn",
    )
    tile = jax.ShapeDtypeStruct((8, BLOCK, 2 * UNITS), bf16)
    parts = call(
        core_sum_kernel,
        (tile,) * 4,
        [x[None], kept, ring(sent, "c", 2, 1)],
        1 << 20, 5 << 20, smem=1, name="core_sum",
    )
    total = call(
        x_sum_kernel,
        tile,
        [parts[0]] + [ring(parts[step], "x", 4, step) for step in range(1, 4)],
        1 << 20, 2 << 20, name="x_sum",
    )
    away1, away2, away3, _ = lax.optimization_barrier((away1, away2, away3, parts[0]))
    for step, away in ((1, away1), (2, away2), (3, away3)):
        own = own + ring(away, "y", 4, 4 - step).astype(f32)
    encoded = (own * (flags > 0).astype(f32)).astype(bf16)
    total = lax.all_to_all(total, ZX, split_axis=0, concat_axis=0, tiled=True)
    grad_pair = call(
        last_kernel,
        jax.ShapeDtypeStruct((2, BLOCK, UNITS), f32),
        [total],
        1 << 18, 1 << 19, name="last",
    )
    return (encoded, jnp.transpose(grad_pair, (2, 0, 1)))


def solution(mesh):
    names = ("zh", "x", "c", "y", "zl")
    fine = Mesh(np.asarray(mesh.devices).reshape(4, 4, 2, 4, 2), names)
    dp = ("zh", "x", "c")
    fsdp = ("y", "zl")
    everyone = dp + fsdp
    return jax.shard_map(
        per_device,
        mesh=fine,
        in_specs=(
            P(everyone, None),
            P(fsdp, None),
            P(fsdp, None),
            P(fsdp, None, dp),
            P(everyone, None),
            P(everyone),
            P(everyone, None),
        ),
        out_specs=(P(everyone, None), P(fsdp, None, dp)),
        check_vma=False,
    )
```

```python
import functools

import jax
import jax.numpy as jnp
import numpy as np
from jax import lax
from jax.experimental import pallas as pl
from jax.experimental.pallas import tpu as pltpu
from jax.sharding import Mesh
from jax.sharding import PartitionSpec as P

epsilon = 1e-05
bf16 = jnp.bfloat16
f32 = jnp.float32
i32 = jnp.int32

N_DP = 32
CAP = 6
PAD = 8
SLOTS = 192
CH = 512
D = 1280
UNITS = 320
LANES = 384
WIDE = 2 * LANES
BLOCK = 40
ZX = ("zh", "zl")

VMEM = pl.BlockSpec(memory_space=pltpu.VMEM)
SMEM = pl.BlockSpec(memory_space=pltpu.SMEM)
HBM = pl.BlockSpec(memory_space=pltpu.HBM)


def dot(a, b, dims=((1,), (0,))):
    return lax.dot_general(a, b, (dims, ((), ())), preferred_element_type=f32)


def iota(shape, dim):
    return lax.broadcasted_iota(i32, shape, dim)


def normalize(values):
    mean_value = jnp.mean(values, axis=-1, keepdims=True)
    centered = values - mean_value
    variance = jnp.mean(centered * centered, axis=-1, keepdims=True)
    return centered * lax.rsqrt(variance + epsilon)


def call(kernel, out_shape, args, flops, bytes_accessed, scratch=(), vmem=12 << 20, smem=0, hbm=0, name=None):
    args = list(args)
    for k in range(len(args) - hbm, len(args)):
        args[k] = pltpu.with_memory_space_constraint(args[k], pltpu.HBM)
    return pl.pallas_call(
        kernel,
        out_shape=out_shape,
        in_specs=[SMEM] * smem + [VMEM] * (len(args) - smem - hbm) + [HBM] * hbm,
        out_specs=jax.tree.map(lambda _: VMEM, out_shape),
        scratch_shapes=list(scratch),
        compiler_params=pltpu.CompilerParams(vmem_limit_bytes=vmem),
        cost_estimate=pl.CostEstimate(
            flops=flops, bytes_accessed=bytes_accessed, transcendentals=0
        ),
        name=name,
    )(*args)


def pack_kernel(pair, packed):
    up = pair[0].astype(f32)
    down = pair[1].astype(f32)
    blank = jnp.zeros((BLOCK, LANES - UNITS), f32)
    up = jnp.concatenate([up, blank], axis=1)
    down = jnp.concatenate([down, blank], axis=1)
    packed[...] = pack_pair(up, down).astype(bf16)


def pack_pair(up, down):
    turned = pltpu.roll(down, 64, 1)
    lane = iota((BLOCK, 128), 1)
    middle = jnp.where(lane < 64, up[:, 256:], turned[:, :128])
    return jnp.concatenate([up[:, :256], middle, turned[:, 128:]], axis=1)


def unpack_pair(packed):
    used = iota((BLOCK, LANES), 1) < UNITS
    up = jnp.where(used, packed[:, :LANES], 0.0)
    down = pltpu.roll(packed[:, 256:], LANES - 64, 1)
    return up, jnp.where(used, down, 0.0)


def route_kernel(owner_in, live_in, rows_in, outgoing, owner, live, rows, arrival):
    copies = [
        pltpu.make_async_copy(owner_in, owner, arrival.at[0]),
        pltpu.make_async_copy(live_in, live, arrival.at[1]),
        pltpu.make_async_copy(rows_in, rows, arrival.at[2]),
    ]
    for copy in copies:
        copy.start()
    copies[0].wait()
    copies[1].wait()
    count = rows.shape[0]
    diagonal = iota((count, count), 0) == iota((count, count), 1)
    target = jnp.sum(jnp.where(diagonal, owner[...], 0), axis=1, keepdims=True)
    onehot = (target == iota((count, 128), 1)).astype(f32)
    earlier = (iota((count, count), 1) < iota((count, count), 0)).astype(bf16)
    before = dot(earlier, onehot.astype(bf16))
    position = jnp.sum(before * onehot, axis=1, keepdims=True).astype(i32)
    state = 1.0 + jnp.sum(
        jnp.where(diagonal, live[...].astype(f32), 0.0), axis=1, keepdims=True
    )
    slot = iota((count, N_DP * PAD), 1)
    placement = (target * PAD + position == slot).astype(bf16)
    flag_row = (target * PAD + CAP == slot).astype(bf16)
    flag_value = jnp.where(position == iota((count, 128), 1), state, 0.0).astype(bf16)
    first = ((0,), (0,))
    copies[2].wait()
    outgoing[...] = dot(placement, rows[...], first).astype(bf16)
    flags = dot(flag_row, flag_value, first)
    outgoing[:, :128] = (outgoing[:, :128].astype(f32) + flags).astype(bf16)


def front_kernel(place, incoming, *refs):
    pieces, (block, flags_out, conv, arrival) = refs[:4], refs[4:]
    y, zl = place[0], place[1]
    copies = []
    for step in range(4):
        for other in range(2):
            k = step * 2 + other
            start = lax.rem(y - step + 4, 4) * 256 + lax.rem(zl + other, 2) * 128
            rows = pl.ds(pl.multiple_of(start, 128), 128)
            source = pieces[step].at[pl.ds(other * 128, 128), :]
            copies.append(pltpu.make_async_copy(source, conv.at[rows, :], arrival.at[k]))
            copies[-1].start()
    for copy in copies:
        copy.wait()
    raw = incoming[...]
    conv_out = dot(raw, conv[...])
    active = 0.5 * conv_out * (1.0 + lax.erf(conv_out * 0.7071067811865476))
    features = normalize(active).astype(bf16)
    slot = iota((SLOTS, N_DP * PAD), 0)
    row = iota((SLOTS, N_DP * PAD), 1)
    owner, rank = slot // CAP, slot % CAP
    compact = (row == owner * PAD + rank).astype(bf16)
    block[:SLOTS, :] = dot(compact, features).astype(bf16)
    flag_rows = dot((row == owner * PAD + CAP).astype(bf16), raw[:, :128])
    lane = iota((SLOTS, 128), 1)
    flags = jnp.sum(
        jnp.where(lane == iota((SLOTS, 128), 0) % CAP, flag_rows, 0.0), axis=1, keepdims=True
    )
    flags_out[...] = flags
    wide = iota((SLOTS, CH), 1) == iota((SLOTS, CH), 0)
    as_row = jnp.sum(jnp.where(wide, flags, 0.0), axis=0, keepdims=True)
    block[SLOTS:, :] = jnp.broadcast_to(as_row, (16, CH)).astype(bf16)


def ffn_kernel(place, blocks, own_pair, other_pair, *refs):
    cots, protos, refs = refs[:4], refs[4:8], refs[8:]
    own, away1, away2, away3, kept, sent, refs = *refs[:6], refs[6:]
    proj, feats, live, normed, hidden, grad_pre, grad_out, wide_up, wide_down, *refs = refs
    cot, up, down, raw, arrival = refs
    y, zl, c = place[0], place[1], place[2]
    copies = []

    def fetch(source, target):
        copy = pltpu.make_async_copy(source, target, arrival.at[len(copies)])
        copy.start()
        copies.append(copy)

    for k, pair in enumerate((own_pair, other_pair)):
        for other in range(2):
            fetch(pair.at[:, other], raw.at[lax.rem(c + k, 2), lax.rem(zl + other, 2)])
    for step in range(4):
        fetch(blocks.at[lax.rem(y - step + 4, 4)], feats.at[step])
    for step in range(4):
        for other in range(2):
            start = lax.rem(y - step + 4, 4) * 128 + lax.rem(zl + other, 2) * 64
            rows = pl.ds(pl.multiple_of(start, 64), 64)
            fetch(protos[step].at[pl.ds(other * 64, 64), :], proj.at[rows, :])
    for step in range(4):
        fetch(cots[step], cot.at[pl.ds(step * SLOTS, SLOTS), :])
    for copy in copies[:4]:
        copy.wait()

    def assemble(place, carry):
        rows = pl.ds(pl.multiple_of(place * 2 * BLOCK, 16), 2 * BLOCK)
        for half in range(2):
            lanes = slice(half * LANES, (half + 1) * LANES)
            up0, down0 = unpack_pair(raw[0, half, place].astype(f32))
            up1, down1 = unpack_pair(raw[1, half, place].astype(f32))
            up[rows, lanes] = jnp.concatenate([up0, up1], axis=0).astype(bf16)
            down[rows, lanes] = jnp.concatenate([down0, down1], axis=0).astype(bf16)
        return carry

    lax.fori_loop(0, 16, assemble, 0, unroll=4)
    for copy in copies[4:]:
        copy.wait()
    for step in range(4):
        flags = feats[step, SLOTS : SLOTS + 16, :].astype(f32)[:1, :]
        wide = iota((SLOTS, CH), 1) == iota((SLOTS, CH), 0)
        flags = jnp.sum(jnp.where(wide, flags, 0.0), axis=1, keepdims=True)
        live[step] = (flags == 2.0).astype(f32)

    def forward(step, carry):
        rows = pl.ds(pl.multiple_of(step * SLOTS, SLOTS), SLOTS)
        stream = dot(feats[step, :SLOTS, :], proj[...]).astype(bf16).astype(f32)
        normed[rows, :] = normalize(stream).astype(bf16)
        pre = dot(normed[rows, :], up[...])
        cumulative = 0.5 * (1.0 + lax.erf(pre * 0.7071067811865476))
        density = jnp.exp(-0.5 * pre * pre) * 0.3989422804014327
        hidden[rows, :] = (pre * cumulative).astype(bf16)
        slope = cumulative + pre * density
        partial = dot(hidden[rows, :], down[...], ((1,), (1,)))

        @pl.when(step == 0)
        def _():
            own[...] = partial + stream

        for k, away in enumerate((away1, away2, away3)):

            @pl.when(step == k + 1)
            def _():
                away[...] = partial.astype(bf16)

        masked = cot[rows, :].astype(f32) * live[step]
        grad_out[rows, :] = masked.astype(bf16)
        grad_hidden = dot(grad_out[rows, :], down[...])
        grad_pre[rows, :] = (grad_hidden * slope).astype(bf16)
        return carry

    lax.fori_loop(0, 4, forward, 0)

    def backward(part, carry):
        columns = pl.ds(pl.multiple_of(part * 640, 640), 640)
        first = ((0,), (0,))
        wide_up[...] = dot(normed[:, columns], grad_pre[...], first)
        wide_down[...] = dot(grad_out[:, columns], hidden[...], first)

        def place_block(k, carry):
            zh, x = k // 4, lax.rem(k, 4)
            for other, out in enumerate((kept, sent)):
                row = zh * 320 + x * 80 + lax.rem(c + other, 2) * BLOCK
                rows = pl.ds(pl.multiple_of(row, 8), BLOCK)
                for half in range(2):
                    lanes = slice(half * LANES, (half + 1) * LANES)
                    block = pack_pair(wide_up[rows, lanes], wide_down[rows, lanes])
                    out[x, (part * 2 + zh) * 2 + half] = block.astype(bf16)
            return carry

        lax.fori_loop(0, 8, place_block, 0)
        return carry

    lax.fori_loop(0, 2, backward, 0)


def core_sum_kernel(place, kept, arrived, *outs):
    x = place[0]
    for step, out in enumerate(outs):
        there = lax.rem(x + step, 4)
        out[...] = (kept[there].astype(f32) + arrived[there].astype(f32)).astype(bf16)


def x_sum_kernel(*refs):
    total = refs[0][...].astype(f32)
    for ref in refs[1:-1]:
        total = total + ref[...].astype(f32)
    refs[-1][...] = total.astype(bf16)


def last_kernel(arrived, out):
    total = arrived[0].astype(f32)
    for k in range(1, 8):
        total = total + arrived[k].astype(f32)
    up, down = unpack_pair(total)
    out[0] = up[:, :UNITS]
    out[1] = down[:, :UNITS]


def ring(values, axis, size, step):
    return lax.ppermute(values, axis, [(k, (k + step) % size) for k in range(size)])


def around(values, axis, size):
    return [values] + [ring(values, axis, size, step) for step in range(1, size)]


def per_device(waveform_rows, conv_weight, proj_weight, ffn_pair, owner, frame_live, cotangent):
    dp = ("zh", "x", "c")
    zh, x, c, y, zl = (lax.axis_index(name).astype(i32) for name in ("zh", "x", "c", "y", "zl"))
    packed = call(
        pack_kernel,
        jax.ShapeDtypeStruct((BLOCK, 2 * UNITS), bf16),
        [jnp.transpose(ffn_pair, (1, 2, 0))],
        1 << 16, 1 << 17, name="pack",
    )
    both = jnp.stack([packed, ring(packed, "zl", 2, 1)])
    conv_pair = jnp.concatenate([conv_weight, ring(conv_weight, "zl", 2, 1)], axis=0)
    proj_pair = jnp.concatenate([proj_weight, ring(proj_weight, "zl", 2, 1)], axis=0)
    own_pair = lax.all_gather(both, ("zh", "x"), axis=0)

    outgoing = call(
        route_kernel,
        jax.ShapeDtypeStruct((N_DP * PAD, 1024), bf16),
        [owner.reshape(1, -1), frame_live.reshape(1, -1), waveform_rows],
        2 * 256 * 128 * 1152, 1 << 20,
        scratch=[
            pltpu.VMEM((1, 128), i32),
            pltpu.VMEM((1, 128), i32),
            pltpu.VMEM((128, 1024), bf16),
            pltpu.SemaphoreType.DMA((3,)),
        ],
        hbm=3, name="route",
    )
    cot_pieces = around(cotangent, "y", 4)
    outgoing, both, conv_pair, proj_pair, cot_pieces[1], cot_pieces[3] = (
        lax.optimization_barrier(
            (outgoing, both, conv_pair, proj_pair, cot_pieces[1], cot_pieces[3])
        )
    )
    conv_pieces = around(conv_pair, "y", 4)
    proj_pair, *conv_pieces[1:] = lax.optimization_barrier((proj_pair, *conv_pieces[1:]))
    proj_pieces = around(proj_pair, "y", 4)
    incoming = lax.all_to_all(
        outgoing.reshape(N_DP, PAD, 1024), dp, split_axis=0, concat_axis=0, tiled=True
    ).reshape(N_DP * PAD, 1024)

    block, flags = call(
        front_kernel,
        (
            jax.ShapeDtypeStruct((SLOTS + 16, CH), bf16),
            jax.ShapeDtypeStruct((SLOTS, 1), f32),
        ),
        [jnp.stack([y, zl]), incoming, *conv_pieces],
        2 * 256 * 1024 * 512, 2 << 20,
        scratch=[pltpu.VMEM((1024, CH), bf16), pltpu.SemaphoreType.DMA((8,))],
        smem=1, hbm=4, name="front",
    )
    block, cot_pieces[2], *proj_pieces = lax.optimization_barrier(
        (block, cot_pieces[2], *proj_pieces)
    )
    blocks = lax.all_to_all(
        jnp.broadcast_to(block[None], (4,) + block.shape), "y", split_axis=0, concat_axis=0
    )
    blocks, own_pair = lax.optimization_barrier((blocks, own_pair))
    other_pair = ring(own_pair, "c", 2, 1)

    rows = 4 * SLOTS
    piece = jax.ShapeDtypeStruct((SLOTS, D), bf16)
    terms = jax.ShapeDtypeStruct((4, 8, BLOCK, 2 * UNITS), bf16)
    own, away1, away2, away3, kept, sent = call(
        ffn_kernel,
        (jax.ShapeDtypeStruct((SLOTS, D), f32), piece, piece, piece, terms, terms),
        [jnp.stack([y, zl, c]), blocks, own_pair, other_pair, *cot_pieces, *proj_pieces],
        2 * rows * D * (CH + 5 * WIDE), 16 << 20,
        scratch=[
            pltpu.VMEM((CH, D), bf16),
            pltpu.VMEM((4, SLOTS + 16, CH), bf16),
            pltpu.VMEM((4, SLOTS, 1), f32),
            pltpu.VMEM((rows, D), bf16),
            pltpu.VMEM((rows, WIDE), bf16),
            pltpu.VMEM((rows, WIDE), bf16),
            pltpu.VMEM((rows, D), bf16),
            pltpu.VMEM((640, WIDE), f32),
            pltpu.VMEM((640, WIDE), f32),
            pltpu.VMEM((rows, D), bf16),
            pltpu.VMEM((D, WIDE), bf16),
            pltpu.VMEM((D, WIDE), bf16),
            pltpu.VMEM((2, 2, 16, BLOCK, 2 * UNITS), bf16),
            pltpu.SemaphoreType.DMA((20,)),
        ],
        vmem=36 << 20, smem=1, hbm=11, name="ffn",
    )
    tile = jax.ShapeDtypeStruct((8, BLOCK, 2 * UNITS), bf16)
    parts = call(
        core_sum_kernel,
        (tile,) * 4,
        [x[None], kept, ring(sent, "c", 2, 1)],
        1 << 20, 5 << 20, smem=1, name="core_sum",
    )
    total = call(
        x_sum_kernel,
        tile,
        [parts[0]] + [ring(parts[step], "x", 4, step) for step in range(1, 4)],
        1 << 20, 2 << 20, name="x_sum",
    )
    away1, away2, away3, _ = lax.optimization_barrier((away1, away2, away3, parts[0]))
    for step, away in ((1, away1), (2, away2), (3, away3)):
        own = own + ring(away, "y", 4, 4 - step).astype(f32)
    encoded = (own * (flags > 0).astype(f32)).astype(bf16)
    total = lax.all_to_all(total, ZX, split_axis=0, concat_axis=0, tiled=True)
    grad_pair = call(
        last_kernel,
        jax.ShapeDtypeStruct((2, BLOCK, UNITS), f32),
        [total],
        1 << 18, 1 << 19, name="last",
    )
    return (encoded, jnp.transpose(grad_pair, (2, 0, 1)))


def solution(mesh):
    names = ("zh", "x", "c", "y", "zl")
    fine = Mesh(np.asarray(mesh.devices).reshape(4, 4, 2, 4, 2), names)
    dp = ("zh", "x", "c")
    fsdp = ("y", "zl")
    everyone = dp + fsdp
    return jax.shard_map(
        per_device,
        mesh=fine,
        in_specs=(
            P(everyone, None),
            P(fsdp, None),
            P(fsdp, None),
            P(fsdp, None, dp),
            P(everyone, None),
            P(everyone),
            P(everyone, None),
        ),
        out_specs=(P(everyone, None), P(fsdp, None, dp)),
        check_vma=False,
    )
```

```python
import functools

import jax
import jax.numpy as jnp
import numpy as np
from jax import lax
from jax.experimental import pallas as pl
from jax.experimental.pallas import tpu as pltpu
from jax.sharding import Mesh
from jax.sharding import PartitionSpec as P

epsilon = 1e-05
bf16 = jnp.bfloat16
f32 = jnp.float32
i32 = jnp.int32

N_DP = 32
CAP = 6
PAD = 8
SLOTS = 192
CH = 512
D = 1280
UNITS = 320
LANES = 384
WIDE = 2 * LANES
BLOCK = 40
ZX = ("zh", "zl")

VMEM = pl.BlockSpec(memory_space=pltpu.VMEM)
SMEM = pl.BlockSpec(memory_space=pltpu.SMEM)
HBM = pl.BlockSpec(memory_space=pltpu.HBM)


def dot(a, b, dims=((1,), (0,))):
    return lax.dot_general(a, b, (dims, ((), ())), preferred_element_type=f32)


def iota(shape, dim):
    return lax.broadcasted_iota(i32, shape, dim)


def normalize(values):
    mean_value = jnp.mean(values, axis=-1, keepdims=True)
    centered = values - mean_value
    variance = jnp.mean(centered * centered, axis=-1, keepdims=True)
    return centered * lax.rsqrt(variance + epsilon)


def call(kernel, out_shape, args, flops, bytes_accessed, scratch=(), vmem=12 << 20, smem=0, hbm=0, name=None):
    args = list(args)
    for k in range(len(args) - hbm, len(args)):
        args[k] = pltpu.with_memory_space_constraint(args[k], pltpu.HBM)
    return pl.pallas_call(
        kernel,
        out_shape=out_shape,
        in_specs=[SMEM] * smem + [VMEM] * (len(args) - smem - hbm) + [HBM] * hbm,
        out_specs=jax.tree.map(lambda _: VMEM, out_shape),
        scratch_shapes=list(scratch),
        compiler_params=pltpu.CompilerParams(vmem_limit_bytes=vmem),
        cost_estimate=pl.CostEstimate(
            flops=flops, bytes_accessed=bytes_accessed, transcendentals=0
        ),
        name=name,
    )(*args)


def pack_kernel(place, pair_in, conv_in, proj_in, packed, wire, pair, arrival):
    c = place[0]
    conv_rows = pl.ds(pl.multiple_of(c * 64, 64), 64)
    proj_rows = pl.ds(pl.multiple_of(c * 32, 32), 32)
    low = pl.ds(pl.multiple_of(c * 32, 16), 16)
    high = pl.ds(pl.multiple_of(c * 32 + 16, 16), 16)
    routes = (
        (pair_in, pair),
        (conv_in.at[conv_rows, :], wire.at[pl.ds(0, 64), :]),
        (proj_in.at[proj_rows, pl.ds(0, 512)], wire.at[pl.ds(64, 32), :]),
        (proj_in.at[proj_rows, pl.ds(512, 512)], wire.at[pl.ds(96, 32), :]),
        (proj_in.at[low, pl.ds(1024, 256)], wire.at[pl.ds(128, 16), pl.ds(0, 256)]),
        (proj_in.at[high, pl.ds(1024, 256)], wire.at[pl.ds(128, 16), pl.ds(256, 256)]),
    )
    copies = [
        pltpu.make_async_copy(source, target, arrival.at[k])
        for k, (source, target) in enumerate(routes)
    ]
    for copy in copies:
        copy.start()
    for copy in copies:
        copy.wait()
    up = pair[0].astype(f32)
    down = pair[1].astype(f32)
    blank = jnp.zeros((BLOCK, LANES - UNITS), f32)
    up = jnp.concatenate([up, blank], axis=1)
    down = jnp.concatenate([down, blank], axis=1)
    packed[...] = pack_pair(up, down).astype(bf16)


def pack_pair(up, down):
    turned = pltpu.roll(down, 64, 1)
    lane = iota((BLOCK, 128), 1)
    middle = jnp.where(lane < 64, up[:, 256:], turned[:, :128])
    return jnp.concatenate([up[:, :256], middle, turned[:, 128:]], axis=1)


def unpack_pair(packed):
    used = iota((BLOCK, LANES), 1) < UNITS
    up = jnp.where(used, packed[:, :LANES], 0.0)
    down = pltpu.roll(packed[:, 256:], LANES - 64, 1)
    return up, jnp.where(used, down, 0.0)


def route_kernel(owner_in, live_in, rows_in, outgoing, owner, live, rows, arrival):
    copies = [
        pltpu.make_async_copy(owner_in, owner, arrival.at[0]),
        pltpu.make_async_copy(live_in, live, arrival.at[1]),
        pltpu.make_async_copy(rows_in, rows, arrival.at[2]),
    ]
    for copy in copies:
        copy.start()
    copies[0].wait()
    copies[1].wait()
    count = rows.shape[0]
    diagonal = iota((count, count), 0) == iota((count, count), 1)
    target = jnp.sum(jnp.where(diagonal, owner[...], 0), axis=1, keepdims=True)
    onehot = (target == iota((count, 128), 1)).astype(f32)
    earlier = (iota((count, count), 1) < iota((count, count), 0)).astype(bf16)
    before = dot(earlier, onehot.astype(bf16))
    position = jnp.sum(before * onehot, axis=1, keepdims=True).astype(i32)
    state = 1.0 + jnp.sum(
        jnp.where(diagonal, live[...].astype(f32), 0.0), axis=1, keepdims=True
    )
    slot = iota((count, N_DP * PAD), 1)
    placement = (target * PAD + position == slot).astype(bf16)
    flag_row = (target * PAD + CAP == slot).astype(bf16)
    flag_value = jnp.where(position == iota((count, 128), 1), state, 0.0).astype(bf16)
    first = ((0,), (0,))
    copies[2].wait()
    outgoing[...] = dot(placement, rows[...], first).astype(bf16)
    flags = dot(flag_row, flag_value, first)
    outgoing[:, :128] = (outgoing[:, :128].astype(f32) + flags).astype(bf16)


def wire_places(place, rows_each):
    y, zl, c = place[0], place[1], place[2]
    for step in range(4):
        for k in range(4):
            source = lax.rem(y - step + 4, 4) * 4 + lax.rem(zl + k // 2, 2) * 2
            source = source + lax.rem(c + k % 2, 2)
            yield step, k, pl.multiple_of(source * rows_each, rows_each)


def proj_kernel(place, *refs):
    wires, proj = refs[:4], refs[4]
    for step, k, row in wire_places(place, 32):
        rows = pl.ds(row, 32)
        proj[rows, :512] = wires[k][step, 64:96, :]
        proj[rows, 512:1024] = wires[k][step, 96:128, :]
        proj[pl.ds(row, 16), 1024:] = wires[k][step, 128:144, :256]
        proj[pl.ds(pl.multiple_of(row + 16, 16), 16), 1024:] = wires[k][step, 128:144, 256:]


def front_kernel(place, incoming, *refs):
    wires, (block, flags_out, conv, arrival) = refs[:4], refs[4:]
    copies = []
    for step, k, row in wire_places(place, 64):
        source = wires[k].at[step, pl.ds(0, 64), :]
        target = conv.at[pl.ds(row, 64), :]
        copies.append(pltpu.make_async_copy(source, target, arrival.at[step * 4 + k]))
        copies[-1].start()
    for copy in copies:
        copy.wait()
    raw = incoming[...]
    conv_out = dot(raw, conv[...])
    active = 0.5 * conv_out * (1.0 + lax.erf(conv_out * 0.7071067811865476))
    features = normalize(active).astype(bf16)
    slot = iota((SLOTS, N_DP * PAD), 0)
    row = iota((SLOTS, N_DP * PAD), 1)
    owner, rank = slot // CAP, slot % CAP
    compact = (row == owner * PAD + rank).astype(bf16)
    block[:SLOTS, :] = dot(compact, features).astype(bf16)
    flag_rows = dot((row == owner * PAD + CAP).astype(bf16), raw[:, :128])
    lane = iota((SLOTS, 128), 1)
    flags = jnp.sum(
        jnp.where(lane == iota((SLOTS, 128), 0) % CAP, flag_rows, 0.0), axis=1, keepdims=True
    )
    flags_out[...] = flags
    wide = iota((SLOTS, CH), 1) == iota((SLOTS, CH), 0)
    as_row = jnp.sum(jnp.where(wide, flags, 0.0), axis=0, keepdims=True)
    block[SLOTS:, :] = jnp.broadcast_to(as_row, (16, CH)).astype(bf16)


def ffn_kernel(place, blocks, own_pair, other_pair, *refs):
    cots, proj_in, refs = refs[:4], refs[4], refs[5:]
    own, away1, away2, away3, kept, sent, refs = *refs[:6], refs[6:]
    proj, feats, live, normed, hidden, grad_pre, grad_out, wide_up, wide_down, *refs = refs
    cot, up, down, raw, arrival = refs
    y, zl, c, zh = place[0], place[1], place[2], place[3]
    copies = []

    def fetch(source, target):
        copy = pltpu.make_async_copy(source, target, arrival.at[len(copies)])
        copy.start()
        copies.append(copy)

    for k, pair in enumerate((own_pair, other_pair)):
        for step in range(4):
            for other in range(2):
                target = raw.at[
                    lax.rem(c + k, 2), lax.rem(zl + other, 2), lax.rem(zh - step + 4, 4)
                ]
                fetch(pair.at[:, step, other], target)
    for step in range(4):
        fetch(blocks.at[lax.rem(y - step + 4, 4)], feats.at[step])
    fetch(proj_in, proj)
    for step in range(4):
        fetch(cots[step], cot.at[pl.ds(step * SLOTS, SLOTS), :])
    for copy in copies[:16]:
        copy.wait()

    def assemble(spot, carry):
        rows = pl.ds(pl.multiple_of(spot * 2 * BLOCK, 16), 2 * BLOCK)
        high, x = spot // 4, lax.rem(spot, 4)
        for half in range(2):
            lanes = slice(half * LANES, (half + 1) * LANES)
            up0, down0 = unpack_pair(raw[0, half, high, x].astype(f32))
            up1, down1 = unpack_pair(raw[1, half, high, x].astype(f32))
            up[rows, lanes] = jnp.concatenate([up0, up1], axis=0).astype(bf16)
            down[rows, lanes] = jnp.concatenate([down0, down1], axis=0).astype(bf16)
        return carry

    lax.fori_loop(0, 16, assemble, 0, unroll=4)
    for copy in copies[16:]:
        copy.wait()
    for step in range(4):
        flags = feats[step, SLOTS : SLOTS + 16, :].astype(f32)[:1, :]
        wide = iota((SLOTS, CH), 1) == iota((SLOTS, CH), 0)
        flags = jnp.sum(jnp.where(wide, flags, 0.0), axis=1, keepdims=True)
        live[step] = (flags == 2.0).astype(f32)

    def forward(step, carry):
        rows = pl.ds(pl.multiple_of(step * SLOTS, SLOTS), SLOTS)
        stream = dot(feats[step, :SLOTS, :], proj[...]).astype(bf16).astype(f32)
        normed[rows, :] = normalize(stream).astype(bf16)
        pre = dot(normed[rows, :], up[...])
        cumulative = 0.5 * (1.0 + lax.erf(pre * 0.7071067811865476))
        density = jnp.exp(-0.5 * pre * pre) * 0.3989422804014327
        hidden[rows, :] = (pre * cumulative).astype(bf16)
        slope = cumulative + pre * density
        partial = dot(hidden[rows, :], down[...], ((1,), (1,)))

        @pl.when(step == 0)
        def _():
            own[...] = partial + stream

        for k, away in enumerate((away1, away2, away3)):

            @pl.when(step == k + 1)
            def _():
                away[...] = partial.astype(bf16)

        masked = cot[rows, :].astype(f32) * live[step]
        grad_out[rows, :] = masked.astype(bf16)
        grad_hidden = dot(grad_out[rows, :], down[...])
        grad_pre[rows, :] = (grad_hidden * slope).astype(bf16)
        return carry

    lax.fori_loop(0, 4, forward, 0)

    def backward(part, carry):
        columns = pl.ds(pl.multiple_of(part * 640, 640), 640)
        first = ((0,), (0,))
        wide_up[...] = dot(normed[:, columns], grad_pre[...], first)
        wide_down[...] = dot(grad_out[:, columns], hidden[...], first)

        def place_block(k, carry):
            zh, x = k // 4, lax.rem(k, 4)
            for other, out in enumerate((kept, sent)):
                row = zh * 320 + x * 80 + lax.rem(c + other, 2) * BLOCK
                rows = pl.ds(pl.multiple_of(row, 8), BLOCK)
                for half in range(2):
                    lanes = slice(half * LANES, (half + 1) * LANES)
                    block = pack_pair(wide_up[rows, lanes], wide_down[rows, lanes])
                    out[x, (part * 2 + zh) * 2 + half] = block.astype(bf16)
            return carry

        lax.fori_loop(0, 8, place_block, 0)
        return carry

    lax.fori_loop(0, 2, backward, 0)


def core_sum_kernel(place, kept, arrived, *outs):
    x = place[0]
    for step, out in enumerate(outs):
        there = lax.rem(x + step, 4)
        out[...] = (kept[there].astype(f32) + arrived[there].astype(f32)).astype(bf16)


def x_sum_kernel(*refs):
    total = refs[0][...].astype(f32)
    for ref in refs[1:-1]:
        total = total + ref[...].astype(f32)
    refs[-1][...] = total.astype(bf16)


def last_kernel(arrived, out):
    total = arrived[0].astype(f32)
    for k in range(1, 8):
        total = total + arrived[k].astype(f32)
    up, down = unpack_pair(total)
    out[0] = up[:, :UNITS]
    out[1] = down[:, :UNITS]


def ring(values, axis, size, step):
    return lax.ppermute(values, axis, [(k, (k + step) % size) for k in range(size)])


def around(values, axis, size):
    return [values] + [ring(values, axis, size, step) for step in range(1, size)]


def per_device(waveform_rows, conv_weight, proj_weight, ffn_pair, owner, frame_live, cotangent):
    dp = ("zh", "x", "c")
    zh, x, c, y, zl = (lax.axis_index(name).astype(i32) for name in ("zh", "x", "c", "y", "zl"))
    packed, wire = call(
        pack_kernel,
        (
            jax.ShapeDtypeStruct((BLOCK, 2 * UNITS), bf16),
            jax.ShapeDtypeStruct((144, CH), bf16),
        ),
        [c[None], jnp.transpose(ffn_pair, (1, 2, 0)), conv_weight, proj_weight],
        1 << 16, 1 << 19,
        scratch=[pltpu.VMEM((2, BLOCK, UNITS), bf16), pltpu.SemaphoreType.DMA((6,))],
        smem=1, hbm=3, name="pack",
    )
    both = jnp.stack([packed, ring(packed, "zl", 2, 1)])
    wire_y = jnp.stack(around(wire, "y", 4))
    along_z = jnp.stack(around(both, "zh", 4))
    own_pair = lax.all_gather(along_z, "x", axis=0)
    cot_pieces = around(cotangent, "y", 4)

    outgoing = call(
        route_kernel,
        jax.ShapeDtypeStruct((N_DP * PAD, 1024), bf16),
        [owner.reshape(1, -1), frame_live.reshape(1, -1), waveform_rows],
        2 * 256 * 128 * 1152, 1 << 20,
        scratch=[
            pltpu.VMEM((1, 128), i32),
            pltpu.VMEM((1, 128), i32),
            pltpu.VMEM((128, 1024), bf16),
            pltpu.SemaphoreType.DMA((3,)),
        ],
        hbm=3, name="route",
    )
    outgoing, wire_y, along_z = lax.optimization_barrier((outgoing, wire_y, along_z))
    wire_z = ring(wire_y, "zl", 2, 1)
    wires = [wire_y, ring(wire_y, "c", 2, 1), wire_z, ring(wire_z, "c", 2, 1)]
    incoming = lax.all_to_all(
        outgoing.reshape(N_DP, PAD, 1024), dp, split_axis=0, concat_axis=0, tiled=True
    ).reshape(N_DP * PAD, 1024)
    incoming, cot_pieces[1], cot_pieces[3] = lax.optimization_barrier(
        (incoming, cot_pieces[1], cot_pieces[3])
    )
    where = jnp.stack([y, zl, c])
    proj_full = call(
        proj_kernel,
        jax.ShapeDtypeStruct((CH, D), bf16),
        [where, *wires],
        1 << 18, 3 << 20, smem=1, name="proj",
    )

    block, flags = call(
        front_kernel,
        (
            jax.ShapeDtypeStruct((SLOTS + 16, CH), bf16),
            jax.ShapeDtypeStruct((SLOTS, 1), f32),
        ),
        [where, incoming, *wires],
        2 * 256 * 1024 * 512, 2 << 20,
        scratch=[pltpu.VMEM((1024, CH), bf16), pltpu.SemaphoreType.DMA((16,))],
        smem=1, hbm=4, name="front",
    )
    block, proj_full = lax.optimization_barrier((block, proj_full))
    blocks = lax.all_to_all(
        jnp.broadcast_to(block[None], (4,) + block.shape), "y", split_axis=0, concat_axis=0
    )
    blocks, own_pair, cot_pieces[2] = lax.optimization_barrier(
        (blocks, own_pair, cot_pieces[2])
    )
    other_pair = ring(own_pair, "c", 2, 1)

    rows = 4 * SLOTS
    piece = jax.ShapeDtypeStruct((SLOTS, D), bf16)
    terms = jax.ShapeDtypeStruct((4, 8, BLOCK, 2 * UNITS), bf16)
    own, away1, away2, away3, kept, sent = call(
        ffn_kernel,
        (jax.ShapeDtypeStruct((SLOTS, D), f32), piece, piece, piece, terms, terms),
        [jnp.stack([y, zl, c, zh]), blocks, own_pair, other_pair, *cot_pieces, proj_full],
        2 * rows * D * (CH + 5 * WIDE), 16 << 20,
        scratch=[
            pltpu.VMEM((CH, D), bf16),
            pltpu.VMEM((4, SLOTS + 16, CH), bf16),
            pltpu.VMEM((4, SLOTS, 1), f32),
            pltpu.VMEM((rows, D), bf16),
            pltpu.VMEM((rows, WIDE), bf16),
            pltpu.VMEM((rows, WIDE), bf16),
            pltpu.VMEM((rows, D), bf16),
            pltpu.VMEM((640, WIDE), f32),
            pltpu.VMEM((640, WIDE), f32),
            pltpu.VMEM((rows, D), bf16),
            pltpu.VMEM((D, WIDE), bf16),
            pltpu.VMEM((D, WIDE), bf16),
            pltpu.VMEM((2, 2, 4, 4, BLOCK, 2 * UNITS), bf16),
            pltpu.SemaphoreType.DMA((25,)),
        ],
        vmem=40 << 20, smem=1, hbm=8, name="ffn",
    )
    tile = jax.ShapeDtypeStruct((8, BLOCK, 2 * UNITS), bf16)
    parts = call(
        core_sum_kernel,
        (tile,) * 4,
        [x[None], kept, ring(sent, "c", 2, 1)],
        1 << 20, 5 << 20, smem=1, name="core_sum",
    )
    total = call(
        x_sum_kernel,
        tile,
        [parts[0]] + [ring(parts[step], "x", 4, step) for step in range(1, 4)],
        1 << 20, 2 << 20, name="x_sum",
    )
    away1, away2, away3, _ = lax.optimization_barrier((away1, away2, away3, parts[0]))
    for step, away in ((1, away1), (2, away2), (3, away3)):
        own = own + ring(away, "y", 4, 4 - step).astype(f32)
    encoded = (own * (flags > 0).astype(f32)).astype(bf16)
    total = lax.all_to_all(total, ZX, split_axis=0, concat_axis=0, tiled=True)
    grad_pair = call(
        last_kernel,
        jax.ShapeDtypeStruct((2, BLOCK, UNITS), f32),
        [total],
        1 << 18, 1 << 19, name="last",
    )
    return (encoded, jnp.transpose(grad_pair, (2, 0, 1)))


def solution(mesh):
    names = ("zh", "x", "c", "y", "zl")
    fine = Mesh(np.asarray(mesh.devices).reshape(4, 4, 2, 4, 2), names)
    dp = ("zh", "x", "c")
    fsdp = ("y", "zl")
    everyone = dp + fsdp
    return jax.shard_map(
        per_device,
        mesh=fine,
        in_specs=(
            P(everyone, None),
            P(fsdp, None),
            P(fsdp, None),
            P(fsdp, None, dp),
            P(everyone, None),
            P(everyone),
            P(everyone, None),
        ),
        out_specs=(P(everyone, None), P(fsdp, None, dp)),
        check_vma=False,
    )
```

```python
import functools

import jax
import jax.numpy as jnp
import numpy as np
from jax import lax
from jax.experimental import pallas as pl
from jax.experimental.pallas import tpu as pltpu
from jax.sharding import Mesh
from jax.sharding import PartitionSpec as P

epsilon = 1e-05
bf16 = jnp.bfloat16
f32 = jnp.float32
i32 = jnp.int32

N_DP = 32
CAP = 6
PAD = 8
SLOTS = 192
CH = 512
D = 1280
UNITS = 320
LANES = 384
WIDE = 2 * LANES
BLOCK = 40
ZX = ("zh", "zl")

VMEM = pl.BlockSpec(memory_space=pltpu.VMEM)
SMEM = pl.BlockSpec(memory_space=pltpu.SMEM)
HBM = pl.BlockSpec(memory_space=pltpu.HBM)


def dot(a, b, dims=((1,), (0,))):
    return lax.dot_general(a, b, (dims, ((), ())), preferred_element_type=f32)


def iota(shape, dim):
    return lax.broadcasted_iota(i32, shape, dim)


def normalize(values):
    mean_value = jnp.mean(values, axis=-1, keepdims=True)
    centered = values - mean_value
    variance = jnp.mean(centered * centered, axis=-1, keepdims=True)
    return centered * lax.rsqrt(variance + epsilon)


def call(kernel, out_shape, args, flops, bytes_accessed, scratch=(), vmem=12 << 20, smem=0, hbm=0, name=None):
    args = list(args)
    for k in range(len(args) - hbm, len(args)):
        args[k] = pltpu.with_memory_space_constraint(args[k], pltpu.HBM)
    return pl.pallas_call(
        kernel,
        out_shape=out_shape,
        in_specs=[SMEM] * smem + [VMEM] * (len(args) - smem - hbm) + [HBM] * hbm,
        out_specs=jax.tree.map(lambda _: VMEM, out_shape),
        scratch_shapes=list(scratch),
        compiler_params=pltpu.CompilerParams(vmem_limit_bytes=vmem),
        cost_estimate=pl.CostEstimate(
            flops=flops, bytes_accessed=bytes_accessed, transcendentals=0
        ),
        name=name,
    )(*args)


def pack_kernel(place, pair_in, conv_in, proj_in, packed, wire, pair, arrival):
    c = place[0]
    conv_rows = pl.ds(pl.multiple_of(c * 64, 64), 64)
    proj_rows = pl.ds(pl.multiple_of(c * 32, 32), 32)
    low = pl.ds(pl.multiple_of(c * 32, 16), 16)
    high = pl.ds(pl.multiple_of(c * 32 + 16, 16), 16)
    routes = (
        (pair_in, pair),
        (conv_in.at[conv_rows, :], wire.at[pl.ds(0, 64), :]),
        (proj_in.at[proj_rows, pl.ds(0, 512)], wire.at[pl.ds(64, 32), :]),
        (proj_in.at[proj_rows, pl.ds(512, 512)], wire.at[pl.ds(96, 32), :]),
        (proj_in.at[low, pl.ds(1024, 256)], wire.at[pl.ds(128, 16), pl.ds(0, 256)]),
        (proj_in.at[high, pl.ds(1024, 256)], wire.at[pl.ds(128, 16), pl.ds(256, 256)]),
    )
    copies = [
        pltpu.make_async_copy(source, target, arrival.at[k])
        for k, (source, target) in enumerate(routes)
    ]
    for copy in copies:
        copy.start()
    for copy in copies:
        copy.wait()
    up = pair[0].astype(f32)
    down = pair[1].astype(f32)
    blank = jnp.zeros((BLOCK, LANES - UNITS), f32)
    up = jnp.concatenate([up, blank], axis=1)
    down = jnp.concatenate([down, blank], axis=1)
    packed[...] = pack_pair(up, down).astype(bf16)


def pack_pair(up, down):
    turned = pltpu.roll(down, 64, 1)
    lane = iota((BLOCK, 128), 1)
    middle = jnp.where(lane < 64, up[:, 256:], turned[:, :128])
    return jnp.concatenate([up[:, :256], middle, turned[:, 128:]], axis=1)


def unpack_pair(packed):
    used = iota((BLOCK, LANES), 1) < UNITS
    up = jnp.where(used, packed[:, :LANES], 0.0)
    down = pltpu.roll(packed[:, 256:], LANES - 64, 1)
    return up, jnp.where(used, down, 0.0)


def route_kernel(owner_in, live_in, rows_in, outgoing, owner, live, rows, arrival):
    copies = [
        pltpu.make_async_copy(owner_in, owner, arrival.at[0]),
        pltpu.make_async_copy(live_in, live, arrival.at[1]),
        pltpu.make_async_copy(rows_in, rows, arrival.at[2]),
    ]
    for copy in copies:
        copy.start()
    copies[0].wait()
    copies[1].wait()
    count = rows.shape[0]
    diagonal = iota((count, count), 0) == iota((count, count), 1)
    target = jnp.sum(jnp.where(diagonal, owner[...], 0), axis=1, keepdims=True)
    onehot = (target == iota((count, 128), 1)).astype(f32)
    earlier = (iota((count, count), 1) < iota((count, count), 0)).astype(bf16)
    before = dot(earlier, onehot.astype(bf16))
    position = jnp.sum(before * onehot, axis=1, keepdims=True).astype(i32)
    state = 1.0 + jnp.sum(
        jnp.where(diagonal, live[...].astype(f32), 0.0), axis=1, keepdims=True
    )
    slot = iota((count, N_DP * PAD), 1)
    placement = (target * PAD + position == slot).astype(bf16)
    flag_row = (target * PAD + CAP == slot).astype(bf16)
    flag_value = jnp.where(position == iota((count, 128), 1), state, 0.0).astype(bf16)
    first = ((0,), (0,))
    copies[2].wait()
    outgoing[...] = dot(placement, rows[...], first).astype(bf16)
    flags = dot(flag_row, flag_value, first)
    outgoing[:, :128] = (outgoing[:, :128].astype(f32) + flags).astype(bf16)


def wire_places(place, rows_each):
    y, zl, c = place[0], place[1], place[2]
    for step in range(4):
        for k in range(4):
            source = lax.rem(y - step + 4, 4) * 4 + lax.rem(zl + k // 2, 2) * 2
            source = source + lax.rem(c + k % 2, 2)
            yield step, k // 2, k % 2, pl.multiple_of(source * rows_each, rows_each)


def proj_kernel(place, own, other, proj):
    for step, half, core, row in wire_places(place, 32):
        wire = (own, other)[core]
        rows = pl.ds(row, 32)
        proj[rows, :512] = wire[step, half, 64:96, :]
        proj[rows, 512:1024] = wire[step, half, 96:128, :]
        proj[pl.ds(row, 16), 1024:] = wire[step, half, 128:144, :256]
        proj[pl.ds(pl.multiple_of(row + 16, 16), 16), 1024:] = wire[step, half, 128:144, 256:]


def front_kernel(place, incoming, *refs):
    wires, (block, flags_out, conv, arrival) = refs[:2], refs[2:]
    copies = []
    for step, half, core, row in wire_places(place, 64):
        source = wires[core].at[step, half, pl.ds(0, 64), :]
        target = conv.at[pl.ds(row, 64), :]
        copies.append(pltpu.make_async_copy(source, target, arrival.at[len(copies)]))
        copies[-1].start()
    for copy in copies:
        copy.wait()
    raw = incoming[...]
    conv_out = dot(raw, conv[...])
    active = 0.5 * conv_out * (1.0 + lax.erf(conv_out * 0.7071067811865476))
    features = normalize(active).astype(bf16)
    slot = iota((SLOTS, N_DP * PAD), 0)
    row = iota((SLOTS, N_DP * PAD), 1)
    owner, rank = slot // CAP, slot % CAP
    compact = (row == owner * PAD + rank).astype(bf16)
    block[:SLOTS, :] = dot(compact, features).astype(bf16)
    flag_rows = dot((row == owner * PAD + CAP).astype(bf16), raw[:, :128])
    lane = iota((SLOTS, 128), 1)
    flags = jnp.sum(
        jnp.where(lane == iota((SLOTS, 128), 0) % CAP, flag_rows, 0.0), axis=1, keepdims=True
    )
    flags_out[...] = flags
    wide = iota((SLOTS, CH), 1) == iota((SLOTS, CH), 0)
    as_row = jnp.sum(jnp.where(wide, flags, 0.0), axis=0, keepdims=True)
    block[SLOTS:, :] = jnp.broadcast_to(as_row, (16, CH)).astype(bf16)


def ffn_kernel(place, blocks, own_pair, other_pair, *refs):
    cots, proj_in, refs = refs[0], refs[1], refs[2:]
    own, away1, away2, away3, kept, sent, refs = *refs[:6], refs[6:]
    proj, feats, live, normed, hidden, grad_pre, grad_out, wide_up, wide_down, *refs = refs
    cot, up, down, raw, arrival = refs
    y, zl, c, zh, x = place[0], place[1], place[2], place[3], place[4]
    copies = []

    def fetch(source, target):
        copy = pltpu.make_async_copy(source, target, arrival.at[len(copies)])
        copy.start()
        copies.append(copy)

    for k, pair in enumerate((own_pair, other_pair)):
        for step in range(4):
            for other in range(2):
                target = raw.at[
                    lax.rem(c + k, 2), lax.rem(zl + other, 2), lax.rem(zh - step + 4, 4)
                ]
                fetch(pair.at[:, step, other], target)
    for step in range(4):
        fetch(blocks.at[lax.rem(y - step + 4, 4)], feats.at[step])
    fetch(proj_in, proj)
    for step in range(4):
        fetch(cots.at[lax.rem(y - step + 4, 4)], cot.at[pl.ds(step * SLOTS, SLOTS), :])
    for copy in copies[:16]:
        copy.wait()

    def assemble(spot, carry):
        high, behind = spot // 4, lax.rem(spot, 4)
        row = high * 320 + lax.rem(x - behind + 4, 4) * 2 * BLOCK
        rows = pl.ds(pl.multiple_of(row, 16), 2 * BLOCK)
        for half in range(2):
            lanes = slice(half * LANES, (half + 1) * LANES)
            up0, down0 = unpack_pair(raw[0, half, high, behind].astype(f32))
            up1, down1 = unpack_pair(raw[1, half, high, behind].astype(f32))
            up[rows, lanes] = jnp.concatenate([up0, up1], axis=0).astype(bf16)
            down[rows, lanes] = jnp.concatenate([down0, down1], axis=0).astype(bf16)
        return carry

    lax.fori_loop(0, 16, assemble, 0, unroll=4)
    for copy in copies[16:]:
        copy.wait()
    for step in range(4):
        flags = feats[step, SLOTS : SLOTS + 16, :].astype(f32)[:1, :]
        wide = iota((SLOTS, CH), 1) == iota((SLOTS, CH), 0)
        flags = jnp.sum(jnp.where(wide, flags, 0.0), axis=1, keepdims=True)
        live[step] = (flags == 2.0).astype(f32)

    def forward(step, carry):
        rows = pl.ds(pl.multiple_of(step * SLOTS, SLOTS), SLOTS)
        stream = dot(feats[step, :SLOTS, :], proj[...]).astype(bf16).astype(f32)
        normed[rows, :] = normalize(stream).astype(bf16)
        pre = dot(normed[rows, :], up[...])
        cumulative = 0.5 * (1.0 + lax.erf(pre * 0.7071067811865476))
        density = jnp.exp(-0.5 * pre * pre) * 0.3989422804014327
        hidden[rows, :] = (pre * cumulative).astype(bf16)
        slope = cumulative + pre * density
        partial = dot(hidden[rows, :], down[...], ((1,), (1,)))

        @pl.when(step == 0)
        def _():
            own[...] = partial + stream

        for k, away in enumerate((away1, away2, away3)):

            @pl.when(step == k + 1)
            def _():
                away[...] = partial.astype(bf16)

        masked = cot[rows, :].astype(f32) * live[step]
        grad_out[rows, :] = masked.astype(bf16)
        grad_hidden = dot(grad_out[rows, :], down[...])
        grad_pre[rows, :] = (grad_hidden * slope).astype(bf16)
        return carry

    lax.fori_loop(0, 4, forward, 0)

    def backward(part, carry):
        columns = pl.ds(pl.multiple_of(part * 640, 640), 640)
        first = ((0,), (0,))
        wide_up[...] = dot(normed[:, columns], grad_pre[...], first)
        wide_down[...] = dot(grad_out[:, columns], hidden[...], first)

        def place_block(k, carry):
            zh, x = k // 4, lax.rem(k, 4)
            for other, out in enumerate((kept, sent)):
                row = zh * 320 + x * 80 + lax.rem(c + other, 2) * BLOCK
                rows = pl.ds(pl.multiple_of(row, 8), BLOCK)
                for half in range(2):
                    lanes = slice(half * LANES, (half + 1) * LANES)
                    block = pack_pair(wide_up[rows, lanes], wide_down[rows, lanes])
                    out[x, (part * 2 + zh) * 2 + half] = block.astype(bf16)
            return carry

        lax.fori_loop(0, 8, place_block, 0)
        return carry

    lax.fori_loop(0, 2, backward, 0)


def core_sum_kernel(place, kept, arrived, *outs):
    x = place[0]
    for step, out in enumerate(outs):
        there = lax.rem(x + step, 4)
        out[...] = (kept[there].astype(f32) + arrived[there].astype(f32)).astype(bf16)


def x_sum_kernel(*refs):
    total = refs[0][...].astype(f32)
    for ref in refs[1:-1]:
        total = total + ref[...].astype(f32)
    refs[-1][...] = total.astype(bf16)


def last_kernel(arrived, out):
    total = arrived[0].astype(f32)
    for k in range(1, 8):
        total = total + arrived[k].astype(f32)
    up, down = unpack_pair(total)
    out[0] = up[:, :UNITS]
    out[1] = down[:, :UNITS]


def ring(values, axis, size, step):
    return lax.ppermute(values, axis, [(k, (k + step) % size) for k in range(size)])


def around(values, axis, size):
    return [values] + [ring(values, axis, size, step) for step in range(1, size)]


def per_device(waveform_rows, conv_weight, proj_weight, ffn_pair, owner, frame_live, cotangent):
    dp = ("zh", "x", "c")
    zh, x, c, y, zl = (lax.axis_index(name).astype(i32) for name in ("zh", "x", "c", "y", "zl"))
    packed, wire = call(
        pack_kernel,
        (
            jax.ShapeDtypeStruct((BLOCK, 2 * UNITS), bf16),
            jax.ShapeDtypeStruct((144, CH), bf16),
        ),
        [c[None], jnp.transpose(ffn_pair, (1, 2, 0)), conv_weight, proj_weight],
        1 << 16, 1 << 19,
        scratch=[pltpu.VMEM((2, BLOCK, UNITS), bf16), pltpu.SemaphoreType.DMA((6,))],
        smem=1, hbm=3, name="pack",
    )
    cot_all = lax.all_gather(cotangent, "y", axis=0)
    both = jnp.stack([packed, ring(packed, "zl", 2, 1)])
    wire_pair = jnp.stack([wire, ring(wire, "zl", 2, 1)])

    outgoing = call(
        route_kernel,
        jax.ShapeDtypeStruct((N_DP * PAD, 1024), bf16),
        [owner.reshape(1, -1), frame_live.reshape(1, -1), waveform_rows],
        2 * 256 * 128 * 1152, 1 << 20,
        scratch=[
            pltpu.VMEM((1, 128), i32),
            pltpu.VMEM((1, 128), i32),
            pltpu.VMEM((128, 1024), bf16),
            pltpu.SemaphoreType.DMA((3,)),
        ],
        hbm=3, name="route",
    )
    along_z = jnp.stack(around(both, "zh", 4))
    outgoing, along_z, wire_pair = lax.optimization_barrier((outgoing, along_z, wire_pair))
    wire_own = jnp.stack(around(wire_pair, "y", 4))
    wires = [wire_own, ring(wire_own, "c", 2, 1)]
    along_x = around(along_z, "x", 4)
    incoming = lax.all_to_all(
        outgoing.reshape(N_DP, PAD, 1024), dp, split_axis=0, concat_axis=0, tiled=True
    ).reshape(N_DP * PAD, 1024)
    incoming, *along_x = lax.optimization_barrier((incoming, *along_x))
    where = jnp.stack([y, zl, c])
    proj_full = call(
        proj_kernel,
        jax.ShapeDtypeStruct((CH, D), bf16),
        [where, *wires],
        1 << 18, 3 << 20, smem=1, name="proj",
    )

    block, flags = call(
        front_kernel,
        (
            jax.ShapeDtypeStruct((SLOTS + 16, CH), bf16),
            jax.ShapeDtypeStruct((SLOTS, 1), f32),
        ),
        [where, incoming, *wires],
        2 * 256 * 1024 * 512, 2 << 20,
        scratch=[pltpu.VMEM((1024, CH), bf16), pltpu.SemaphoreType.DMA((16,))],
        smem=1, hbm=2, name="front",
    )
    block, proj_full = lax.optimization_barrier((block, proj_full))
    blocks = lax.all_to_all(
        jnp.broadcast_to(block[None], (4,) + block.shape), "y", split_axis=0, concat_axis=0
    )
    own_pair = jnp.stack(along_x)
    other_pair = ring(own_pair, "c", 2, 1)

    rows = 4 * SLOTS
    piece = jax.ShapeDtypeStruct((SLOTS, D), bf16)
    terms = jax.ShapeDtypeStruct((4, 8, BLOCK, 2 * UNITS), bf16)
    own, away1, away2, away3, kept, sent = call(
        ffn_kernel,
        (jax.ShapeDtypeStruct((SLOTS, D), f32), piece, piece, piece, terms, terms),
        [jnp.stack([y, zl, c, zh, x]), blocks, own_pair, other_pair, cot_all, proj_full],
        2 * rows * D * (CH + 5 * WIDE), 16 << 20,
        scratch=[
            pltpu.VMEM((CH, D), bf16),
            pltpu.VMEM((4, SLOTS + 16, CH), bf16),
            pltpu.VMEM((4, SLOTS, 1), f32),
            pltpu.VMEM((rows, D), bf16),
            pltpu.VMEM((rows, WIDE), bf16),
            pltpu.VMEM((rows, WIDE), bf16),
            pltpu.VMEM((rows, D), bf16),
            pltpu.VMEM((640, WIDE), f32),
            pltpu.VMEM((640, WIDE), f32),
            pltpu.VMEM((rows, D), bf16),
            pltpu.VMEM((D, WIDE), bf16),
            pltpu.VMEM((D, WIDE), bf16),
            pltpu.VMEM((2, 2, 4, 4, BLOCK, 2 * UNITS), bf16),
            pltpu.SemaphoreType.DMA((25,)),
        ],
        vmem=40 << 20, smem=1, hbm=5, name="ffn",
    )
    tile = jax.ShapeDtypeStruct((8, BLOCK, 2 * UNITS), bf16)
    parts = call(
        core_sum_kernel,
        (tile,) * 4,
        [x[None], kept, ring(sent, "c", 2, 1)],
        1 << 20, 5 << 20, smem=1, name="core_sum",
    )
    total = call(
        x_sum_kernel,
        tile,
        [parts[0]] + [ring(parts[step], "x", 4, step) for step in range(1, 4)],
        1 << 20, 2 << 20, name="x_sum",
    )
    away1, away2, away3, _ = lax.optimization_barrier((away1, away2, away3, parts[0]))
    for step, away in ((1, away1), (2, away2), (3, away3)):
        own = own + ring(away, "y", 4, 4 - step).astype(f32)
    encoded = (own * (flags > 0).astype(f32)).astype(bf16)
    total = lax.all_to_all(total, ZX, split_axis=0, concat_axis=0, tiled=True)
    grad_pair = call(
        last_kernel,
        jax.ShapeDtypeStruct((2, BLOCK, UNITS), f32),
        [total],
        1 << 18, 1 << 19, name="last",
    )
    return (encoded, jnp.transpose(grad_pair, (2, 0, 1)))


def solution(mesh):
    names = ("zh", "x", "c", "y", "zl")
    fine = Mesh(np.asarray(mesh.devices).reshape(4, 4, 2, 4, 2), names)
    dp = ("zh", "x", "c")
    fsdp = ("y", "zl")
    everyone = dp + fsdp
    return jax.shard_map(
        per_device,
        mesh=fine,
        in_specs=(
            P(everyone, None),
            P(fsdp, None),
            P(fsdp, None),
            P(fsdp, None, dp),
            P(everyone, None),
            P(everyone),
            P(everyone, None),
        ),
        out_specs=(P(everyone, None), P(fsdp, None, dp)),
        check_vma=False,
    )
```

```python
import functools

import jax
import jax.numpy as jnp
import numpy as np
from jax import lax
from jax.experimental import pallas as pl
from jax.experimental.pallas import tpu as pltpu
from jax.sharding import Mesh
from jax.sharding import PartitionSpec as P

epsilon = 1e-05
bf16 = jnp.bfloat16
f32 = jnp.float32
i32 = jnp.int32

N_DP = 32
CAP = 6
PAD = 8
SLOTS = 192
CH = 512
D = 1280
UNITS = 320
LANES = 384
WIDE = 2 * LANES
BLOCK = 40
ZX = ("zh", "zl")

VMEM = pl.BlockSpec(memory_space=pltpu.VMEM)
SMEM = pl.BlockSpec(memory_space=pltpu.SMEM)
HBM = pl.BlockSpec(memory_space=pltpu.HBM)
ANY = pl.BlockSpec(memory_space=pl.ANY)


def dot(a, b, dims=((1,), (0,))):
    return lax.dot_general(a, b, (dims, ((), ())), preferred_element_type=f32)


def iota(shape, dim):
    return lax.broadcasted_iota(i32, shape, dim)


def normalize(values):
    mean_value = jnp.mean(values, axis=-1, keepdims=True)
    centered = values - mean_value
    variance = jnp.mean(centered * centered, axis=-1, keepdims=True)
    return centered * lax.rsqrt(variance + epsilon)


def call(kernel, out_shape, args, flops, bytes_accessed, scratch=(), vmem=12 << 20, smem=0, hbm=0, free=0, name=None):
    args = list(args)
    for k in range(len(args) - hbm, len(args)):
        args[k] = pltpu.with_memory_space_constraint(args[k], pltpu.HBM)
    return pl.pallas_call(
        kernel,
        out_shape=out_shape,
        in_specs=[SMEM] * smem + [VMEM] * (len(args) - smem - free - hbm) + [ANY] * free + [HBM] * hbm,
        out_specs=jax.tree.map(lambda _: VMEM, out_shape),
        scratch_shapes=list(scratch),
        compiler_params=pltpu.CompilerParams(vmem_limit_bytes=vmem),
        cost_estimate=pl.CostEstimate(
            flops=flops, bytes_accessed=bytes_accessed, transcendentals=0
        ),
        name=name,
    )(*args)


def pack_kernel(place, pair_in, conv_in, proj_in, packed, wire, pair, arrival):
    c = place[0]
    conv_rows = pl.ds(pl.multiple_of(c * 64, 64), 64)
    proj_rows = pl.ds(pl.multiple_of(c * 32, 32), 32)
    low = pl.ds(pl.multiple_of(c * 32, 16), 16)
    high = pl.ds(pl.multiple_of(c * 32 + 16, 16), 16)
    routes = (
        (pair_in, pair),
        (conv_in.at[conv_rows, :], wire.at[pl.ds(0, 64), :]),
        (proj_in.at[proj_rows, pl.ds(0, 512)], wire.at[pl.ds(64, 32), :]),
        (proj_in.at[proj_rows, pl.ds(512, 512)], wire.at[pl.ds(96, 32), :]),
        (proj_in.at[low, pl.ds(1024, 256)], wire.at[pl.ds(128, 16), pl.ds(0, 256)]),
        (proj_in.at[high, pl.ds(1024, 256)], wire.at[pl.ds(128, 16), pl.ds(256, 256)]),
    )
    copies = [
        pltpu.make_async_copy(source, target, arrival.at[k])
        for k, (source, target) in enumerate(routes)
    ]
    for copy in copies:
        copy.start()
    for copy in copies:
        copy.wait()
    up = pair[0].astype(f32)
    down = pair[1].astype(f32)
    blank = jnp.zeros((BLOCK, LANES - UNITS), f32)
    up = jnp.concatenate([up, blank], axis=1)
    down = jnp.concatenate([down, blank], axis=1)
    packed[...] = pack_pair(up, down).astype(bf16)


def pack_pair(up, down):
    turned = pltpu.roll(down, 64, 1)
    lane = iota((BLOCK, 128), 1)
    middle = jnp.where(lane < 64, up[:, 256:], turned[:, :128])
    return jnp.concatenate([up[:, :256], middle, turned[:, 128:]], axis=1)


def unpack_pair(packed):
    used = iota((BLOCK, LANES), 1) < UNITS
    up = jnp.where(used, packed[:, :LANES], 0.0)
    down = pltpu.roll(packed[:, 256:], LANES - 64, 1)
    return up, jnp.where(used, down, 0.0)


def route_kernel(owner_in, live_in, rows_in, outgoing, owner, live, rows, arrival):
    copies = [
        pltpu.make_async_copy(owner_in, owner, arrival.at[0]),
        pltpu.make_async_copy(live_in, live, arrival.at[1]),
        pltpu.make_async_copy(rows_in, rows, arrival.at[2]),
    ]
    for copy in copies:
        copy.start()
    copies[0].wait()
    copies[1].wait()
    count = rows.shape[0]
    diagonal = iota((count, count), 0) == iota((count, count), 1)
    target = jnp.sum(jnp.where(diagonal, owner[...], 0), axis=1, keepdims=True)
    onehot = (target == iota((count, 128), 1)).astype(f32)
    earlier = (iota((count, count), 1) < iota((count, count), 0)).astype(bf16)
    before = dot(earlier, onehot.astype(bf16))
    position = jnp.sum(before * onehot, axis=1, keepdims=True).astype(i32)
    state = 1.0 + jnp.sum(
        jnp.where(diagonal, live[...].astype(f32), 0.0), axis=1, keepdims=True
    )
    slot = iota((count, N_DP * PAD), 1)
    placement = (target * PAD + position == slot).astype(bf16)
    flag_row = (target * PAD + CAP == slot).astype(bf16)
    flag_value = jnp.where(position == iota((count, 128), 1), state, 0.0).astype(bf16)
    first = ((0,), (0,))
    copies[2].wait()
    outgoing[...] = dot(placement, rows[...], first).astype(bf16)
    flags = dot(flag_row, flag_value, first)
    outgoing[:, :128] = (outgoing[:, :128].astype(f32) + flags).astype(bf16)


def wire_places(place, rows_each):
    y, zl, c = place[0], place[1], place[2]
    for step in range(4):
        for k in range(4):
            source = lax.rem(y - step + 4, 4) * 4 + lax.rem(zl + k // 2, 2) * 2
            source = source + lax.rem(c + k % 2, 2)
            yield step, k // 2, k % 2, pl.multiple_of(source * rows_each, rows_each)


def proj_kernel(place, own, other, proj):
    for step, half, core, row in wire_places(place, 32):
        wire = (own, other)[core]
        rows = pl.ds(row, 32)
        proj[rows, :512] = wire[step, half, 64:96, :]
        proj[rows, 512:1024] = wire[step, half, 96:128, :]
        proj[pl.ds(row, 16), 1024:] = wire[step, half, 128:144, :256]
        proj[pl.ds(pl.multiple_of(row + 16, 16), 16), 1024:] = wire[step, half, 128:144, 256:]


def front_kernel(place, incoming, *refs):
    wires, (block, flags_out, conv, arrival) = refs[:2], refs[2:]
    copies = []
    for step, half, core, row in wire_places(place, 64):
        source = wires[core].at[step, half, pl.ds(0, 64), :]
        target = conv.at[pl.ds(row, 64), :]
        copies.append(pltpu.make_async_copy(source, target, arrival.at[len(copies)]))
        copies[-1].start()
    for copy in copies:
        copy.wait()
    raw = incoming[...]
    conv_out = dot(raw, conv[...])
    active = 0.5 * conv_out * (1.0 + lax.erf(conv_out * 0.7071067811865476))
    features = normalize(active).astype(bf16)
    slot = iota((SLOTS, N_DP * PAD), 0)
    row = iota((SLOTS, N_DP * PAD), 1)
    owner, rank = slot // CAP, slot % CAP
    compact = (row == owner * PAD + rank).astype(bf16)
    compacted = dot(compact, features).astype(bf16)
    for copy in range(4):
        block[copy, :SLOTS, :] = compacted
    flag_rows = dot((row == owner * PAD + CAP).astype(bf16), raw[:, :128])
    lane = iota((SLOTS, 128), 1)
    flags = jnp.sum(
        jnp.where(lane == iota((SLOTS, 128), 0) % CAP, flag_rows, 0.0), axis=1, keepdims=True
    )
    flags_out[...] = flags
    wide = iota((SLOTS, CH), 1) == iota((SLOTS, CH), 0)
    as_row = jnp.sum(jnp.where(wide, flags, 0.0), axis=0, keepdims=True)
    for copy in range(4):
        block[copy, SLOTS:, :] = jnp.broadcast_to(as_row, (16, CH)).astype(bf16)


def ffn_kernel(place, blocks, *refs):
    pieces, cots, proj_in, refs = refs[:8], refs[8], refs[9], refs[10:]
    own, away1, away2, away3, kept, sent, refs = *refs[:6], refs[6:]
    proj, feats, live, normed, hidden, grad_pre, grad_out, wide_up, wide_down, *refs = refs
    cot, up, down, raw, arrival = refs
    y, zl, c, zh, x = place[0], place[1], place[2], place[3], place[4]
    copies = []

    def fetch(source, target):
        copy = pltpu.make_async_copy(source, target, arrival.at[len(copies)])
        copy.start()
        copies.append(copy)

    for k, piece in enumerate(pieces):
        fetch(piece, raw.at[k // 4, k % 4])
    for step in range(4):
        fetch(blocks.at[lax.rem(y - step + 4, 4)], feats.at[step])
    fetch(proj_in, proj)
    for step in range(4):
        fetch(cots.at[lax.rem(y - step + 4, 4)], cot.at[pl.ds(step * SLOTS, SLOTS), :])
    for copy in copies[:8]:
        copy.wait()

    def assemble(spot, carry):
        above, behind = spot // 4, lax.rem(spot, 4)
        row = lax.rem(zh - above + 4, 4) * 320 + lax.rem(x - behind + 4, 4) * 2 * BLOCK
        rows = pl.ds(pl.multiple_of(row, 16), 2 * BLOCK)
        for half in range(2):
            lanes = slice(half * LANES, (half + 1) * LANES)
            other = lax.rem(zl + half, 2)
            up0, down0 = unpack_pair(raw[c, behind, above, other].astype(f32))
            up1, down1 = unpack_pair(raw[1 - c, behind, above, other].astype(f32))
            up[rows, lanes] = jnp.concatenate([up0, up1], axis=0).astype(bf16)
            down[rows, lanes] = jnp.concatenate([down0, down1], axis=0).astype(bf16)
        return carry

    lax.fori_loop(0, 16, assemble, 0, unroll=4)
    for copy in copies[8:]:
        copy.wait()
    for step in range(4):
        flags = feats[step, SLOTS : SLOTS + 16, :].astype(f32)[:1, :]
        wide = iota((SLOTS, CH), 1) == iota((SLOTS, CH), 0)
        flags = jnp.sum(jnp.where(wide, flags, 0.0), axis=1, keepdims=True)
        live[step] = (flags == 2.0).astype(f32)

    def forward(step, carry):
        rows = pl.ds(pl.multiple_of(step * SLOTS, SLOTS), SLOTS)
        stream = dot(feats[step, :SLOTS, :], proj[...]).astype(bf16).astype(f32)
        normed[rows, :] = normalize(stream).astype(bf16)
        pre = dot(normed[rows, :], up[...])
        cumulative = 0.5 * (1.0 + lax.erf(pre * 0.7071067811865476))
        density = jnp.exp(-0.5 * pre * pre) * 0.3989422804014327
        hidden[rows, :] = (pre * cumulative).astype(bf16)
        slope = cumulative + pre * density
        partial = dot(hidden[rows, :], down[...], ((1,), (1,)))

        @pl.when(step == 0)
        def _():
            own[...] = partial + stream

        for k, away in enumerate((away1, away2, away3)):

            @pl.when(step == k + 1)
            def _():
                away[...] = partial.astype(bf16)

        masked = cot[rows, :].astype(f32) * live[step]
        grad_out[rows, :] = masked.astype(bf16)
        grad_hidden = dot(grad_out[rows, :], down[...])
        grad_pre[rows, :] = (grad_hidden * slope).astype(bf16)
        return carry

    lax.fori_loop(0, 4, forward, 0)

    def backward(part, carry):
        columns = pl.ds(pl.multiple_of(part * 640, 640), 640)
        first = ((0,), (0,))
        wide_up[...] = dot(normed[:, columns], grad_pre[...], first)
        wide_down[...] = dot(grad_out[:, columns], hidden[...], first)

        def place_block(k, carry):
            zh, x = k // 4, lax.rem(k, 4)
            for other, out in enumerate((kept, sent)):
                row = zh * 320 + x * 80 + lax.rem(c + other, 2) * BLOCK
                rows = pl.ds(pl.multiple_of(row, 8), BLOCK)
                for half in range(2):
                    lanes = slice(half * LANES, (half + 1) * LANES)
                    block = pack_pair(wide_up[rows, lanes], wide_down[rows, lanes])
                    out[x, (part * 2 + zh) * 2 + half] = block.astype(bf16)
            return carry

        lax.fori_loop(0, 8, place_block, 0)
        return carry

    lax.fori_loop(0, 2, backward, 0)


def core_sum_kernel(place, kept, arrived, *outs):
    x = place[0]
    for step, out in enumerate(outs):
        there = lax.rem(x + step, 4)
        out[...] = (kept[there].astype(f32) + arrived[there].astype(f32)).astype(bf16)


def x_sum_kernel(*refs):
    total = refs[0][...].astype(f32)
    for ref in refs[1:-1]:
        total = total + ref[...].astype(f32)
    refs[-1][...] = total.astype(bf16)


def last_kernel(arrived, out):
    total = arrived[0].astype(f32)
    for k in range(1, 8):
        total = total + arrived[k].astype(f32)
    up, down = unpack_pair(total)
    out[0] = up[:, :UNITS]
    out[1] = down[:, :UNITS]


def ring(values, axis, size, step):
    return lax.ppermute(values, axis, [(k, (k + step) % size) for k in range(size)])


def around(values, axis, size):
    return [values] + [ring(values, axis, size, step) for step in range(1, size)]


def per_device(waveform_rows, conv_weight, proj_weight, ffn_pair, owner, frame_live, cotangent):
    dp = ("zh", "x", "c")
    zh, x, c, y, zl = (lax.axis_index(name).astype(i32) for name in ("zh", "x", "c", "y", "zl"))
    packed, wire = call(
        pack_kernel,
        (
            jax.ShapeDtypeStruct((BLOCK, 2 * UNITS), bf16),
            jax.ShapeDtypeStruct((144, CH), bf16),
        ),
        [c[None], jnp.transpose(ffn_pair, (1, 2, 0)), conv_weight, proj_weight],
        1 << 16, 1 << 19,
        scratch=[pltpu.VMEM((2, BLOCK, UNITS), bf16), pltpu.SemaphoreType.DMA((6,))],
        smem=1, hbm=3, name="pack",
    )
    cot_all = lax.all_gather(cotangent, "y", axis=0)
    both = jnp.stack([packed, ring(packed, "zl", 2, 1)])
    wire_pair = jnp.stack([wire, ring(wire, "zl", 2, 1)])

    outgoing = call(
        route_kernel,
        jax.ShapeDtypeStruct((N_DP * PAD, 1024), bf16),
        [owner.reshape(1, -1), frame_live.reshape(1, -1), waveform_rows],
        2 * 256 * 128 * 1152, 1 << 20,
        scratch=[
            pltpu.VMEM((1, 128), i32),
            pltpu.VMEM((1, 128), i32),
            pltpu.VMEM((128, 1024), bf16),
            pltpu.SemaphoreType.DMA((3,)),
        ],
        hbm=3, name="route",
    )
    along_z = jnp.stack(around(both, "zh", 4))
    wire_own = jnp.stack(around(wire_pair, "y", 4))
    outgoing, along_z, wire_own = lax.optimization_barrier((outgoing, along_z, wire_own))
    wires = [wire_own, ring(wire_own, "c", 2, 1)]
    along_x = around(along_z, "x", 4)
    incoming = lax.all_to_all(
        outgoing.reshape(N_DP, PAD, 1024), dp, split_axis=0, concat_axis=0, tiled=True
    ).reshape(N_DP * PAD, 1024)
    where = jnp.stack([y, zl, c])
    proj_full = call(
        proj_kernel,
        jax.ShapeDtypeStruct((CH, D), bf16),
        [where, *wires],
        1 << 18, 3 << 20, smem=1, name="proj",
    )

    block, flags = call(
        front_kernel,
        (
            jax.ShapeDtypeStruct((4, SLOTS + 16, CH), bf16),
            jax.ShapeDtypeStruct((SLOTS, 1), f32),
        ),
        [where, incoming, *wires],
        2 * 256 * 1024 * 512, 2 << 20,
        scratch=[pltpu.VMEM((1024, CH), bf16), pltpu.SemaphoreType.DMA((16,))],
        smem=1, free=2, name="front",
    )
    block, proj_full, *along_x = lax.optimization_barrier((block, proj_full, *along_x))
    blocks = lax.all_to_all(block, "y", split_axis=0, concat_axis=0, tiled=True)
    pieces = along_x + [ring(piece, "c", 2, 1) for piece in along_x]

    rows = 4 * SLOTS
    piece = jax.ShapeDtypeStruct((SLOTS, D), bf16)
    terms = jax.ShapeDtypeStruct((4, 8, BLOCK, 2 * UNITS), bf16)
    own, away1, away2, away3, kept, sent = call(
        ffn_kernel,
        (jax.ShapeDtypeStruct((SLOTS, D), f32), piece, piece, piece, terms, terms),
        [jnp.stack([y, zl, c, zh, x]), blocks, *pieces, cot_all, proj_full],
        2 * rows * D * (CH + 5 * WIDE), 16 << 20,
        scratch=[
            pltpu.VMEM((CH, D), bf16),
            pltpu.VMEM((4, SLOTS + 16, CH), bf16),
            pltpu.VMEM((4, SLOTS, 1), f32),
            pltpu.VMEM((rows, D), bf16),
            pltpu.VMEM((rows, WIDE), bf16),
            pltpu.VMEM((rows, WIDE), bf16),
            pltpu.VMEM((rows, D), bf16),
            pltpu.VMEM((640, WIDE), f32),
            pltpu.VMEM((640, WIDE), f32),
            pltpu.VMEM((rows, D), bf16),
            pltpu.VMEM((D, WIDE), bf16),
            pltpu.VMEM((D, WIDE), bf16),
            pltpu.VMEM((2, 4, 4, 2, BLOCK, 2 * UNITS), bf16),
            pltpu.SemaphoreType.DMA((17,)),
        ],
        vmem=40 << 20, smem=1, hbm=10, free=1, name="ffn",
    )
    tile = jax.ShapeDtypeStruct((8, BLOCK, 2 * UNITS), bf16)
    parts = call(
        core_sum_kernel,
        (tile,) * 4,
        [x[None], kept, ring(sent, "c", 2, 1)],
        1 << 20, 5 << 20, smem=1, name="core_sum",
    )
    total = call(
        x_sum_kernel,
        tile,
        [parts[0]] + [ring(parts[step], "x", 4, step) for step in range(1, 4)],
        1 << 20, 2 << 20, name="x_sum",
    )
    away1, away2, away3, _ = lax.optimization_barrier((away1, away2, away3, parts[0]))
    for step, away in ((1, away1), (2, away2), (3, away3)):
        own = own + ring(away, "y", 4, 4 - step).astype(f32)
    encoded = (own * (flags > 0).astype(f32)).astype(bf16)
    total = lax.all_to_all(total, ZX, split_axis=0, concat_axis=0, tiled=True)
    grad_pair = call(
        last_kernel,
        jax.ShapeDtypeStruct((2, BLOCK, UNITS), f32),
        [total],
        1 << 18, 1 << 19, name="last",
    )
    return (encoded, jnp.transpose(grad_pair, (2, 0, 1)))


def solution(mesh):
    names = ("zh", "x", "c", "y", "zl")
    fine = Mesh(np.asarray(mesh.devices).reshape(4, 4, 2, 4, 2), names)
    dp = ("zh", "x", "c")
    fsdp = ("y", "zl")
    everyone = dp + fsdp
    return jax.shard_map(
        per_device,
        mesh=fine,
        in_specs=(
            P(everyone, None),
            P(fsdp, None),
            P(fsdp, None),
            P(fsdp, None, dp),
            P(everyone, None),
            P(everyone),
            P(everyone, None),
        ),
        out_specs=(P(everyone, None), P(fsdp, None, dp)),
        check_vma=False,
    )
```

```python
import functools

import jax
import jax.numpy as jnp
import numpy as np
from jax import lax
from jax.experimental import pallas as pl
from jax.experimental.pallas import tpu as pltpu
from jax.sharding import Mesh
from jax.sharding import PartitionSpec as P

epsilon = 1e-05
bf16 = jnp.bfloat16
f32 = jnp.float32
i32 = jnp.int32

N_DP = 32
CAP = 6
PAD = 8
SLOTS = 192
CH = 512
D = 1280
UNITS = 320
LANES = 384
WIDE = 2 * LANES
BLOCK = 40
ZX = ("zh", "zl")

VMEM = pl.BlockSpec(memory_space=pltpu.VMEM)
SMEM = pl.BlockSpec(memory_space=pltpu.SMEM)
HBM = pl.BlockSpec(memory_space=pltpu.HBM)
ANY = pl.BlockSpec(memory_space=pl.ANY)


def dot(a, b, dims=((1,), (0,))):
    return lax.dot_general(a, b, (dims, ((), ())), preferred_element_type=f32)


def iota(shape, dim):
    return lax.broadcasted_iota(i32, shape, dim)


def normalize(values):
    mean_value = jnp.mean(values, axis=-1, keepdims=True)
    centered = values - mean_value
    variance = jnp.mean(centered * centered, axis=-1, keepdims=True)
    return centered * lax.rsqrt(variance + epsilon)


def call(kernel, out_shape, args, flops, bytes_accessed, scratch=(), vmem=12 << 20, smem=0, hbm=0, free=0, name=None):
    args = list(args)
    for k in range(len(args) - hbm, len(args)):
        args[k] = pltpu.with_memory_space_constraint(args[k], pltpu.HBM)
    return pl.pallas_call(
        kernel,
        out_shape=out_shape,
        in_specs=[SMEM] * smem + [VMEM] * (len(args) - smem - free - hbm) + [ANY] * free + [HBM] * hbm,
        out_specs=jax.tree.map(lambda _: VMEM, out_shape),
        scratch_shapes=list(scratch),
        compiler_params=pltpu.CompilerParams(vmem_limit_bytes=vmem),
        cost_estimate=pl.CostEstimate(
            flops=flops, bytes_accessed=bytes_accessed, transcendentals=0
        ),
        name=name,
    )(*args)


def pack_kernel(place, pair_in, conv_in, proj_in, packed, wire, pair, arrival):
    c = place[0]
    conv_rows = pl.ds(pl.multiple_of(c * 64, 64), 64)
    proj_rows = pl.ds(pl.multiple_of(c * 32, 32), 32)
    low = pl.ds(pl.multiple_of(c * 32, 16), 16)
    high = pl.ds(pl.multiple_of(c * 32 + 16, 16), 16)
    routes = (
        (pair_in, pair),
        (conv_in.at[conv_rows, :], wire.at[pl.ds(0, 64), :]),
        (proj_in.at[proj_rows, pl.ds(0, 512)], wire.at[pl.ds(64, 32), :]),
        (proj_in.at[proj_rows, pl.ds(512, 512)], wire.at[pl.ds(96, 32), :]),
        (proj_in.at[low, pl.ds(1024, 256)], wire.at[pl.ds(128, 16), pl.ds(0, 256)]),
        (proj_in.at[high, pl.ds(1024, 256)], wire.at[pl.ds(128, 16), pl.ds(256, 256)]),
    )
    copies = [
        pltpu.make_async_copy(source, target, arrival.at[k])
        for k, (source, target) in enumerate(routes)
    ]
    for copy in copies:
        copy.start()
    for copy in copies:
        copy.wait()
    up = pair[0].astype(f32)
    down = pair[1].astype(f32)
    blank = jnp.zeros((BLOCK, LANES - UNITS), f32)
    up = jnp.concatenate([up, blank], axis=1)
    down = jnp.concatenate([down, blank], axis=1)
    packed[...] = pack_pair(up, down).astype(bf16)


def pack_pair(up, down):
    turned = pltpu.roll(down, 64, 1)
    lane = iota((BLOCK, 128), 1)
    middle = jnp.where(lane < 64, up[:, 256:], turned[:, :128])
    return jnp.concatenate([up[:, :256], middle, turned[:, 128:]], axis=1)


def unpack_pair(packed):
    used = iota((BLOCK, LANES), 1) < UNITS
    up = jnp.where(used, packed[:, :LANES], 0.0)
    down = pltpu.roll(packed[:, 256:], LANES - 64, 1)
    return up, jnp.where(used, down, 0.0)


def route_kernel(owner_in, live_in, rows_in, outgoing, owner, live, rows, arrival):
    copies = [
        pltpu.make_async_copy(owner_in, owner, arrival.at[0]),
        pltpu.make_async_copy(live_in, live, arrival.at[1]),
        pltpu.make_async_copy(rows_in, rows, arrival.at[2]),
    ]
    for copy in copies:
        copy.start()
    copies[0].wait()
    copies[1].wait()
    count = rows.shape[0]
    diagonal = iota((count, count), 0) == iota((count, count), 1)
    target = jnp.sum(jnp.where(diagonal, owner[...], 0), axis=1, keepdims=True)
    onehot = (target == iota((count, 128), 1)).astype(f32)
    earlier = (iota((count, count), 1) < iota((count, count), 0)).astype(bf16)
    before = dot(earlier, onehot.astype(bf16))
    position = jnp.sum(before * onehot, axis=1, keepdims=True).astype(i32)
    state = 1.0 + jnp.sum(
        jnp.where(diagonal, live[...].astype(f32), 0.0), axis=1, keepdims=True
    )
    slot = iota((count, N_DP * PAD), 1)
    placement = (target * PAD + position == slot).astype(bf16)
    flag_row = (target * PAD + CAP == slot).astype(bf16)
    flag_value = jnp.where(position == iota((count, 128), 1), state, 0.0).astype(bf16)
    first = ((0,), (0,))
    copies[2].wait()
    outgoing[...] = dot(placement, rows[...], first).astype(bf16)
    flags = dot(flag_row, flag_value, first)
    outgoing[:, :128] = (outgoing[:, :128].astype(f32) + flags).astype(bf16)


def wire_places(place, rows_each):
    y, zl, c = place[0], place[1], place[2]
    for step in range(4):
        for k in range(4):
            source = lax.rem(y - step + 4, 4) * 4 + lax.rem(zl + k // 2, 2) * 2
            source = source + lax.rem(c + k % 2, 2)
            yield step, k // 2, k % 2, pl.multiple_of(source * rows_each, rows_each)


def proj_kernel(place, own, other, proj):
    for step, half, core, row in wire_places(place, 32):
        wire = (own, other)[core]
        rows = pl.ds(row, 32)
        proj[rows, :512] = wire[step, half, 64:96, :]
        proj[rows, 512:1024] = wire[step, half, 96:128, :]
        proj[pl.ds(row, 16), 1024:] = wire[step, half, 128:144, :256]
        proj[pl.ds(pl.multiple_of(row + 16, 16), 16), 1024:] = wire[step, half, 128:144, 256:]


def front_kernel(place, incoming, *refs):
    wires, (block, flags_out, conv, arrival) = refs[:2], refs[2:]
    copies = []
    for step, half, core, row in wire_places(place, 64):
        source = wires[core].at[step, half, pl.ds(0, 64), :]
        target = conv.at[pl.ds(row, 64), :]
        copies.append(pltpu.make_async_copy(source, target, arrival.at[len(copies)]))
        copies[-1].start()
    for copy in copies:
        copy.wait()
    raw = incoming[...]
    conv_out = dot(raw, conv[...])
    active = 0.5 * conv_out * (1.0 + lax.erf(conv_out * 0.7071067811865476))
    features = normalize(active).astype(bf16)
    slot = iota((SLOTS, N_DP * PAD), 0)
    row = iota((SLOTS, N_DP * PAD), 1)
    owner, rank = slot // CAP, slot % CAP
    compact = (row == owner * PAD + rank).astype(bf16)
    compacted = dot(compact, features).astype(bf16)
    for copy in range(4):
        block[copy, :SLOTS, :] = compacted
    flag_rows = dot((row == owner * PAD + CAP).astype(bf16), raw[:, :128])
    lane = iota((SLOTS, 128), 1)
    flags = jnp.sum(
        jnp.where(lane == iota((SLOTS, 128), 0) % CAP, flag_rows, 0.0), axis=1, keepdims=True
    )
    flags_out[...] = flags
    wide = iota((SLOTS, CH), 1) == iota((SLOTS, CH), 0)
    as_row = jnp.sum(jnp.where(wide, flags, 0.0), axis=0, keepdims=True)
    for copy in range(4):
        block[copy, SLOTS:, :] = jnp.broadcast_to(as_row, (16, CH)).astype(bf16)


def ffn_kernel(place, blocks, *refs):
    pieces, cots, proj_in, refs = refs[:8], refs[8], refs[9], refs[10:]
    own, away1, away2, away3, kept, sent, refs = *refs[:6], refs[6:]
    proj, feats, live, normed, hidden, grad_pre, grad_out, wide_up, wide_down, *refs = refs
    cot, up, down, raw, arrival = refs
    y, zl, c, zh, x = place[0], place[1], place[2], place[3], place[4]
    copies = []

    def fetch(source, target):
        copy = pltpu.make_async_copy(source, target, arrival.at[len(copies)])
        copy.start()
        copies.append(copy)

    for k, piece in enumerate(pieces):
        fetch(piece, raw.at[k // 4, k % 4])
    for step in range(4):
        fetch(blocks.at[lax.rem(y - step + 4, 4)], feats.at[step])
    fetch(proj_in, proj)
    for step in range(4):
        fetch(cots.at[lax.rem(y - step + 4, 4)], cot.at[pl.ds(step * SLOTS, SLOTS), :])
    for copy in copies[:8]:
        copy.wait()

    def assemble(spot, carry):
        above, behind = spot // 4, lax.rem(spot, 4)
        row = lax.rem(zh - above + 4, 4) * 320 + lax.rem(x - behind + 4, 4) * 2 * BLOCK
        rows = pl.ds(pl.multiple_of(row, 16), 2 * BLOCK)
        for half in range(2):
            lanes = slice(half * LANES, (half + 1) * LANES)
            other = lax.rem(zl + half, 2)
            up0, down0 = unpack_pair(raw[c, behind, above, other].astype(f32))
            up1, down1 = unpack_pair(raw[1 - c, behind, above, other].astype(f32))
            up[rows, lanes] = jnp.concatenate([up0, up1], axis=0).astype(bf16)
            down[rows, lanes] = jnp.concatenate([down0, down1], axis=0).astype(bf16)
        return carry

    lax.fori_loop(0, 16, assemble, 0, unroll=4)
    for copy in copies[8:]:
        copy.wait()
    for step in range(4):
        flags = feats[step, SLOTS : SLOTS + 16, :].astype(f32)[:1, :]
        wide = iota((SLOTS, CH), 1) == iota((SLOTS, CH), 0)
        flags = jnp.sum(jnp.where(wide, flags, 0.0), axis=1, keepdims=True)
        live[step] = (flags == 2.0).astype(f32)

    def forward(step, carry):
        rows = pl.ds(pl.multiple_of(step * SLOTS, SLOTS), SLOTS)
        stream = dot(feats[step, :SLOTS, :], proj[...]).astype(bf16).astype(f32)
        normed[rows, :] = normalize(stream).astype(bf16)
        pre = dot(normed[rows, :], up[...])
        cumulative = 0.5 * (1.0 + lax.erf(pre * 0.7071067811865476))
        density = jnp.exp(-0.5 * pre * pre) * 0.3989422804014327
        hidden[rows, :] = (pre * cumulative).astype(bf16)
        slope = cumulative + pre * density
        partial = dot(hidden[rows, :], down[...], ((1,), (1,)))

        @pl.when(step == 0)
        def _():
            own[...] = partial + stream

        for k, away in enumerate((away1, away2, away3)):

            @pl.when(step == k + 1)
            def _():
                away[...] = partial.astype(bf16)

        masked = cot[rows, :].astype(f32) * live[step]
        grad_out[rows, :] = masked.astype(bf16)
        grad_hidden = dot(grad_out[rows, :], down[...])
        grad_pre[rows, :] = (grad_hidden * slope).astype(bf16)
        return carry

    lax.fori_loop(0, 4, forward, 0)

    def backward(part, carry):
        columns = pl.ds(pl.multiple_of(part * 640, 640), 640)
        first = ((0,), (0,))
        wide_up[...] = dot(normed[:, columns], grad_pre[...], first)
        wide_down[...] = dot(grad_out[:, columns], hidden[...], first)

        def place_block(k, carry):
            zh, x = k // 4, lax.rem(k, 4)
            for other, out in enumerate((kept, sent)):
                row = zh * 320 + x * 80 + lax.rem(c + other, 2) * BLOCK
                rows = pl.ds(pl.multiple_of(row, 8), BLOCK)
                for half in range(2):
                    lanes = slice(half * LANES, (half + 1) * LANES)
                    block = pack_pair(wide_up[rows, lanes], wide_down[rows, lanes])
                    out[x, (part * 2 + zh) * 2 + half] = block.astype(bf16)
            return carry

        lax.fori_loop(0, 8, place_block, 0)
        return carry

    lax.fori_loop(0, 2, backward, 0)


def core_sum_kernel(place, kept, arrived, *outs):
    x = place[0]
    for step, out in enumerate(outs):
        there = lax.rem(x + step, 4)
        out[...] = (kept[there].astype(f32) + arrived[there].astype(f32)).astype(bf16)


def x_sum_kernel(*refs):
    total = refs[0][...].astype(f32)
    for ref in refs[1:-1]:
        total = total + ref[...].astype(f32)
    refs[-1][...] = total.astype(bf16)


def last_kernel(arrived, out):
    total = arrived[0].astype(f32)
    for k in range(1, 8):
        total = total + arrived[k].astype(f32)
    up, down = unpack_pair(total)
    out[0] = up[:, :UNITS]
    out[1] = down[:, :UNITS]


def ring(values, axis, size, step):
    return lax.ppermute(values, axis, [(k, (k + step) % size) for k in range(size)])


def around(values, axis, size):
    return [values] + [ring(values, axis, size, step) for step in range(1, size)]


def per_device(waveform_rows, conv_weight, proj_weight, ffn_pair, owner, frame_live, cotangent):
    dp = ("zh", "x", "c")
    zh, x, c, y, zl = (lax.axis_index(name).astype(i32) for name in ("zh", "x", "c", "y", "zl"))
    packed, wire = call(
        pack_kernel,
        (
            jax.ShapeDtypeStruct((BLOCK, 2 * UNITS), bf16),
            jax.ShapeDtypeStruct((144, CH), bf16),
        ),
        [c[None], jnp.transpose(ffn_pair, (1, 2, 0)), conv_weight, proj_weight],
        1 << 16, 1 << 19,
        scratch=[pltpu.VMEM((2, BLOCK, UNITS), bf16), pltpu.SemaphoreType.DMA((6,))],
        smem=1, hbm=3, name="pack",
    )
    both = jnp.stack([packed, ring(packed, "zl", 2, 1)])
    wire_pair = jnp.stack([wire, ring(wire, "zl", 2, 1)])

    outgoing = call(
        route_kernel,
        jax.ShapeDtypeStruct((N_DP * PAD, 1024), bf16),
        [owner.reshape(1, -1), frame_live.reshape(1, -1), waveform_rows],
        2 * 256 * 128 * 1152, 1 << 20,
        scratch=[
            pltpu.VMEM((1, 128), i32),
            pltpu.VMEM((1, 128), i32),
            pltpu.VMEM((128, 1024), bf16),
            pltpu.SemaphoreType.DMA((3,)),
        ],
        hbm=3, name="route",
    )
    along_z = jnp.stack(around(both, "zh", 4))
    wire_own = jnp.stack(around(wire_pair, "y", 4))
    outgoing, along_z, wire_own = lax.optimization_barrier((outgoing, along_z, wire_own))
    cotangent, wire_own = lax.optimization_barrier((cotangent, wire_own))
    cot_all = lax.all_gather(cotangent, "y", axis=0)
    wires = [wire_own, ring(wire_own, "c", 2, 1)]
    along_x = around(along_z, "x", 4)
    incoming = lax.all_to_all(
        outgoing.reshape(N_DP, PAD, 1024), dp, split_axis=0, concat_axis=0, tiled=True
    ).reshape(N_DP * PAD, 1024)
    where = jnp.stack([y, zl, c])
    proj_full = call(
        proj_kernel,
        jax.ShapeDtypeStruct((CH, D), bf16),
        [where, *wires],
        1 << 18, 3 << 20, smem=1, name="proj",
    )

    block, flags = call(
        front_kernel,
        (
            jax.ShapeDtypeStruct((4, SLOTS + 16, CH), bf16),
            jax.ShapeDtypeStruct((SLOTS, 1), f32),
        ),
        [where, incoming, *wires],
        2 * 256 * 1024 * 512, 2 << 20,
        scratch=[pltpu.VMEM((1024, CH), bf16), pltpu.SemaphoreType.DMA((16,))],
        smem=1, free=2, name="front",
    )
    block, proj_full, *along_x = lax.optimization_barrier((block, proj_full, *along_x))
    blocks = lax.all_to_all(block, "y", split_axis=0, concat_axis=0, tiled=True)
    pieces = along_x + [ring(piece, "c", 2, 1) for piece in along_x]

    rows = 4 * SLOTS
    piece = jax.ShapeDtypeStruct((SLOTS, D), bf16)
    terms = jax.ShapeDtypeStruct((4, 8, BLOCK, 2 * UNITS), bf16)
    own, away1, away2, away3, kept, sent = call(
        ffn_kernel,
        (jax.ShapeDtypeStruct((SLOTS, D), f32), piece, piece, piece, terms, terms),
        [jnp.stack([y, zl, c, zh, x]), blocks, *pieces, cot_all, proj_full],
        2 * rows * D * (CH + 5 * WIDE), 16 << 20,
        scratch=[
            pltpu.VMEM((CH, D), bf16),
            pltpu.VMEM((4, SLOTS + 16, CH), bf16),
            pltpu.VMEM((4, SLOTS, 1), f32),
            pltpu.VMEM((rows, D), bf16),
            pltpu.VMEM((rows, WIDE), bf16),
            pltpu.VMEM((rows, WIDE), bf16),
            pltpu.VMEM((rows, D), bf16),
            pltpu.VMEM((640, WIDE), f32),
            pltpu.VMEM((640, WIDE), f32),
            pltpu.VMEM((rows, D), bf16),
            pltpu.VMEM((D, WIDE), bf16),
            pltpu.VMEM((D, WIDE), bf16),
            pltpu.VMEM((2, 4, 4, 2, BLOCK, 2 * UNITS), bf16),
            pltpu.SemaphoreType.DMA((17,)),
        ],
        vmem=40 << 20, smem=1, hbm=10, free=1, name="ffn",
    )
    tile = jax.ShapeDtypeStruct((8, BLOCK, 2 * UNITS), bf16)
    parts = call(
        core_sum_kernel,
        (tile,) * 4,
        [x[None], kept, ring(sent, "c", 2, 1)],
        1 << 20, 5 << 20, smem=1, name="core_sum",
    )
    total = call(
        x_sum_kernel,
        tile,
        [parts[0]] + [ring(parts[step], "x", 4, step) for step in range(1, 4)],
        1 << 20, 2 << 20, name="x_sum",
    )
    away1, away2, away3, _ = lax.optimization_barrier((away1, away2, away3, parts[0]))
    for step, away in ((1, away1), (2, away2), (3, away3)):
        own = own + ring(away, "y", 4, 4 - step).astype(f32)
    encoded = (own * (flags > 0).astype(f32)).astype(bf16)
    total = lax.all_to_all(total, ZX, split_axis=0, concat_axis=0, tiled=True)
    grad_pair = call(
        last_kernel,
        jax.ShapeDtypeStruct((2, BLOCK, UNITS), f32),
        [total],
        1 << 18, 1 << 19, name="last",
    )
    return (encoded, jnp.transpose(grad_pair, (2, 0, 1)))


def solution(mesh):
    names = ("zh", "x", "c", "y", "zl")
    fine = Mesh(np.asarray(mesh.devices).reshape(4, 4, 2, 4, 2), names)
    dp = ("zh", "x", "c")
    fsdp = ("y", "zl")
    everyone = dp + fsdp
    return jax.shard_map(
        per_device,
        mesh=fine,
        in_specs=(
            P(everyone, None),
            P(fsdp, None),
            P(fsdp, None),
            P(fsdp, None, dp),
            P(everyone, None),
            P(everyone),
            P(everyone, None),
        ),
        out_specs=(P(everyone, None), P(fsdp, None, dp)),
        check_vma=False,
    )
```

```python
import functools

import jax
import jax.numpy as jnp
import numpy as np
from jax import lax
from jax.experimental import pallas as pl
from jax.experimental.pallas import tpu as pltpu
from jax.sharding import Mesh
from jax.sharding import PartitionSpec as P

epsilon = 1e-05
bf16 = jnp.bfloat16
f32 = jnp.float32
i32 = jnp.int32

N_DP = 32
CAP = 6
PAD = 8
SLOTS = 192
CH = 512
D = 1280
UNITS = 320
LANES = 384
WIDE = 2 * LANES
BLOCK = 40

VMEM = pl.BlockSpec(memory_space=pltpu.VMEM)
SMEM = pl.BlockSpec(memory_space=pltpu.SMEM)
HBM = pl.BlockSpec(memory_space=pltpu.HBM)
ANY = pl.BlockSpec(memory_space=pl.ANY)


def dot(a, b, dims=((1,), (0,))):
    return lax.dot_general(a, b, (dims, ((), ())), preferred_element_type=f32)


def iota(shape, dim):
    return lax.broadcasted_iota(i32, shape, dim)


def normalize(values):
    mean_value = jnp.mean(values, axis=-1, keepdims=True)
    centered = values - mean_value
    variance = jnp.mean(centered * centered, axis=-1, keepdims=True)
    return centered * lax.rsqrt(variance + epsilon)


def call(kernel, out_shape, args, flops, bytes_accessed, scratch=(), vmem=12 << 20, smem=0, hbm=0, free=0, name=None):
    args = list(args)
    for k in range(len(args) - hbm, len(args)):
        args[k] = pltpu.with_memory_space_constraint(args[k], pltpu.HBM)
    return pl.pallas_call(
        kernel,
        out_shape=out_shape,
        in_specs=[SMEM] * smem + [VMEM] * (len(args) - smem - free - hbm) + [ANY] * free + [HBM] * hbm,
        out_specs=jax.tree.map(lambda _: VMEM, out_shape),
        scratch_shapes=list(scratch),
        compiler_params=pltpu.CompilerParams(vmem_limit_bytes=vmem),
        cost_estimate=pl.CostEstimate(
            flops=flops, bytes_accessed=bytes_accessed, transcendentals=0
        ),
        name=name,
    )(*args)


def pack_kernel(place, pair_in, conv_in, proj_in, packed, wire, pair, arrival):
    c = place[0]
    conv_rows = pl.ds(pl.multiple_of(c * 64, 64), 64)
    proj_rows = pl.ds(pl.multiple_of(c * 32, 32), 32)
    low = pl.ds(pl.multiple_of(c * 32, 16), 16)
    high = pl.ds(pl.multiple_of(c * 32 + 16, 16), 16)
    routes = (
        (pair_in, pair),
        (conv_in.at[conv_rows, :], wire.at[pl.ds(0, 64), :]),
        (proj_in.at[proj_rows, pl.ds(0, 512)], wire.at[pl.ds(64, 32), :]),
        (proj_in.at[proj_rows, pl.ds(512, 512)], wire.at[pl.ds(96, 32), :]),
        (proj_in.at[low, pl.ds(1024, 256)], wire.at[pl.ds(128, 16), pl.ds(0, 256)]),
        (proj_in.at[high, pl.ds(1024, 256)], wire.at[pl.ds(128, 16), pl.ds(256, 256)]),
    )
    copies = [
        pltpu.make_async_copy(source, target, arrival.at[k])
        for k, (source, target) in enumerate(routes)
    ]
    for copy in copies:
        copy.start()
    for copy in copies:
        copy.wait()
    up = pair[0].astype(f32)
    down = pair[1].astype(f32)
    blank = jnp.zeros((BLOCK, LANES - UNITS), f32)
    up = jnp.concatenate([up, blank], axis=1)
    down = jnp.concatenate([down, blank], axis=1)
    packed[...] = pack_pair(up, down).astype(bf16)


def pack_pair(up, down):
    turned = pltpu.roll(down, 64, 1)
    lane = iota((BLOCK, 128), 1)
    middle = jnp.where(lane < 64, up[:, 256:], turned[:, :128])
    return jnp.concatenate([up[:, :256], middle, turned[:, 128:]], axis=1)


def unpack_pair(packed):
    used = iota((BLOCK, LANES), 1) < UNITS
    up = jnp.where(used, packed[:, :LANES], 0.0)
    down = pltpu.roll(packed[:, 256:], LANES - 64, 1)
    return up, jnp.where(used, down, 0.0)


def route_kernel(owner_in, live_in, rows_in, outgoing, owner, live, rows, arrival):
    copies = [
        pltpu.make_async_copy(owner_in, owner, arrival.at[0]),
        pltpu.make_async_copy(live_in, live, arrival.at[1]),
        pltpu.make_async_copy(rows_in, rows, arrival.at[2]),
    ]
    for copy in copies:
        copy.start()
    copies[0].wait()
    copies[1].wait()
    count = rows.shape[0]
    diagonal = iota((count, count), 0) == iota((count, count), 1)
    target = jnp.sum(jnp.where(diagonal, owner[...], 0), axis=1, keepdims=True)
    onehot = (target == iota((count, 128), 1)).astype(f32)
    earlier = (iota((count, count), 1) < iota((count, count), 0)).astype(bf16)
    before = dot(earlier, onehot.astype(bf16))
    position = jnp.sum(before * onehot, axis=1, keepdims=True).astype(i32)
    state = 1.0 + jnp.sum(
        jnp.where(diagonal, live[...].astype(f32), 0.0), axis=1, keepdims=True
    )
    slot = iota((count, N_DP * PAD), 1)
    placement = (target * PAD + position == slot).astype(bf16)
    flag_row = (target * PAD + CAP == slot).astype(bf16)
    flag_value = jnp.where(position == iota((count, 128), 1), state, 0.0).astype(bf16)
    first = ((0,), (0,))
    copies[2].wait()
    outgoing[...] = dot(placement, rows[...], first).astype(bf16)
    flags = dot(flag_row, flag_value, first)
    outgoing[:, :128] = (outgoing[:, :128].astype(f32) + flags).astype(bf16)


def wire_places(place, rows_each):
    y, zl, c = place[0], place[1], place[2]
    for step in range(4):
        for k in range(4):
            source = lax.rem(y - step + 4, 4) * 4 + lax.rem(zl + k // 2, 2) * 2
            source = source + lax.rem(c + k % 2, 2)
            yield step, k // 2, k % 2, pl.multiple_of(source * rows_each, rows_each)


def proj_kernel(place, own, other, proj):
    for step, half, core, row in wire_places(place, 32):
        wire = (own, other)[core]
        rows = pl.ds(row, 32)
        proj[rows, :512] = wire[step, half, 64:96, :]
        proj[rows, 512:1024] = wire[step, half, 96:128, :]
        proj[pl.ds(row, 16), 1024:] = wire[step, half, 128:144, :256]
        proj[pl.ds(pl.multiple_of(row + 16, 16), 16), 1024:] = wire[step, half, 128:144, 256:]


def front_kernel(place, incoming, *refs):
    wires, (block, flags_out, conv, arrival) = refs[:2], refs[2:]
    copies = []
    for step, half, core, row in wire_places(place, 64):
        source = wires[core].at[step, half, pl.ds(0, 64), :]
        target = conv.at[pl.ds(row, 64), :]
        copies.append(pltpu.make_async_copy(source, target, arrival.at[len(copies)]))
        copies[-1].start()
    for copy in copies:
        copy.wait()
    raw = incoming[...]
    conv_out = dot(raw, conv[...])
    active = 0.5 * conv_out * (1.0 + lax.erf(conv_out * 0.7071067811865476))
    features = normalize(active).astype(bf16)
    slot = iota((SLOTS, N_DP * PAD), 0)
    row = iota((SLOTS, N_DP * PAD), 1)
    owner, rank = slot // CAP, slot % CAP
    compact = (row == owner * PAD + rank).astype(bf16)
    compacted = dot(compact, features).astype(bf16)
    for copy in range(4):
        block[copy, :SLOTS, :] = compacted
    flag_rows = dot((row == owner * PAD + CAP).astype(bf16), raw[:, :128])
    lane = iota((SLOTS, 128), 1)
    flags = jnp.sum(
        jnp.where(lane == iota((SLOTS, 128), 0) % CAP, flag_rows, 0.0), axis=1, keepdims=True
    )
    flags_out[...] = flags
    wide = iota((SLOTS, CH), 1) == iota((SLOTS, CH), 0)
    as_row = jnp.sum(jnp.where(wide, flags, 0.0), axis=0, keepdims=True)
    for copy in range(4):
        block[copy, SLOTS:, :] = jnp.broadcast_to(as_row, (16, CH)).astype(bf16)


def ffn_kernel(place, blocks, *refs):
    pieces, cots, proj_in, refs = refs[:8], refs[8], refs[9], refs[10:]
    own, away1, away2, away3, kept, sent, refs = *refs[:6], refs[6:]
    proj, feats, live, normed, hidden, grad_pre, grad_out, wide_up, wide_down, *refs = refs
    cot, up, down, raw, arrival = refs
    y, zl, c, zh, x = place[0], place[1], place[2], place[3], place[4]
    copies = []

    def fetch(source, target):
        copy = pltpu.make_async_copy(source, target, arrival.at[len(copies)])
        copy.start()
        copies.append(copy)

    for k, piece in enumerate(pieces):
        fetch(piece, raw.at[k // 4, k % 4])
    for step in range(4):
        fetch(blocks.at[lax.rem(y - step + 4, 4)], feats.at[step])
    fetch(proj_in, proj)
    for step in range(4):
        fetch(cots.at[lax.rem(y - step + 4, 4)], cot.at[pl.ds(step * SLOTS, SLOTS), :])
    for copy in copies[:8]:
        copy.wait()

    def assemble(spot, carry):
        above, behind = spot // 4, lax.rem(spot, 4)
        row = lax.rem(zh - above + 4, 4) * 320 + lax.rem(x - behind + 4, 4) * 2 * BLOCK
        rows = pl.ds(pl.multiple_of(row, 16), 2 * BLOCK)
        for half in range(2):
            lanes = slice(half * LANES, (half + 1) * LANES)
            other = lax.rem(zl + half, 2)
            up0, down0 = unpack_pair(raw[c, behind, above, other].astype(f32))
            up1, down1 = unpack_pair(raw[1 - c, behind, above, other].astype(f32))
            up[rows, lanes] = jnp.concatenate([up0, up1], axis=0).astype(bf16)
            down[rows, lanes] = jnp.concatenate([down0, down1], axis=0).astype(bf16)
        return carry

    lax.fori_loop(0, 16, assemble, 0, unroll=4)
    for copy in copies[8:]:
        copy.wait()
    for step in range(4):
        flags = feats[step, SLOTS : SLOTS + 16, :].astype(f32)[:1, :]
        wide = iota((SLOTS, CH), 1) == iota((SLOTS, CH), 0)
        flags = jnp.sum(jnp.where(wide, flags, 0.0), axis=1, keepdims=True)
        live[step] = (flags == 2.0).astype(f32)

    def forward(step, carry):
        rows = pl.ds(pl.multiple_of(step * SLOTS, SLOTS), SLOTS)
        stream = dot(feats[step, :SLOTS, :], proj[...]).astype(bf16).astype(f32)
        normed[rows, :] = normalize(stream).astype(bf16)
        pre = dot(normed[rows, :], up[...])
        cumulative = 0.5 * (1.0 + lax.erf(pre * 0.7071067811865476))
        density = jnp.exp(-0.5 * pre * pre) * 0.3989422804014327
        hidden[rows, :] = (pre * cumulative).astype(bf16)
        slope = cumulative + pre * density
        partial = dot(hidden[rows, :], down[...], ((1,), (1,)))

        @pl.when(step == 0)
        def _():
            own[...] = partial + stream

        for k, away in enumerate((away1, away2, away3)):

            @pl.when(step == k + 1)
            def _():
                away[...] = partial.astype(bf16)

        masked = cot[rows, :].astype(f32) * live[step]
        grad_out[rows, :] = masked.astype(bf16)
        grad_hidden = dot(grad_out[rows, :], down[...])
        grad_pre[rows, :] = (grad_hidden * slope).astype(bf16)
        return carry

    lax.fori_loop(0, 4, forward, 0)

    def backward(part, carry):
        columns = pl.ds(pl.multiple_of(part * 640, 640), 640)
        first = ((0,), (0,))
        wide_up[...] = dot(normed[:, columns], grad_pre[...], first)
        wide_down[...] = dot(grad_out[:, columns], hidden[...], first)

        def place_block(k, carry):
            zh, x = k // 4, lax.rem(k, 4)
            for other, out in enumerate((kept, sent)):
                row = zh * 320 + x * 80 + lax.rem(c + other, 2) * BLOCK
                rows = pl.ds(pl.multiple_of(row, 8), BLOCK)
                for half in range(2):
                    lanes = slice(half * LANES, (half + 1) * LANES)
                    block = pack_pair(wide_up[rows, lanes], wide_down[rows, lanes])
                    out[x, (part * 2 + zh) * 2 + half] = block.astype(bf16)
            return carry

        lax.fori_loop(0, 8, place_block, 0)
        return carry

    lax.fori_loop(0, 2, backward, 0)


def core_sum_kernel(place, kept, arrived, *outs):
    x = place[0]
    for step, out in enumerate(outs):
        there = lax.rem(x + step, 4)
        out[...] = (kept[there].astype(f32) + arrived[there].astype(f32)).astype(bf16)


def x_sum_kernel(place, *refs):
    zl, arrived, (kept, sent) = place[0], refs[:4], refs[4:]
    for high in range(4):
        for other, out in enumerate((kept, sent)):
            there = high * 2 + lax.rem(zl + other, 2)
            total = arrived[0][there].astype(f32)
            for ref in arrived[1:]:
                total = total + ref[there].astype(f32)
            out[high] = total.astype(bf16)


def last_kernel(*refs):
    arrived, out = refs[:4], refs[4]
    total = arrived[0][...].astype(f32)
    for ref in arrived[1:]:
        total = total + ref[...].astype(f32)
    up, down = unpack_pair(total)
    out[0] = up[:, :UNITS]
    out[1] = down[:, :UNITS]


def ring(values, axis, size, step):
    return lax.ppermute(values, axis, [(k, (k + step) % size) for k in range(size)])


def around(values, axis, size):
    return [values] + [ring(values, axis, size, step) for step in range(1, size)]


def per_device(waveform_rows, conv_weight, proj_weight, ffn_pair, owner, frame_live, cotangent):
    dp = ("zh", "x", "c")
    zh, x, c, y, zl = (lax.axis_index(name).astype(i32) for name in ("zh", "x", "c", "y", "zl"))
    packed, wire = call(
        pack_kernel,
        (
            jax.ShapeDtypeStruct((BLOCK, 2 * UNITS), bf16),
            jax.ShapeDtypeStruct((144, CH), bf16),
        ),
        [c[None], jnp.transpose(ffn_pair, (1, 2, 0)), conv_weight, proj_weight],
        1 << 16, 1 << 19,
        scratch=[pltpu.VMEM((2, BLOCK, UNITS), bf16), pltpu.SemaphoreType.DMA((6,))],
        smem=1, hbm=3, name="pack",
    )
    both = jnp.stack([packed, ring(packed, "zl", 2, 1)])
    wire_pair = jnp.stack([wire, ring(wire, "zl", 2, 1)])

    outgoing = call(
        route_kernel,
        jax.ShapeDtypeStruct((N_DP * PAD, 1024), bf16),
        [owner.reshape(1, -1), frame_live.reshape(1, -1), waveform_rows],
        2 * 256 * 128 * 1152, 1 << 20,
        scratch=[
            pltpu.VMEM((1, 128), i32),
            pltpu.VMEM((1, 128), i32),
            pltpu.VMEM((128, 1024), bf16),
            pltpu.SemaphoreType.DMA((3,)),
        ],
        hbm=3, name="route",
    )
    along_z = jnp.stack(around(both, "zh", 4))
    wire_own = jnp.stack(around(wire_pair, "y", 4))
    outgoing, along_z, wire_own = lax.optimization_barrier((outgoing, along_z, wire_own))
    cotangent, wire_own = lax.optimization_barrier((cotangent, wire_own))
    cot_all = lax.all_gather(cotangent, "y", axis=0)
    wires = [wire_own, ring(wire_own, "c", 2, 1)]
    along_x = around(along_z, "x", 4)
    incoming = lax.all_to_all(
        outgoing.reshape(N_DP, PAD, 1024), dp, split_axis=0, concat_axis=0, tiled=True
    ).reshape(N_DP * PAD, 1024)
    where = jnp.stack([y, zl, c])
    proj_full = call(
        proj_kernel,
        jax.ShapeDtypeStruct((CH, D), bf16),
        [where, *wires],
        1 << 18, 3 << 20, smem=1, name="proj",
    )

    block, flags = call(
        front_kernel,
        (
            jax.ShapeDtypeStruct((4, SLOTS + 16, CH), bf16),
            jax.ShapeDtypeStruct((SLOTS, 1), f32),
        ),
        [where, incoming, *wires],
        2 * 256 * 1024 * 512, 2 << 20,
        scratch=[pltpu.VMEM((1024, CH), bf16), pltpu.SemaphoreType.DMA((16,))],
        smem=1, free=2, name="front",
    )
    block, proj_full, along_x[1], along_x[3] = lax.optimization_barrier(
        (block, proj_full, along_x[1], along_x[3])
    )
    blocks = lax.all_to_all(block, "y", split_axis=0, concat_axis=0, tiled=True)
    pieces = along_x + [ring(piece, "c", 2, 1) for piece in along_x]

    rows = 4 * SLOTS
    piece = jax.ShapeDtypeStruct((SLOTS, D), bf16)
    terms = jax.ShapeDtypeStruct((4, 8, BLOCK, 2 * UNITS), bf16)
    own, away1, away2, away3, kept, sent = call(
        ffn_kernel,
        (jax.ShapeDtypeStruct((SLOTS, D), f32), piece, piece, piece, terms, terms),
        [jnp.stack([y, zl, c, zh, x]), blocks, *pieces, cot_all, proj_full],
        2 * rows * D * (CH + 5 * WIDE), 16 << 20,
        scratch=[
            pltpu.VMEM((CH, D), bf16),
            pltpu.VMEM((4, SLOTS + 16, CH), bf16),
            pltpu.VMEM((4, SLOTS, 1), f32),
            pltpu.VMEM((rows, D), bf16),
            pltpu.VMEM((rows, WIDE), bf16),
            pltpu.VMEM((rows, WIDE), bf16),
            pltpu.VMEM((rows, D), bf16),
            pltpu.VMEM((640, WIDE), f32),
            pltpu.VMEM((640, WIDE), f32),
            pltpu.VMEM((rows, D), bf16),
            pltpu.VMEM((D, WIDE), bf16),
            pltpu.VMEM((D, WIDE), bf16),
            pltpu.VMEM((2, 4, 4, 2, BLOCK, 2 * UNITS), bf16),
            pltpu.SemaphoreType.DMA((17,)),
        ],
        vmem=40 << 20, smem=1, hbm=10, free=1, name="ffn",
    )
    tile = jax.ShapeDtypeStruct((8, BLOCK, 2 * UNITS), bf16)
    parts = call(
        core_sum_kernel,
        (tile,) * 4,
        [x[None], kept, ring(sent, "c", 2, 1)],
        1 << 20, 5 << 20, smem=1, name="core_sum",
    )
    half = jax.ShapeDtypeStruct((4, BLOCK, 2 * UNITS), bf16)
    kept, sent = call(
        x_sum_kernel,
        (half, half),
        [zl[None], parts[0]] + [ring(parts[step], "x", 4, step) for step in range(1, 4)],
        1 << 20, 2 << 20, smem=1, name="x_sum",
    )
    quarters = call(
        core_sum_kernel,
        (jax.ShapeDtypeStruct((BLOCK, 2 * UNITS), bf16),) * 4,
        [zh[None], kept, ring(sent, "zl", 2, 1)],
        1 << 18, 1 << 19, smem=1, name="z_sum",
    )
    away1, away2, away3, _ = lax.optimization_barrier((away1, away2, away3, parts[0]))
    for step, away in ((1, away1), (2, away2), (3, away3)):
        own = own + ring(away, "y", 4, 4 - step).astype(f32)
    encoded = (own * (flags > 0).astype(f32)).astype(bf16)
    grad_pair = call(
        last_kernel,
        jax.ShapeDtypeStruct((2, BLOCK, UNITS), f32),
        [quarters[0]] + [ring(quarters[step], "zh", 4, step) for step in range(1, 4)],
        1 << 18, 1 << 19, name="last",
    )
    return (encoded, jnp.transpose(grad_pair, (2, 0, 1)))


def solution(mesh):
    names = ("zh", "x", "c", "y", "zl")
    fine = Mesh(np.asarray(mesh.devices).reshape(4, 4, 2, 4, 2), names)
    dp = ("zh", "x", "c")
    fsdp = ("y", "zl")
    everyone = dp + fsdp
    return jax.shard_map(
        per_device,
        mesh=fine,
        in_specs=(
            P(everyone, None),
            P(fsdp, None),
            P(fsdp, None),
            P(fsdp, None, dp),
            P(everyone, None),
            P(everyone),
            P(everyone, None),
        ),
        out_specs=(P(everyone, None), P(fsdp, None, dp)),
        check_vma=False,
    )
```

```python
import functools

import jax
import jax.numpy as jnp
import numpy as np
from jax import lax
from jax.experimental import pallas as pl
from jax.experimental.pallas import tpu as pltpu
from jax.sharding import Mesh
from jax.sharding import PartitionSpec as P

epsilon = 1e-05
bf16 = jnp.bfloat16
f32 = jnp.float32
i32 = jnp.int32

N_DP = 32
CAP = 6
PAD = 8
SLOTS = 192
CH = 512
D = 1280
UNITS = 320
LANES = 384
WIDE = 2 * LANES
BLOCK = 40

VMEM = pl.BlockSpec(memory_space=pltpu.VMEM)
SMEM = pl.BlockSpec(memory_space=pltpu.SMEM)
HBM = pl.BlockSpec(memory_space=pltpu.HBM)
ANY = pl.BlockSpec(memory_space=pl.ANY)


def dot(a, b, dims=((1,), (0,))):
    return lax.dot_general(a, b, (dims, ((), ())), preferred_element_type=f32)


def iota(shape, dim):
    return lax.broadcasted_iota(i32, shape, dim)


def normalize(values):
    mean_value = jnp.mean(values, axis=-1, keepdims=True)
    centered = values - mean_value
    variance = jnp.mean(centered * centered, axis=-1, keepdims=True)
    return centered * lax.rsqrt(variance + epsilon)


def call(kernel, out_shape, args, flops, bytes_accessed, scratch=(), vmem=12 << 20, smem=0, hbm=0, free=0, name=None):
    args = list(args)
    for k in range(len(args) - hbm, len(args)):
        args[k] = pltpu.with_memory_space_constraint(args[k], pltpu.HBM)
    return pl.pallas_call(
        kernel,
        out_shape=out_shape,
        in_specs=[SMEM] * smem + [VMEM] * (len(args) - smem - free - hbm) + [ANY] * free + [HBM] * hbm,
        out_specs=jax.tree.map(lambda _: VMEM, out_shape),
        scratch_shapes=list(scratch),
        compiler_params=pltpu.CompilerParams(vmem_limit_bytes=vmem),
        cost_estimate=pl.CostEstimate(
            flops=flops, bytes_accessed=bytes_accessed, transcendentals=0
        ),
        name=name,
    )(*args)


def pack_kernel(place, pair_in, conv_in, proj_in, packed, wire, pair, arrival):
    c = place[0]
    conv_rows = pl.ds(pl.multiple_of(c * 64, 64), 64)
    proj_rows = pl.ds(pl.multiple_of(c * 32, 32), 32)
    low = pl.ds(pl.multiple_of(c * 32, 16), 16)
    high = pl.ds(pl.multiple_of(c * 32 + 16, 16), 16)
    routes = (
        (pair_in, pair),
        (conv_in.at[conv_rows, :], wire.at[pl.ds(0, 64), :]),
        (proj_in.at[proj_rows, pl.ds(0, 512)], wire.at[pl.ds(64, 32), :]),
        (proj_in.at[proj_rows, pl.ds(512, 512)], wire.at[pl.ds(96, 32), :]),
        (proj_in.at[low, pl.ds(1024, 256)], wire.at[pl.ds(128, 16), pl.ds(0, 256)]),
        (proj_in.at[high, pl.ds(1024, 256)], wire.at[pl.ds(128, 16), pl.ds(256, 256)]),
    )
    copies = [
        pltpu.make_async_copy(source, target, arrival.at[k])
        for k, (source, target) in enumerate(routes)
    ]
    for copy in copies:
        copy.start()
    for copy in copies:
        copy.wait()
    up = pair[0].astype(f32)
    down = pair[1].astype(f32)
    blank = jnp.zeros((BLOCK, LANES - UNITS), f32)
    up = jnp.concatenate([up, blank], axis=1)
    down = jnp.concatenate([down, blank], axis=1)
    packed[...] = pack_pair(up, down).astype(bf16)


def pack_pair(up, down):
    turned = pltpu.roll(down, 64, 1)
    lane = iota((BLOCK, 128), 1)
    middle = jnp.where(lane < 64, up[:, 256:], turned[:, :128])
    return jnp.concatenate([up[:, :256], middle, turned[:, 128:]], axis=1)


def unpack_pair(packed):
    used = iota((BLOCK, LANES), 1) < UNITS
    up = jnp.where(used, packed[:, :LANES], 0.0)
    down = pltpu.roll(packed[:, 256:], LANES - 64, 1)
    return up, jnp.where(used, down, 0.0)


def route_kernel(owner_in, live_in, rows_in, outgoing, owner, live, rows, arrival):
    copies = [
        pltpu.make_async_copy(owner_in, owner, arrival.at[0]),
        pltpu.make_async_copy(live_in, live, arrival.at[1]),
        pltpu.make_async_copy(rows_in, rows, arrival.at[2]),
    ]
    for copy in copies:
        copy.start()
    copies[0].wait()
    copies[1].wait()
    count = rows.shape[0]
    diagonal = iota((count, count), 0) == iota((count, count), 1)
    target = jnp.sum(jnp.where(diagonal, owner[...], 0), axis=1, keepdims=True)
    onehot = (target == iota((count, 128), 1)).astype(f32)
    earlier = (iota((count, count), 1) < iota((count, count), 0)).astype(bf16)
    before = dot(earlier, onehot.astype(bf16))
    position = jnp.sum(before * onehot, axis=1, keepdims=True).astype(i32)
    state = 1.0 + jnp.sum(
        jnp.where(diagonal, live[...].astype(f32), 0.0), axis=1, keepdims=True
    )
    slot = iota((count, N_DP * PAD), 1)
    placement = (target * PAD + position == slot).astype(bf16)
    flag_row = (target * PAD + CAP == slot).astype(bf16)
    flag_value = jnp.where(position == iota((count, 128), 1), state, 0.0).astype(bf16)
    first = ((0,), (0,))
    copies[2].wait()
    outgoing[...] = dot(placement, rows[...], first).astype(bf16)
    flags = dot(flag_row, flag_value, first)
    outgoing[:, :128] = (outgoing[:, :128].astype(f32) + flags).astype(bf16)


def wire_places(place, rows_each):
    y, zl, c = place[0], place[1], place[2]
    for step in range(4):
        for k in range(4):
            source = lax.rem(y - step + 4, 4) * 4 + lax.rem(zl + k // 2, 2) * 2
            source = source + lax.rem(c + k % 2, 2)
            yield step, k // 2, k % 2, pl.multiple_of(source * rows_each, rows_each)


def proj_kernel(place, own, other, proj):
    for step, half, core, row in wire_places(place, 32):
        wire = (own, other)[core]
        rows = pl.ds(row, 32)
        proj[rows, :512] = wire[step, half, 64:96, :]
        proj[rows, 512:1024] = wire[step, half, 96:128, :]
        proj[pl.ds(row, 16), 1024:] = wire[step, half, 128:144, :256]
        proj[pl.ds(pl.multiple_of(row + 16, 16), 16), 1024:] = wire[step, half, 128:144, 256:]


def front_kernel(place, incoming, *refs):
    wires, (block, flags_out, conv, arrival) = refs[:2], refs[2:]
    copies = []
    for step, half, core, row in wire_places(place, 64):
        source = wires[core].at[step, half, pl.ds(0, 64), :]
        target = conv.at[pl.ds(row, 64), :]
        copies.append(pltpu.make_async_copy(source, target, arrival.at[len(copies)]))
        copies[-1].start()
    for copy in copies:
        copy.wait()
    raw = incoming[...]
    conv_out = dot(raw, conv[...])
    active = 0.5 * conv_out * (1.0 + lax.erf(conv_out * 0.7071067811865476))
    features = normalize(active).astype(bf16)
    slot = iota((SLOTS, N_DP * PAD), 0)
    row = iota((SLOTS, N_DP * PAD), 1)
    owner, rank = slot // CAP, slot % CAP
    compact = (row == owner * PAD + rank).astype(bf16)
    compacted = dot(compact, features).astype(bf16)
    for copy in range(4):
        block[copy, :SLOTS, :] = compacted
    flag_rows = dot((row == owner * PAD + CAP).astype(bf16), raw[:, :128])
    lane = iota((SLOTS, 128), 1)
    flags = jnp.sum(
        jnp.where(lane == iota((SLOTS, 128), 0) % CAP, flag_rows, 0.0), axis=1, keepdims=True
    )
    flags_out[...] = flags
    wide = iota((SLOTS, CH), 1) == iota((SLOTS, CH), 0)
    as_row = jnp.sum(jnp.where(wide, flags, 0.0), axis=0, keepdims=True)
    for copy in range(4):
        block[copy, SLOTS:, :] = jnp.broadcast_to(as_row, (16, CH)).astype(bf16)


def ffn_kernel(place, blocks, *refs):
    pieces, cots, proj_in, refs = refs[:8], refs[8], refs[9], refs[10:]
    own, away1, away2, away3, kept, sent, refs = *refs[:6], refs[6:]
    proj, feats, live, normed, hidden, grad_pre, grad_out, wide_up, wide_down, *refs = refs
    cot, up, down, raw, arrival = refs
    y, zl, c, zh, x = place[0], place[1], place[2], place[3], place[4]
    copies = []

    def fetch(source, target):
        copy = pltpu.make_async_copy(source, target, arrival.at[len(copies)])
        copy.start()
        copies.append(copy)

    for k, piece in enumerate(pieces):
        fetch(piece, raw.at[k // 4, k % 4])
    for step in range(4):
        fetch(blocks.at[lax.rem(y - step + 4, 4)], feats.at[step])
    fetch(proj_in, proj)
    for step in range(4):
        fetch(cots.at[lax.rem(y - step + 4, 4)], cot.at[pl.ds(step * SLOTS, SLOTS), :])
    for copy in copies[:8]:
        copy.wait()

    def assemble(spot, carry):
        above, behind = spot // 4, lax.rem(spot, 4)
        row = lax.rem(zh - above + 4, 4) * 320 + lax.rem(x - behind + 4, 4) * 2 * BLOCK
        rows = pl.ds(pl.multiple_of(row, 16), 2 * BLOCK)
        for half in range(2):
            lanes = slice(half * LANES, (half + 1) * LANES)
            other = lax.rem(zl + half, 2)
            up0, down0 = unpack_pair(raw[c, behind, above, other].astype(f32))
            up1, down1 = unpack_pair(raw[1 - c, behind, above, other].astype(f32))
            up[rows, lanes] = jnp.concatenate([up0, up1], axis=0).astype(bf16)
            down[rows, lanes] = jnp.concatenate([down0, down1], axis=0).astype(bf16)
        return carry

    lax.fori_loop(0, 16, assemble, 0, unroll=4)
    for copy in copies[8:]:
        copy.wait()
    for step in range(4):
        flags = feats[step, SLOTS : SLOTS + 16, :].astype(f32)[:1, :]
        wide = iota((SLOTS, CH), 1) == iota((SLOTS, CH), 0)
        flags = jnp.sum(jnp.where(wide, flags, 0.0), axis=1, keepdims=True)
        live[step] = (flags == 2.0).astype(f32)

    for step in range(4):
        rows = slice(step * SLOTS, (step + 1) * SLOTS)
        masked = (cot[rows, :].astype(f32) * live[step]).astype(bf16)
        grad_out[rows, :] = masked
        stream = dot(feats[step, :SLOTS, :], proj[...]).astype(bf16).astype(f32)
        grad_hidden = dot(masked, down[...])
        level = normalize(stream).astype(bf16)
        normed[rows, :] = level
        pre = dot(level, up[...])
        cumulative = 0.5 * (1.0 + lax.erf(pre * 0.7071067811865476))
        density = jnp.exp(-0.5 * pre * pre) * 0.3989422804014327
        active = (pre * cumulative).astype(bf16)
        hidden[rows, :] = active
        grad_pre[rows, :] = (grad_hidden * (cumulative + pre * density)).astype(bf16)
        partial = dot(active, down[...], ((1,), (1,)))
        if step == 0:
            own[...] = partial + stream
        else:
            (away1, away2, away3)[step - 1][...] = partial.astype(bf16)

    def backward(part, carry):
        columns = pl.ds(pl.multiple_of(part * 640, 640), 640)
        first = ((0,), (0,))
        wide_up[...] = dot(normed[:, columns], grad_pre[...], first)
        wide_down[...] = dot(grad_out[:, columns], hidden[...], first)

        def place_block(k, carry):
            zh, x = k // 4, lax.rem(k, 4)
            for other, out in enumerate((kept, sent)):
                row = zh * 320 + x * 80 + lax.rem(c + other, 2) * BLOCK
                rows = pl.ds(pl.multiple_of(row, 8), BLOCK)
                for half in range(2):
                    lanes = slice(half * LANES, (half + 1) * LANES)
                    block = pack_pair(wide_up[rows, lanes], wide_down[rows, lanes])
                    out[x, (part * 2 + zh) * 2 + half] = block.astype(bf16)
            return carry

        lax.fori_loop(0, 8, place_block, 0)
        return carry

    lax.fori_loop(0, 2, backward, 0)


def core_sum_kernel(place, kept, arrived, *outs):
    x = place[0]
    for step, out in enumerate(outs):
        there = lax.rem(x + step, 4)
        out[...] = (kept[there].astype(f32) + arrived[there].astype(f32)).astype(bf16)


def x_sum_kernel(place, *refs):
    zl, arrived, (kept, sent) = place[0], refs[:4], refs[4:]
    for high in range(4):
        for other, out in enumerate((kept, sent)):
            there = high * 2 + lax.rem(zl + other, 2)
            total = arrived[0][there].astype(f32)
            for ref in arrived[1:]:
                total = total + ref[there].astype(f32)
            out[high] = total.astype(bf16)


def last_kernel(*refs):
    arrived, out = refs[:4], refs[4]
    total = arrived[0][...].astype(f32)
    for ref in arrived[1:]:
        total = total + ref[...].astype(f32)
    up, down = unpack_pair(total)
    out[0] = up[:, :UNITS]
    out[1] = down[:, :UNITS]


def ring(values, axis, size, step):
    return lax.ppermute(values, axis, [(k, (k + step) % size) for k in range(size)])


def around(values, axis, size):
    return [values] + [ring(values, axis, size, step) for step in range(1, size)]


def per_device(waveform_rows, conv_weight, proj_weight, ffn_pair, owner, frame_live, cotangent):
    dp = ("zh", "x", "c")
    zh, x, c, y, zl = (lax.axis_index(name).astype(i32) for name in ("zh", "x", "c", "y", "zl"))
    packed, wire = call(
        pack_kernel,
        (
            jax.ShapeDtypeStruct((BLOCK, 2 * UNITS), bf16),
            jax.ShapeDtypeStruct((144, CH), bf16),
        ),
        [c[None], jnp.transpose(ffn_pair, (1, 2, 0)), conv_weight, proj_weight],
        1 << 16, 1 << 19,
        scratch=[pltpu.VMEM((2, BLOCK, UNITS), bf16), pltpu.SemaphoreType.DMA((6,))],
        smem=1, hbm=3, name="pack",
    )
    both = jnp.stack([packed, ring(packed, "zl", 2, 1)])
    wire_pair = jnp.stack([wire, ring(wire, "zl", 2, 1)])

    outgoing = call(
        route_kernel,
        jax.ShapeDtypeStruct((N_DP * PAD, 1024), bf16),
        [owner.reshape(1, -1), frame_live.reshape(1, -1), waveform_rows],
        2 * 256 * 128 * 1152, 1 << 20,
        scratch=[
            pltpu.VMEM((1, 128), i32),
            pltpu.VMEM((1, 128), i32),
            pltpu.VMEM((128, 1024), bf16),
            pltpu.SemaphoreType.DMA((3,)),
        ],
        hbm=3, name="route",
    )
    along_z = jnp.stack(around(both, "zh", 4))
    wire_own = jnp.stack(around(wire_pair, "y", 4))
    outgoing, along_z, wire_own = lax.optimization_barrier((outgoing, along_z, wire_own))
    cotangent, wire_own = lax.optimization_barrier((cotangent, wire_own))
    cot_all = lax.all_gather(cotangent, "y", axis=0)
    wires = [wire_own, ring(wire_own, "c", 2, 1)]
    along_x = around(along_z, "x", 4)
    incoming = lax.all_to_all(
        outgoing.reshape(N_DP, PAD, 1024), dp, split_axis=0, concat_axis=0, tiled=True
    ).reshape(N_DP * PAD, 1024)
    where = jnp.stack([y, zl, c])
    proj_full = call(
        proj_kernel,
        jax.ShapeDtypeStruct((CH, D), bf16),
        [where, *wires],
        1 << 18, 3 << 20, smem=1, name="proj",
    )

    block, flags = call(
        front_kernel,
        (
            jax.ShapeDtypeStruct((4, SLOTS + 16, CH), bf16),
            jax.ShapeDtypeStruct((SLOTS, 1), f32),
        ),
        [where, incoming, *wires],
        2 * 256 * 1024 * 512, 2 << 20,
        scratch=[pltpu.VMEM((1024, CH), bf16), pltpu.SemaphoreType.DMA((16,))],
        smem=1, free=2, name="front",
    )
    block, proj_full, along_x[1], along_x[3] = lax.optimization_barrier(
        (block, proj_full, along_x[1], along_x[3])
    )
    blocks = lax.all_to_all(block, "y", split_axis=0, concat_axis=0, tiled=True)
    pieces = along_x + [ring(piece, "c", 2, 1) for piece in along_x]

    rows = 4 * SLOTS
    piece = jax.ShapeDtypeStruct((SLOTS, D), bf16)
    terms = jax.ShapeDtypeStruct((4, 8, BLOCK, 2 * UNITS), bf16)
    own, away1, away2, away3, kept, sent = call(
        ffn_kernel,
        (jax.ShapeDtypeStruct((SLOTS, D), f32), piece, piece, piece, terms, terms),
        [jnp.stack([y, zl, c, zh, x]), blocks, *pieces, cot_all, proj_full],
        2 * rows * D * (CH + 5 * WIDE), 16 << 20,
        scratch=[
            pltpu.VMEM((CH, D), bf16),
            pltpu.VMEM((4, SLOTS + 16, CH), bf16),
            pltpu.VMEM((4, SLOTS, 1), f32),
            pltpu.VMEM((rows, D), bf16),
            pltpu.VMEM((rows, WIDE), bf16),
            pltpu.VMEM((rows, WIDE), bf16),
            pltpu.VMEM((rows, D), bf16),
            pltpu.VMEM((640, WIDE), f32),
            pltpu.VMEM((640, WIDE), f32),
            pltpu.VMEM((rows, D), bf16),
            pltpu.VMEM((D, WIDE), bf16),
            pltpu.VMEM((D, WIDE), bf16),
            pltpu.VMEM((2, 4, 4, 2, BLOCK, 2 * UNITS), bf16),
            pltpu.SemaphoreType.DMA((17,)),
        ],
        vmem=40 << 20, smem=1, hbm=10, free=1, name="ffn",
    )
    tile = jax.ShapeDtypeStruct((8, BLOCK, 2 * UNITS), bf16)
    parts = call(
        core_sum_kernel,
        (tile,) * 4,
        [x[None], kept, ring(sent, "c", 2, 1)],
        1 << 20, 5 << 20, smem=1, name="core_sum",
    )
    half = jax.ShapeDtypeStruct((4, BLOCK, 2 * UNITS), bf16)
    kept, sent = call(
        x_sum_kernel,
        (half, half),
        [zl[None], parts[0]] + [ring(parts[step], "x", 4, step) for step in range(1, 4)],
        1 << 20, 2 << 20, smem=1, name="x_sum",
    )
    quarters = call(
        core_sum_kernel,
        (jax.ShapeDtypeStruct((BLOCK, 2 * UNITS), bf16),) * 4,
        [zh[None], kept, ring(sent, "zl", 2, 1)],
        1 << 18, 1 << 19, smem=1, name="z_sum",
    )
    away1, away2, away3, _ = lax.optimization_barrier((away1, away2, away3, parts[0]))
    for step, away in ((1, away1), (2, away2), (3, away3)):
        own = own + ring(away, "y", 4, 4 - step).astype(f32)
    encoded = (own * (flags > 0).astype(f32)).astype(bf16)
    grad_pair = call(
        last_kernel,
        jax.ShapeDtypeStruct((2, BLOCK, UNITS), f32),
        [quarters[0]] + [ring(quarters[step], "zh", 4, step) for step in range(1, 4)],
        1 << 18, 1 << 19, name="last",
    )
    return (encoded, jnp.transpose(grad_pair, (2, 0, 1)))


def solution(mesh):
    names = ("zh", "x", "c", "y", "zl")
    fine = Mesh(np.asarray(mesh.devices).reshape(4, 4, 2, 4, 2), names)
    dp = ("zh", "x", "c")
    fsdp = ("y", "zl")
    everyone = dp + fsdp
    return jax.shard_map(
        per_device,
        mesh=fine,
        in_specs=(
            P(everyone, None),
            P(fsdp, None),
            P(fsdp, None),
            P(fsdp, None, dp),
            P(everyone, None),
            P(everyone),
            P(everyone, None),
        ),
        out_specs=(P(everyone, None), P(fsdp, None, dp)),
        check_vma=False,
    )
```

```python
import functools

import jax
import jax.numpy as jnp
import numpy as np
from jax import lax
from jax.experimental import pallas as pl
from jax.experimental.pallas import tpu as pltpu
from jax.sharding import Mesh
from jax.sharding import PartitionSpec as P

epsilon = 1e-05
bf16 = jnp.bfloat16
f32 = jnp.float32
i32 = jnp.int32

N_DP = 32
CAP = 6
PAD = 8
SLOTS = 192
CH = 512
D = 1280
UNITS = 320
LANES = 384
WIDE = 2 * LANES
BLOCK = 40

VMEM = pl.BlockSpec(memory_space=pltpu.VMEM)
SMEM = pl.BlockSpec(memory_space=pltpu.SMEM)
HBM = pl.BlockSpec(memory_space=pltpu.HBM)
ANY = pl.BlockSpec(memory_space=pl.ANY)


def dot(a, b, dims=((1,), (0,))):
    return lax.dot_general(a, b, (dims, ((), ())), preferred_element_type=f32)


def iota(shape, dim):
    return lax.broadcasted_iota(i32, shape, dim)


def normalize(values):
    mean_value = jnp.mean(values, axis=-1, keepdims=True)
    centered = values - mean_value
    variance = jnp.mean(centered * centered, axis=-1, keepdims=True)
    return centered * lax.rsqrt(variance + epsilon)


def call(kernel, out_shape, args, flops, bytes_accessed, scratch=(), vmem=12 << 20, smem=0, hbm=0, free=0, name=None):
    args = list(args)
    for k in range(len(args) - hbm, len(args)):
        args[k] = pltpu.with_memory_space_constraint(args[k], pltpu.HBM)
    return pl.pallas_call(
        kernel,
        out_shape=out_shape,
        in_specs=[SMEM] * smem + [VMEM] * (len(args) - smem - free - hbm) + [ANY] * free + [HBM] * hbm,
        out_specs=jax.tree.map(lambda _: VMEM, out_shape),
        scratch_shapes=list(scratch),
        compiler_params=pltpu.CompilerParams(vmem_limit_bytes=vmem),
        cost_estimate=pl.CostEstimate(
            flops=flops, bytes_accessed=bytes_accessed, transcendentals=0
        ),
        name=name,
    )(*args)


def pack_kernel(place, pair_in, conv_in, proj_in, packed, wire, pair, arrival):
    c = place[0]
    conv_rows = pl.ds(pl.multiple_of(c * 64, 64), 64)
    proj_rows = pl.ds(pl.multiple_of(c * 32, 32), 32)
    low = pl.ds(pl.multiple_of(c * 32, 16), 16)
    high = pl.ds(pl.multiple_of(c * 32 + 16, 16), 16)
    routes = (
        (pair_in, pair),
        (conv_in.at[conv_rows, :], wire.at[pl.ds(0, 64), :]),
        (proj_in.at[proj_rows, pl.ds(0, 512)], wire.at[pl.ds(64, 32), :]),
        (proj_in.at[proj_rows, pl.ds(512, 512)], wire.at[pl.ds(96, 32), :]),
        (proj_in.at[low, pl.ds(1024, 256)], wire.at[pl.ds(128, 16), pl.ds(0, 256)]),
        (proj_in.at[high, pl.ds(1024, 256)], wire.at[pl.ds(128, 16), pl.ds(256, 256)]),
    )
    copies = [
        pltpu.make_async_copy(source, target, arrival.at[k])
        for k, (source, target) in enumerate(routes)
    ]
    for copy in copies:
        copy.start()
    for copy in copies:
        copy.wait()
    up = pair[0].astype(f32)
    down = pair[1].astype(f32)
    blank = jnp.zeros((BLOCK, LANES - UNITS), f32)
    up = jnp.concatenate([up, blank], axis=1)
    down = jnp.concatenate([down, blank], axis=1)
    packed[...] = pack_pair(up, down).astype(bf16)


def pack_pair(up, down):
    turned = pltpu.roll(down, 64, 1)
    lane = iota((BLOCK, 128), 1)
    middle = jnp.where(lane < 64, up[:, 256:], turned[:, :128])
    return jnp.concatenate([up[:, :256], middle, turned[:, 128:]], axis=1)


def unpack_pair(packed):
    used = iota((BLOCK, LANES), 1) < UNITS
    up = jnp.where(used, packed[:, :LANES], 0.0)
    down = pltpu.roll(packed[:, 256:], LANES - 64, 1)
    return up, jnp.where(used, down, 0.0)


def route_kernel(owner_in, live_in, rows_in, outgoing, owner, live, rows, arrival):
    copies = [
        pltpu.make_async_copy(owner_in, owner, arrival.at[0]),
        pltpu.make_async_copy(live_in, live, arrival.at[1]),
        pltpu.make_async_copy(rows_in, rows, arrival.at[2]),
    ]
    for copy in copies:
        copy.start()
    copies[0].wait()
    copies[1].wait()
    count = rows.shape[0]
    diagonal = iota((count, count), 0) == iota((count, count), 1)
    target = jnp.sum(jnp.where(diagonal, owner[...], 0), axis=1, keepdims=True)
    onehot = (target == iota((count, 128), 1)).astype(f32)
    earlier = (iota((count, count), 1) < iota((count, count), 0)).astype(bf16)
    before = dot(earlier, onehot.astype(bf16))
    position = jnp.sum(before * onehot, axis=1, keepdims=True).astype(i32)
    state = 1.0 + jnp.sum(
        jnp.where(diagonal, live[...].astype(f32), 0.0), axis=1, keepdims=True
    )
    slot = iota((count, N_DP * PAD), 1)
    placement = (target * PAD + position == slot).astype(bf16)
    flag_row = (target * PAD + CAP == slot).astype(bf16)
    flag_value = jnp.where(position == iota((count, 128), 1), state, 0.0).astype(bf16)
    first = ((0,), (0,))
    copies[2].wait()
    outgoing[...] = dot(placement, rows[...], first).astype(bf16)
    flags = dot(flag_row, flag_value, first)
    outgoing[:, :128] = (outgoing[:, :128].astype(f32) + flags).astype(bf16)


def wire_places(place, rows_each):
    y, zl, c = place[0], place[1], place[2]
    for step in range(4):
        for k in range(4):
            source = lax.rem(y - step + 4, 4) * 4 + lax.rem(zl + k // 2, 2) * 2
            source = source + lax.rem(c + k % 2, 2)
            yield step, k // 2, k % 2, pl.multiple_of(source * rows_each, rows_each)


def proj_kernel(place, own, other, proj):
    for step, half, core, row in wire_places(place, 32):
        wire = (own, other)[core]
        rows = pl.ds(row, 32)
        proj[rows, :512] = wire[step, half, 64:96, :]
        proj[rows, 512:1024] = wire[step, half, 96:128, :]
        proj[pl.ds(row, 16), 1024:] = wire[step, half, 128:144, :256]
        proj[pl.ds(pl.multiple_of(row + 16, 16), 16), 1024:] = wire[step, half, 128:144, 256:]


def front_kernel(place, incoming, *refs):
    wires, (block, flags_out, conv, arrival) = refs[:2], refs[2:]
    copies = []
    for step, half, core, row in wire_places(place, 64):
        source = wires[core].at[step, half, pl.ds(0, 64), :]
        target = conv.at[pl.ds(row, 64), :]
        copies.append(pltpu.make_async_copy(source, target, arrival.at[len(copies)]))
        copies[-1].start()
    for copy in copies:
        copy.wait()
    raw = incoming[...]
    conv_out = dot(raw, conv[...])
    active = 0.5 * conv_out * (1.0 + lax.erf(conv_out * 0.7071067811865476))
    features = normalize(active).astype(bf16)
    slot = iota((SLOTS, N_DP * PAD), 0)
    row = iota((SLOTS, N_DP * PAD), 1)
    owner, rank = slot // CAP, slot % CAP
    compact = (row == owner * PAD + rank).astype(bf16)
    compacted = dot(compact, features).astype(bf16)
    for copy in range(4):
        block[copy, :SLOTS, :] = compacted
    flag_rows = dot((row == owner * PAD + CAP).astype(bf16), raw[:, :128])
    lane = iota((SLOTS, 128), 1)
    flags = jnp.sum(
        jnp.where(lane == iota((SLOTS, 128), 0) % CAP, flag_rows, 0.0), axis=1, keepdims=True
    )
    flags_out[...] = flags
    wide = iota((SLOTS, CH), 1) == iota((SLOTS, CH), 0)
    as_row = jnp.sum(jnp.where(wide, flags, 0.0), axis=0, keepdims=True)
    for copy in range(4):
        block[copy, SLOTS:, :] = jnp.broadcast_to(as_row, (16, CH)).astype(bf16)


def ffn_kernel(place, blocks, *refs):
    pieces, cots, proj_in, refs = refs[:8], refs[8], refs[9], refs[10:]
    own, away1, away2, away3, kept, sent, refs = *refs[:6], refs[6:]
    proj, feats, live, normed, hidden, grad_pre, grad_out, wide_up, wide_down, *refs = refs
    cot, up, down, raw, arrival = refs
    y, zl, c, zh, x = place[0], place[1], place[2], place[3], place[4]
    copies = []

    def fetch(source, target):
        copy = pltpu.make_async_copy(source, target, arrival.at[len(copies)])
        copy.start()
        copies.append(copy)

    for k, piece in enumerate(pieces):
        fetch(piece, raw.at[k // 4, k % 4])
    for step in range(4):
        fetch(blocks.at[lax.rem(y - step + 4, 4)], feats.at[step])
    fetch(proj_in, proj)
    for step in range(4):
        fetch(cots.at[lax.rem(y - step + 4, 4)], cot.at[pl.ds(step * SLOTS, SLOTS), :])
    for copy in copies[:8]:
        copy.wait()

    def assemble(spot, carry):
        above, behind = spot // 4, lax.rem(spot, 4)
        row = lax.rem(zh - above + 4, 4) * 320 + lax.rem(x - behind + 4, 4) * 2 * BLOCK
        rows = pl.ds(pl.multiple_of(row, 16), 2 * BLOCK)
        for half in range(2):
            lanes = slice(half * LANES, (half + 1) * LANES)
            other = lax.rem(zl + half, 2)
            up0, down0 = unpack_pair(raw[c, behind, above, other].astype(f32))
            up1, down1 = unpack_pair(raw[1 - c, behind, above, other].astype(f32))
            up[rows, lanes] = jnp.concatenate([up0, up1], axis=0).astype(bf16)
            down[rows, lanes] = jnp.concatenate([down0, down1], axis=0).astype(bf16)
        return carry

    lax.fori_loop(0, 16, assemble, 0, unroll=4)
    for copy in copies[8:]:
        copy.wait()
    for step in range(4):
        flags = feats[step, SLOTS : SLOTS + 16, :].astype(f32)[:1, :]
        wide = iota((SLOTS, CH), 1) == iota((SLOTS, CH), 0)
        flags = jnp.sum(jnp.where(wide, flags, 0.0), axis=1, keepdims=True)
        live[step] = (flags == 2.0).astype(f32)

    for step in range(4):
        rows = slice(step * SLOTS, (step + 1) * SLOTS)
        masked = (cot[rows, :].astype(f32) * live[step]).astype(bf16)
        grad_out[rows, :] = masked
        stream = dot(feats[step, :SLOTS, :], proj[...]).astype(bf16).astype(f32)
        grad_hidden = dot(masked, down[...])
        level = normalize(stream).astype(bf16)
        normed[rows, :] = level
        pre = dot(level, up[...])
        cumulative = 0.5 * (1.0 + lax.erf(pre * 0.7071067811865476))
        density = jnp.exp(-0.5 * pre * pre) * 0.3989422804014327
        active = (pre * cumulative).astype(bf16)
        hidden[rows, :] = active
        grad_pre[rows, :] = (grad_hidden * (cumulative + pre * density)).astype(bf16)
        partial = dot(active, down[...], ((1,), (1,)))
        if step == 0:
            own[...] = partial + stream
        else:
            (away1, away2, away3)[step - 1][...] = partial.astype(bf16)

    for part in range(2):
        columns = slice(part * 640, (part + 1) * 640)
        first = ((0,), (0,))
        wide_up[part] = dot(normed[:, columns], grad_pre[...], first)
        wide_down[part] = dot(grad_out[:, columns], hidden[...], first)

        def place_block(k, carry):
            high, along = k // 4, lax.rem(k, 4)
            for other, out in enumerate((kept, sent)):
                row = high * 320 + along * 80 + lax.rem(c + other, 2) * BLOCK
                rows = pl.ds(pl.multiple_of(row, 8), BLOCK)
                for half in range(2):
                    lanes = slice(half * LANES, (half + 1) * LANES)
                    block = pack_pair(wide_up[part, rows, lanes], wide_down[part, rows, lanes])
                    out[along, (part * 2 + high) * 2 + half] = block.astype(bf16)
            return carry

        lax.fori_loop(0, 8, place_block, 0, unroll=True)


def core_sum_kernel(place, kept, arrived, *outs):
    x = place[0]
    for step, out in enumerate(outs):
        there = lax.rem(x + step, 4)
        out[...] = (kept[there].astype(f32) + arrived[there].astype(f32)).astype(bf16)


def x_sum_kernel(place, *refs):
    zl, arrived, (kept, sent) = place[0], refs[:4], refs[4:]
    for high in range(4):
        for other, out in enumerate((kept, sent)):
            there = high * 2 + lax.rem(zl + other, 2)
            total = arrived[0][there].astype(f32)
            for ref in arrived[1:]:
                total = total + ref[there].astype(f32)
            out[high] = total.astype(bf16)


def last_kernel(*refs):
    arrived, out = refs[:4], refs[4]
    total = arrived[0][...].astype(f32)
    for ref in arrived[1:]:
        total = total + ref[...].astype(f32)
    up, down = unpack_pair(total)
    out[0] = up[:, :UNITS]
    out[1] = down[:, :UNITS]


def ring(values, axis, size, step):
    return lax.ppermute(values, axis, [(k, (k + step) % size) for k in range(size)])


def around(values, axis, size):
    return [values] + [ring(values, axis, size, step) for step in range(1, size)]


def per_device(waveform_rows, conv_weight, proj_weight, ffn_pair, owner, frame_live, cotangent):
    dp = ("zh", "x", "c")
    zh, x, c, y, zl = (lax.axis_index(name).astype(i32) for name in ("zh", "x", "c", "y", "zl"))
    packed, wire = call(
        pack_kernel,
        (
            jax.ShapeDtypeStruct((BLOCK, 2 * UNITS), bf16),
            jax.ShapeDtypeStruct((144, CH), bf16),
        ),
        [c[None], jnp.transpose(ffn_pair, (1, 2, 0)), conv_weight, proj_weight],
        1 << 16, 1 << 19,
        scratch=[pltpu.VMEM((2, BLOCK, UNITS), bf16), pltpu.SemaphoreType.DMA((6,))],
        smem=1, hbm=3, name="pack",
    )
    both = jnp.stack([packed, ring(packed, "zl", 2, 1)])
    wire_pair = jnp.stack([wire, ring(wire, "zl", 2, 1)])

    outgoing = call(
        route_kernel,
        jax.ShapeDtypeStruct((N_DP * PAD, 1024), bf16),
        [owner.reshape(1, -1), frame_live.reshape(1, -1), waveform_rows],
        2 * 256 * 128 * 1152, 1 << 20,
        scratch=[
            pltpu.VMEM((1, 128), i32),
            pltpu.VMEM((1, 128), i32),
            pltpu.VMEM((128, 1024), bf16),
            pltpu.SemaphoreType.DMA((3,)),
        ],
        hbm=3, name="route",
    )
    along_z = jnp.stack(around(both, "zh", 4))
    wire_own = jnp.stack(around(wire_pair, "y", 4))
    outgoing, along_z, wire_own = lax.optimization_barrier((outgoing, along_z, wire_own))
    cotangent, wire_own = lax.optimization_barrier((cotangent, wire_own))
    cot_all = lax.all_gather(cotangent, "y", axis=0)
    wires = [wire_own, ring(wire_own, "c", 2, 1)]
    along_x = around(along_z, "x", 4)
    incoming = lax.all_to_all(
        outgoing.reshape(N_DP, PAD, 1024), dp, split_axis=0, concat_axis=0, tiled=True
    ).reshape(N_DP * PAD, 1024)
    where = jnp.stack([y, zl, c])
    proj_full = call(
        proj_kernel,
        jax.ShapeDtypeStruct((CH, D), bf16),
        [where, *wires],
        1 << 18, 3 << 20, smem=1, name="proj",
    )

    block, flags = call(
        front_kernel,
        (
            jax.ShapeDtypeStruct((4, SLOTS + 16, CH), bf16),
            jax.ShapeDtypeStruct((SLOTS, 1), f32),
        ),
        [where, incoming, *wires],
        2 * 256 * 1024 * 512, 2 << 20,
        scratch=[pltpu.VMEM((1024, CH), bf16), pltpu.SemaphoreType.DMA((16,))],
        smem=1, free=2, name="front",
    )
    block, proj_full, along_x[1], along_x[3] = lax.optimization_barrier(
        (block, proj_full, along_x[1], along_x[3])
    )
    blocks = lax.all_to_all(block, "y", split_axis=0, concat_axis=0, tiled=True)
    pieces = along_x + [ring(piece, "c", 2, 1) for piece in along_x]

    rows = 4 * SLOTS
    piece = jax.ShapeDtypeStruct((SLOTS, D), bf16)
    terms = jax.ShapeDtypeStruct((4, 8, BLOCK, 2 * UNITS), bf16)
    own, away1, away2, away3, kept, sent = call(
        ffn_kernel,
        (jax.ShapeDtypeStruct((SLOTS, D), f32), piece, piece, piece, terms, terms),
        [jnp.stack([y, zl, c, zh, x]), blocks, *pieces, cot_all, proj_full],
        2 * rows * D * (CH + 5 * WIDE), 16 << 20,
        scratch=[
            pltpu.VMEM((CH, D), bf16),
            pltpu.VMEM((4, SLOTS + 16, CH), bf16),
            pltpu.VMEM((4, SLOTS, 1), f32),
            pltpu.VMEM((rows, D), bf16),
            pltpu.VMEM((rows, WIDE), bf16),
            pltpu.VMEM((rows, WIDE), bf16),
            pltpu.VMEM((rows, D), bf16),
            pltpu.VMEM((2, 640, WIDE), f32),
            pltpu.VMEM((2, 640, WIDE), f32),
            pltpu.VMEM((rows, D), bf16),
            pltpu.VMEM((D, WIDE), bf16),
            pltpu.VMEM((D, WIDE), bf16),
            pltpu.VMEM((2, 4, 4, 2, BLOCK, 2 * UNITS), bf16),
            pltpu.SemaphoreType.DMA((17,)),
        ],
        vmem=40 << 20, smem=1, hbm=10, free=1, name="ffn",
    )
    tile = jax.ShapeDtypeStruct((8, BLOCK, 2 * UNITS), bf16)
    parts = call(
        core_sum_kernel,
        (tile,) * 4,
        [x[None], kept, ring(sent, "c", 2, 1)],
        1 << 20, 5 << 20, smem=1, name="core_sum",
    )
    half = jax.ShapeDtypeStruct((4, BLOCK, 2 * UNITS), bf16)
    kept, sent = call(
        x_sum_kernel,
        (half, half),
        [zl[None], parts[0]] + [ring(parts[step], "x", 4, step) for step in range(1, 4)],
        1 << 20, 2 << 20, smem=1, name="x_sum",
    )
    quarters = call(
        core_sum_kernel,
        (jax.ShapeDtypeStruct((BLOCK, 2 * UNITS), bf16),) * 4,
        [zh[None], kept, ring(sent, "zl", 2, 1)],
        1 << 18, 1 << 19, smem=1, name="z_sum",
    )
    away1, away2, away3, _ = lax.optimization_barrier((away1, away2, away3, parts[0]))
    for step, away in ((1, away1), (2, away2), (3, away3)):
        own = own + ring(away, "y", 4, 4 - step).astype(f32)
    encoded = (own * (flags > 0).astype(f32)).astype(bf16)
    grad_pair = call(
        last_kernel,
        jax.ShapeDtypeStruct((2, BLOCK, UNITS), f32),
        [quarters[0]] + [ring(quarters[step], "zh", 4, step) for step in range(1, 4)],
        1 << 18, 1 << 19, name="last",
    )
    return (encoded, jnp.transpose(grad_pair, (2, 0, 1)))


def solution(mesh):
    names = ("zh", "x", "c", "y", "zl")
    fine = Mesh(np.asarray(mesh.devices).reshape(4, 4, 2, 4, 2), names)
    dp = ("zh", "x", "c")
    fsdp = ("y", "zl")
    everyone = dp + fsdp
    return jax.shard_map(
        per_device,
        mesh=fine,
        in_specs=(
            P(everyone, None),
            P(fsdp, None),
            P(fsdp, None),
            P(fsdp, None, dp),
            P(everyone, None),
            P(everyone),
            P(everyone, None),
        ),
        out_specs=(P(everyone, None), P(fsdp, None, dp)),
        check_vma=False,
    )
```
